32 devices in a mesh: section: 2 (over x), dp: 16 (over z, y, core).
Axes of the slice: x: 2, y: 2, z: 4, core: 2. Of those that a mesh axis runs over, the one named last changes fastest.
Arguments:
- tokens: bfloat16 [2, 6144, 768], P(None, 'dp'), may hold values from -6 to 6
- cotangent: bfloat16 [2, 6144, 768], P(None, 'dp'), may hold values from -6 to 6
- bucket: int32 [2, 16], P(None, 'dp'), may hold values from 0 to 2
- lengths: int32 [2, 96], P(None, 'dp'), may hold values from 16 to 192, as said below
- w_qkv: float32 [2, 768, 2304], P('section', 'dp'), may hold values from -0.21875 to 0.21875
- bias_q: float32 [2, 768], P('section', 'dp'), may hold values from -3 to 3
- bias_v: float32 [2, 768], P('section', 'dp'), may hold values from -3 to 3
- w_out: float32 [2, 768, 768], P('section', 'dp'), may hold values from -0.625 to 0.625
- bias_out: float32 [2, 768], P('section', 'dp'), may hold values from -3 to 3
- gain_attn: float32 [2, 768], P('section', 'dp'), may hold values from 0.25 to 1.75
- shift_attn: float32 [2, 768], P('section', 'dp'), may hold values from -3 to 3
- w_up: float32 [2, 768, 3072], P('section', 'dp'), may hold values from -0.21875 to 0.21875
- bias_up: float32 [2, 3072], P('section', 'dp'), may hold values from -3 to 3
- w_down: float32 [2, 3072, 768], P('section', 'dp'), may hold values from -0.15625 to 0.15625
- bias_down: float32 [2, 768], P('section', 'dp'), may hold values from -3 to 3
- gain_ffn: float32 [2, 768], P('section', 'dp'), may hold values from 0.25 to 1.75
- shift_ffn: float32 [2, 768], P('section', 'dp'), may hold values from -3 to 3
Outputs:
- hidden_states: bfloat16 [2, 2, 6144, 768], P('section', None, 'dp')
- input_grads: bfloat16 [2, 2, 6144, 768], P('section', None, 'dp')
- grad_w_qkv: float32 [2, 768, 2304], P('section', 'dp')
- grad_bias_q: float32 [2, 768], P('section', 'dp')
- grad_bias_v: float32 [2, 768], P('section', 'dp')
- grad_w_out: float32 [2, 768, 768], P('section', 'dp')
- grad_bias_out: float32 [2, 768], P('section', 'dp')
- grad_gain_attn: float32 [2, 768], P('section', 'dp')
- grad_shift_attn: float32 [2, 768], P('section', 'dp')
- grad_w_up: float32 [2, 768, 3072], P('section', 'dp')
- grad_bias_up: float32 [2, 3072], P('section', 'dp')
- grad_w_down: float32 [2, 3072, 768], P('section', 'dp')
- grad_bias_down: float32 [2, 768], P('section', 'dp')
- grad_gain_ffn: float32 [2, 768], P('section', 'dp')
- grad_shift_ffn: float32 [2, 768], P('section', 'dp')
The draws below stay inside these ranges and needn't reach their ends.
Inputs may be any that keep to these rules, and one draw needn't show every extreme that they name: `lengths`: valid length of each pair slot before it is clipped to its segment length; slots past a bucket's pair count are unused.
All inputs are finite; a program needn't handle non-finite values.
Results may differ from the reference program's by a relative error of at most 0.02.
Values may be sent and summed in bfloat16 or wider, within the bound.
No kernel may reach another device: no remote copies, remote signals or barrier semaphores. Data moves between devices by JAX's collectives and lax.ppermute only.
A program may use at most 320 MiB of HBM per device.

```python
import math
import jax
import jax.numpy as jnp
from jax import lax

D = 768
HEADS = 12
FF = 3072
SEGMENT = 64
PAIRS = 6
ROWS = 384
MICRO = 2
TOKENS = 6144
PAIR_SLOTS = 96
N_DP = 16


def draw_lengths(key, part):
    key = jax.random.fold_in(key, 7)
    key_values, key_high, key_low = jax.random.split(key, 3)
    total_slots = MICRO * PAIR_SLOTS
    values = jax.random.randint(key_values, (total_slots,), SEGMENT // 4, 3 * SEGMENT + 1, dtype=jnp.int32)
    high_slot = jax.random.randint(key_high, (), 0, total_slots, dtype=jnp.int32)
    low_slot = (high_slot + 1 + jax.random.randint(key_low, (), 0, total_slots - 1, dtype=jnp.int32)) % total_slots
    positions = jnp.arange(total_slots, dtype=jnp.int32)
    values = jnp.where(positions == high_slot, 3 * SEGMENT, values)
    values = jnp.where(positions == low_slot, SEGMENT // 4, values)
    return values.reshape(MICRO, PAIR_SLOTS)


def place_ends(values, stream_key, smallest, top_value):
    place = [jax.random.randint(jax.random.fold_in(stream_key, axis), (), 0, length) for axis, length in enumerate(values.shape)]
    widest = values.shape.index(max(values.shape))
    neighbour = place[:widest] + [(place[widest] + 1) % values.shape[widest]] + place[widest + 1:]
    return values.at[tuple(place)].set(smallest).at[tuple(neighbour)].set(top_value)


def strengthened(array, rng, source, target, blocks, factor):
    def block_of(dim):
        return (jnp.arange(array.shape[dim]) // (array.shape[dim] // blocks)).reshape((-1,) + (1,) * (array.ndim - 1 - dim))

    one_side = jax.random.permutation(rng, blocks)[block_of(target)]
    other_side = (block_of(target) + blocks // 2) % blocks
    return jnp.where((block_of(source) == one_side) | (block_of(source) == other_side), factor * array, array)


def levels(stream_key, dims, cuts, least, top_value):
    factor_of = 1.0
    for axis_at, blocks in cuts:
        draws = jax.random.uniform(jax.random.fold_in(jax.random.fold_in(stream_key, 6), axis_at), (blocks,), jnp.float32, least / len(cuts), top_value / len(cuts))
        factor_of = factor_of * jnp.repeat(jnp.exp(draws), dims[axis_at] // blocks).reshape((-1,) + (1,) * (len(dims) - 1 - axis_at))
    return factor_of


def gaussian(own_key, shape, spread, reach, shards=(), kind=jnp.bfloat16):
    loudness = levels(own_key, shape, shards, -0.22, 0.18) if shards else 1.0
    array = jax.random.normal(own_key, shape, jnp.float32) * spread * loudness
    return jnp.minimum(jnp.maximum(array, -reach), reach).astype(kind)


def gaussian_with(rng, dims, scale, limit, pieces, heavy, kind=jnp.bfloat16):
    values = scale * jax.random.normal(rng, dims, jnp.float32)
    if pieces:
        values = values * levels(rng, dims, pieces, -0.22, 0.18)
    return jnp.clip(strengthened(values, jax.random.fold_in(rng, 3), *heavy), -limit, limit).astype(kind)


def setup_inputs(seed: int = 0) -> dict:
    splits = jax.random.split(jax.random.key(seed), 18)
    return {
        "tokens": gaussian_with(splits[0], (MICRO, TOKENS, D), 1.0, 6.0, ((1, 16),), (1, 2, 16, 2.0)),
        "cotangent": gaussian_with(splits[1], (MICRO, TOKENS, D), 1.0, 6.0, ((1, 16),), (1, 2, 16, 2.0)),
        "bucket": place_ends(jax.random.randint(splits[2], (MICRO, N_DP), 0, 3), jax.random.fold_in(splits[2], 1), 0, 2).astype(jnp.int32),
        "lengths": draw_lengths(jax.random.fold_in(splits[17], 71), 0),
        "w_qkv": gaussian(splits[4], (2, D, 3 * D), D ** -0.5, 0.21875, ((0, 2), (1, 16)), jnp.float32),
        "bias_q": gaussian(splits[5], (2, D), 0.5, 3.0, ((0, 2), (1, 16)), jnp.float32),
        "bias_v": gaussian(splits[6], (2, D), 0.5, 3.0, ((0, 2), (1, 16)), jnp.float32),
        "w_out": gaussian(splits[7], (2, D, D), (D // 8) ** -0.5, 0.625, ((0, 2), (1, 16)), jnp.float32),
        "bias_out": gaussian(splits[8], (2, D), 0.5, 3.0, ((0, 2), (1, 16)), jnp.float32),
        "gain_attn": jnp.clip(1.0 + 0.15 * jax.random.normal(splits[9], (2, D), jnp.float32), 0.25, 1.75),
        "shift_attn": gaussian(splits[10], (2, D), 0.5, 3.0, ((0, 2), (1, 16)), jnp.float32),
        "w_up": gaussian(splits[11], (2, D, FF), D ** -0.5, 0.21875, ((0, 2), (1, 16)), jnp.float32),
        "bias_up": gaussian(splits[12], (2, FF), 0.5, 3.0, ((0, 2), (1, 16)), jnp.float32),
        "w_down": gaussian(splits[13], (2, FF, D), (FF // 2) ** -0.5, 0.15625, ((0, 2), (1, 16)), jnp.float32),
        "bias_down": gaussian(splits[14], (2, D), 0.5, 3.0, ((0, 2), (1, 16)), jnp.float32),
        "gain_ffn": jnp.clip(1.0 + 0.15 * jax.random.normal(splits[15], (2, D), jnp.float32), 0.25, 1.75),
        "shift_ffn": gaussian(splits[16], (2, D), 0.5, 3.0, ((0, 2), (1, 16)), jnp.float32),
    }


epsilon = 1e-06
masked_score = -1000000000.0
highest = lax.Precision.HIGHEST

@jax.custom_vjp
def low(v):
    return lax.optimization_barrier(v.astype(jnp.bfloat16)).astype(jnp.float32)

@jax.custom_vjp
def low_back(v):
    return v

def low_keep(v):
    return (low(v), None)

def low_pass(kept, grad):
    return (grad,)

def back_keep(v):
    return (v, None)

def back_low(kept, grad):
    return (low(grad),)
low.defvjp(low_keep, low_pass)
low_back.defvjp(back_keep, back_low)

def mask_for(bucket_id, valid_lengths):
    segment_rows = SEGMENT * (bucket_id + 1)
    row_index = jnp.arange(ROWS, dtype=jnp.int32)
    pair_index = row_index // segment_rows
    position = row_index - pair_index * segment_rows
    clipped = jnp.minimum(valid_lengths, segment_rows)
    matches = pair_index[:, None] == jnp.arange(PAIRS, dtype=jnp.int32)[None, :]
    row_valid = lax.optimization_barrier(jnp.sum(jnp.where(matches, clipped[None, :], 0), axis=1))
    return (pair_index[:, None] == pair_index[None, :]) & (position < row_valid)[None, :]

def layer_norm(values, gain, shift):
    centered = values - lax.optimization_barrier(jnp.mean(values, axis=-1, keepdims=True))
    variance = lax.optimization_barrier(jnp.mean(centered * centered, axis=-1, keepdims=True))
    return centered * lax.rsqrt(variance + epsilon) * gain + shift

def layer_apply(inputs, params, allowed):
    w_qkv, bias_q, bias_v, w_out, bias_out, gain_attn, shift_attn, w_up, bias_up, w_down, bias_down, gain_ffn, shift_ffn = params
    row_count, model_width = inputs.shape
    head_dim = model_width // HEADS
    scale = 1.0 / math.sqrt(head_dim)
    bias_all = jnp.concatenate([bias_q, jnp.zeros_like(bias_q), bias_v])
    qkv = low(low_back(jnp.dot(inputs, w_qkv, precision=highest) + bias_all))
    queries = qkv[:, :model_width].reshape(row_count, HEADS, head_dim)
    keys = qkv[:, model_width:2 * model_width].reshape(row_count, HEADS, head_dim)
    values = qkv[:, 2 * model_width:].reshape(row_count, HEADS, head_dim)
    scores = low_back(jnp.einsum('qhd,khd->hqk', queries, keys, precision=highest) * scale)
    scores = jnp.where(allowed[None], scores, masked_score)
    probs = jax.nn.softmax(scores, axis=-1)
    context = jnp.einsum('hqk,khd->qhd', low(probs), values, precision=highest).reshape(row_count, model_width)
    context = low(low_back(context))
    branch = low_back(jnp.dot(context, w_out, precision=highest) + bias_out)
    hidden = layer_norm(inputs + branch, gain_attn, shift_attn)
    pre = low_back(jnp.dot(low(hidden), w_up, precision=highest) + bias_up)
    active = low(jax.nn.gelu(pre, approximate=False))
    ffn_out = low_back(jnp.dot(active, w_down, precision=highest) + bias_down)
    return layer_norm(hidden + ffn_out, gain_ffn, shift_ffn)

def reference(tokens, cotangent, bucket, lengths, w_qkv, bias_q, bias_v, w_out, bias_out, gain_attn, shift_attn, w_up, bias_up, w_down, bias_down, gain_ffn, shift_ffn):
    masters = (w_qkv, bias_q, bias_v, w_out, bias_out, gain_attn, shift_attn, w_up, bias_up, w_down, bias_down, gain_ffn, shift_ffn)
    first_params = tuple((low(master[0]) for master in masters))
    second_params = tuple((low(master[1]) for master in masters))
    slot_count = MICRO * N_DP
    slot_inputs = tokens.astype(jnp.float32).reshape(slot_count, ROWS, D)
    slot_cotangents = cotangent.astype(jnp.float32).reshape(slot_count, ROWS, D)
    slot_buckets = bucket.reshape(slot_count)
    slot_lengths = lengths.reshape(slot_count, PAIRS)
    zero_first = tuple((jnp.zeros_like(param) for param in first_params))
    zero_second = tuple((jnp.zeros_like(param) for param in second_params))

    def slot_step(totals, slot_data):
        inputs, outer_grad, bucket_id, valid_lengths = slot_data
        allowed = mask_for(bucket_id, valid_lengths)
        first_out, back_first = jax.vjp(lambda values, params: layer_apply(values, params, allowed), inputs, first_params)
        middle = low(first_out)
        final_out, back_second = jax.vjp(lambda values, params: layer_apply(values, params, allowed), middle, second_params)
        middle_grad, grads_second = back_second(outer_grad)
        middle_grad = low(middle_grad)
        input_grad, grads_first = back_first(middle_grad)
        totals_first = tuple((total + grad for total, grad in zip(totals[0], grads_first)))
        totals_second = tuple((total + grad for total, grad in zip(totals[1], grads_second)))
        results = (middle.astype(jnp.bfloat16), final_out.astype(jnp.bfloat16), input_grad.astype(jnp.bfloat16), middle_grad.astype(jnp.bfloat16))
        return ((totals_first, totals_second), results)
    totals, results = lax.scan(slot_step, (zero_first, zero_second), (slot_inputs, slot_cotangents, slot_buckets, slot_lengths))
    middle_all, final_all, input_all, middle_grad_all = (result.reshape(MICRO, N_DP * ROWS, D) for result in results)
    hidden_states = jnp.stack([middle_all, final_all])
    input_grads = jnp.stack([input_all, middle_grad_all])
    stacked = tuple((jnp.stack([first, second]) for first, second in zip(totals[0], totals[1])))
    return (hidden_states, input_grads, stacked[0], stacked[1], stacked[2], stacked[3], stacked[4], stacked[5], stacked[6], stacked[7], stacked[8], stacked[9], stacked[10], stacked[11], stacked[12])
```

```python
import functools

import jax
import jax.numpy as jnp
from jax import lax
from jax.experimental import pallas as pl
from jax.experimental.pallas import tpu as pltpu
from jax.sharding import PartitionSpec as P

HEADS = 12
SEGMENT = 64
PAIRS = 6
ROWS = 384
EPSILON = 1e-06
MASKED = -1000000000.0
LANES = 128
FF_TILE = 512
VMEM_LIMIT = 60 * 1024 * 1024
F32 = jnp.float32
BF16 = jnp.bfloat16

BIAS_Q, BIAS_K, BIAS_V, BIAS_OUT, GAIN_ATTN, SHIFT_ATTN, BIAS_DOWN, GAIN_FFN, SHIFT_FFN = range(9)
RUN, MICRO, SECTION, BUCKET, LENGTHS = range(5)

ANY = pl.BlockSpec(memory_space=pl.ANY)
WHOLE = pl.BlockSpec(memory_space=pltpu.VMEM)
SCALARS = pl.BlockSpec(memory_space=pltpu.SMEM)


def dot_nn(a, b):
    return lax.dot_general(a, b, (((1,), (0,)), ((), ())), preferred_element_type=F32)


def dot_nt(a, b):
    return lax.dot_general(a, b, (((1,), (1,)), ((), ())), preferred_element_type=F32)


def dot_tn(a, b):
    return lax.dot_general(a, b, (((0,), (0,)), ((), ())), preferred_element_type=F32)


class Copies:
    def __init__(self, sems):
        self.sems = sems
        self.next = 0

    def start(self, src, dst):
        copy = pltpu.make_async_copy(src, dst, self.sems.at[self.next])
        self.next += 1
        copy.start()
        return copy


def fetch_either(first, one, other, dst, sem):
    @pl.when(first)
    def _():
        pltpu.make_async_copy(one, dst, sem).start()

    @pl.when(jnp.logical_not(first))
    def _():
        pltpu.make_async_copy(other, dst, sem).start()

    return pltpu.make_async_copy(other, dst, sem)


def fold(values):
    rows, n = values.shape
    return jnp.sum(values.reshape(rows // 8, 8, n), axis=0)


def write_bias(info, bias, block, count):
    segment = (info[BUCKET] + 1) * SEGMENT
    per_block = jnp.where(info[BUCKET] == 0, block // SEGMENT, 1)
    k_row = lax.broadcasted_iota(jnp.int32, (block, block), 0)
    q_row = lax.broadcasted_iota(jnp.int32, (block, block), 1)

    def pair_of(row):
        return (row >= segment).astype(jnp.int32) + (row >= 2 * segment).astype(jnp.int32)

    k_pair = pair_of(k_row)
    same = k_pair == pair_of(q_row)
    position = k_row - k_pair * segment
    for at in range(count):
        valid = [
            jnp.minimum(info[LENGTHS + jnp.minimum(at * per_block + i, PAIRS - 1)], segment)
            for i in range(3)
        ]
        length = jnp.where(k_pair == 0, valid[0], jnp.where(k_pair == 1, valid[1], valid[2]))
        bias[at, :block, :block] = jnp.where(same & (position < length), 0.0, MASKED)


def half_masks():
    lane = lax.broadcasted_iota(jnp.int32, (1, LANES), 1)
    low = (lane < LANES // 2).astype(F32)
    return low.astype(BF16), (1.0 - low).astype(BF16)


def by_block(info, body):
    @pl.when(info[BUCKET] == 1)
    def _():
        body(2 * SEGMENT, ROWS // (2 * SEGMENT))

    @pl.when(info[BUCKET] != 1)
    def _():
        body(3 * SEGMENT, ROWS // (3 * SEGMENT))


def attention(info, qkv, context, lse, bias):
    width = context.shape[1]
    low, high = half_masks()

    def body(block, count):
        write_bias(info, bias, block, count)

        def pair_step(pair, carry):
            at_q = pl.multiple_of(pair * LANES, LANES)
            at_k = pl.multiple_of(width + pair * LANES, LANES)
            at_v = pl.multiple_of(2 * width + pair * LANES, LANES)
            is_low = lax.broadcasted_iota(jnp.int32, (block, LANES), 1) < LANES // 2
            for at in range(count):
                rows = pl.ds(at * block, block)
                q = qkv[rows, pl.ds(at_q, LANES)]
                k = qkv[rows, pl.ds(at_k, LANES)]
                v = qkv[rows, pl.ds(at_v, LANES)]
                parts = []
                for half, mask in enumerate((low, high)):
                    scores = dot_nt(k * mask, q) + bias[at, :block, :block]
                    top = jnp.max(scores, axis=0, keepdims=True)
                    weights = jnp.exp(scores - top)
                    total = jnp.sum(weights, axis=0, keepdims=True)
                    probs = weights * (1.0 / total)
                    lse[2 * pair + half, at : at + 1, :block] = top + jnp.log(total)
                    parts.append(dot_tn(probs.astype(BF16), v))
                context[rows, pl.ds(at_q, LANES)] = jnp.where(is_low, parts[0], parts[1]).astype(
                    BF16
                )
            return carry

        lax.fori_loop(0, HEADS // 2, pair_step, 0)

    by_block(info, body)


def attention_back(info, qkv, d_context, lse, bias, d_qkv):
    width = d_context.shape[1]
    low, high = half_masks()
    scale = (width // HEADS) ** -0.5

    def body(block, count):
        write_bias(info, bias, block, count)

        def pair_step(pair, carry):
            at_q = pl.multiple_of(pair * LANES, LANES)
            at_k = pl.multiple_of(width + pair * LANES, LANES)
            at_v = pl.multiple_of(2 * width + pair * LANES, LANES)
            is_low = lax.broadcasted_iota(jnp.int32, (block, LANES), 1) < LANES // 2
            for at in range(count):
                rows = pl.ds(at * block, block)
                q = qkv[rows, pl.ds(at_q, LANES)]
                k = qkv[rows, pl.ds(at_k, LANES)]
                v = qkv[rows, pl.ds(at_v, LANES)]
                d_out = d_context[rows, pl.ds(at_q, LANES)]
                d_q, d_k, d_v = [], [], []
                for half, mask in enumerate((low, high)):
                    scores = dot_nt(k * mask, q) + bias[at, :block, :block]
                    probs = jnp.exp(scores - lse[2 * pair + half, at : at + 1, :block])
                    d_probs = dot_nt(v * mask, d_out)
                    d_v.append(dot_nn(probs.astype(BF16), d_out))
                    inner = jnp.sum(probs * d_probs, axis=0, keepdims=True)
                    d_scores = (probs * (d_probs - inner)).astype(BF16)
                    d_k.append(dot_nn(d_scores, q))
                    d_q.append(dot_tn(d_scores, k))
                d_qkv[rows, pl.ds(at_q, LANES)] = (
                    jnp.where(is_low, d_q[0], d_q[1]) * scale
                ).astype(BF16)
                d_qkv[rows, pl.ds(at_k, LANES)] = jnp.where(is_low, d_k[0], d_k[1]).astype(BF16)
                d_qkv[rows, pl.ds(at_v, LANES)] = jnp.where(is_low, d_v[0], d_v[1]).astype(BF16)
            return carry

        lax.fori_loop(0, HEADS // 2, pair_step, 0)

    by_block(info, body)


def norm(values):
    centered = values - jnp.mean(values, axis=-1, keepdims=True)
    inverse = lax.rsqrt(jnp.mean(centered * centered, axis=-1, keepdims=True) + EPSILON)
    return centered * inverse, inverse


def norm_back(upstream, normed, inverse, gain):
    scaled = upstream * gain
    return inverse * (
        scaled
        - jnp.mean(scaled, axis=-1, keepdims=True)
        - normed * jnp.mean(scaled * normed, axis=-1, keepdims=True)
    )


CHUNK = 64


def forward_kernel(n_saved, info, tok, rec, w_a, w_up, w_down, small, bias_up, *refs):
    refs = refs[len(refs) - (n_saved + 1 + n_saved + 11) :]
    saved_out, produced = refs[:n_saved], refs[n_saved]
    scratch = refs[n_saved + 1 :]
    x, qkv, lse, context, n1, inv1, hid, act, d_act, n2, inv2, out = scratch[:n_saved]
    wa, wu, wd, hid_f, acc, bias, sem_x, sem_a, sem_u, sem_d, sem_out = scratch[n_saved:]
    width = x.shape[1]
    ff = act.shape[1]
    tiles = ff // FF_TILE

    @pl.when(info[RUN] == 1)
    def _():
        micro = info[MICRO]
        get_x = fetch_either(info[SECTION] == 0, tok.at[micro], rec, x, sem_x)

        def get_a(j):
            cols = pl.ds(pl.multiple_of(j * width, LANES), width)
            return pltpu.make_async_copy(w_a.at[:, cols], wa.at[:, cols], sem_a.at[j])

        def get_up(j):
            cols = pl.ds(pl.multiple_of(j * FF_TILE, LANES), FF_TILE)
            return pltpu.make_async_copy(w_up.at[:, cols], wu.at[:, cols], sem_u.at[j])

        def get_down(j):
            rows = pl.ds(pl.multiple_of(j * FF_TILE, LANES), FF_TILE)
            return pltpu.make_async_copy(w_down.at[rows, :], wd.at[rows, :], sem_d.at[j])

        for j in range(4):
            get_a(j).start()
        for j in range(tiles):
            get_up(j).start()
        for j in range(tiles):
            get_down(j).start()
        outs = Copies(sem_out)
        waits = []

        def save(index):
            waits.append(outs.start(scratch[index], saved_out[index].at[micro]))

        get_x.wait()
        save(0)

        def project(j, carry):
            get_a(j).wait()
            cols = pl.ds(pl.multiple_of(j * width, LANES), width)
            factor = jnp.where(j == 0, (width // HEADS) ** -0.5, 1.0)
            part = dot_nn(x[...], wa[:, cols]) + small[pl.ds(j, 1), :]
            qkv[:, cols] = (part * factor).astype(BF16)
            return carry

        lax.fori_loop(0, 3, project, 0)
        save(1)
        attention(info, qkv, context, lse, bias)
        save(2)
        save(3)
        get_a(3).wait()
        acc[...] = dot_nn(context[...], wa[:, 3 * width : 4 * width])

        def norm_one(i, carry):
            rows = pl.ds(pl.multiple_of(i * CHUNK, CHUNK), CHUNK)
            total = x[rows, :].astype(F32) + acc[rows, :] + small[BIAS_OUT : BIAS_OUT + 1, :]
            normed, inverse = norm(total)
            n1[rows, :] = normed
            inv1[rows, :] = jnp.broadcast_to(inverse, (CHUNK, LANES))
            hidden = normed * small[GAIN_ATTN : GAIN_ATTN + 1, :] + small[SHIFT_ATTN : SHIFT_ATTN + 1, :]
            hid_f[rows, :] = hidden
            hid[rows, :] = hidden.astype(BF16)
            return carry

        lax.fori_loop(0, ROWS // CHUNK, norm_one, 0)
        save(4)
        save(5)
        save(6)
        acc[...] = hid_f[...] + small[BIAS_DOWN : BIAS_DOWN + 1, :]

        def up(j):
            cols = pl.ds(pl.multiple_of(j * FF_TILE, LANES), FF_TILE)
            get_up(j).wait()
            pre = dot_nn(hid[...], wu[:, cols]) + bias_up[:, cols]
            below = 0.5 * (1.0 + lax.erf(pre * 0.7071067811865476))
            density = jnp.exp(pre * pre * -0.5) * 0.3989422804014327
            act[:, cols] = (pre * below).astype(BF16)
            d_act[:, cols] = (below + pre * density).astype(BF16)

        def down(j):
            cols = pl.ds(pl.multiple_of(j * FF_TILE, LANES), FF_TILE)
            get_down(j).wait()
            acc[...] += dot_nn(act[:, cols], wd[cols, :])

        up(0)

        def ffn_step(j, carry):
            down(j - 1)
            up(j)
            return carry

        lax.fori_loop(1, tiles, ffn_step, 0)
        save(7)
        save(8)
        down(tiles - 1)

        def norm_two(i, carry):
            rows = pl.ds(pl.multiple_of(i * CHUNK, CHUNK), CHUNK)
            normed, inverse = norm(acc[rows, :])
            n2[rows, :] = normed
            inv2[rows, :] = jnp.broadcast_to(inverse, (CHUNK, LANES))
            out[rows, :] = (
                normed * small[GAIN_FFN : GAIN_FFN + 1, :] + small[SHIFT_FFN : SHIFT_FFN + 1, :]
            ).astype(BF16)
            return carry

        lax.fori_loop(0, ROWS // CHUNK, norm_two, 0)
        waits.append(outs.start(out, produced))
        for index in range(9, 12):
            save(index)
        for copy in waits:
            copy.wait()


def saved_shapes(width, ff):
    return (
        ((ROWS, width), BF16),
        ((ROWS, 3 * width), BF16),
        ((HEADS, 8, 256), F32),
        ((ROWS, width), BF16),
        ((ROWS, width), F32),
        ((ROWS, LANES), F32),
        ((ROWS, width), BF16),
        ((ROWS, ff), BF16),
        ((ROWS, ff), BF16),
        ((ROWS, width), F32),
        ((ROWS, LANES), F32),
        ((ROWS, width), BF16),
    )


def hold(shapes):
    return [jax.ShapeDtypeStruct((2,) + shape, kind) for shape, kind in shapes]


def vmem(shapes):
    return [pltpu.VMEM(shape, kind) for shape, kind in shapes]


def forward(info, tokens, received, w_a, w_up, w_down, small, bias_up, saved=None):
    width, ff = w_up.shape
    shapes = saved_shapes(width, ff)
    n = len(shapes)
    tiles = ff // FF_TILE
    aliased = [] if saved is None else list(saved)
    flops = 2 * ROWS * width * (4 * width + 2 * ff) + 4 * ROWS * ROWS * width
    return pl.pallas_call(
        functools.partial(forward_kernel, n),
        in_specs=[SCALARS, ANY, ANY, ANY, ANY, ANY, WHOLE, WHOLE] + [ANY] * len(aliased),
        out_specs=[ANY] * (n + 1),
        out_shape=hold(shapes) + [jax.ShapeDtypeStruct((ROWS, width), BF16)],
        input_output_aliases={8 + i: i for i in range(len(aliased))},
        scratch_shapes=vmem(shapes)
        + [
            pltpu.VMEM((width, 4 * width), BF16),
            pltpu.VMEM((width, ff), BF16),
            pltpu.VMEM((ff, width), BF16),
            pltpu.VMEM((ROWS, width), F32),
            pltpu.VMEM((ROWS, width), F32),
            pltpu.VMEM((3, 3 * SEGMENT, 3 * SEGMENT), F32),
            pltpu.SemaphoreType.DMA,
            pltpu.SemaphoreType.DMA((4,)),
            pltpu.SemaphoreType.DMA((tiles,)),
            pltpu.SemaphoreType.DMA((tiles,)),
            pltpu.SemaphoreType.DMA((n + 1,)),
        ],
        compiler_params=pltpu.CompilerParams(vmem_limit_bytes=VMEM_LIMIT),
        cost_estimate=pl.CostEstimate(flops=flops, bytes_accessed=30_000_000, transcendentals=0),
        name="layer_forward",
    )(info, tokens, received, w_a, w_up, w_down, small, bias_up, *aliased)


def ffn_back_kernel(info, cot, rec, w_up, w_down, small, n1_h, inv1_h, d_act_h, n2_h, inv2_h, *refs):
    refs = refs[len(refs) - (5 + 16) :]
    d_ffn_h, d_pre_h, d_branch_h, sums_h, d_first_h = refs[:5]
    (
        g,
        n1,
        inv1,
        d_act,
        n2,
        inv2,
        d_ffn,
        d_pre,
        d_branch,
        sums,
        d_second,
        wu,
        wd,
        acc,
        sem_in,
        sem_out,
    ) = refs[5:]
    width = g.shape[1]
    ff = d_pre.shape[1]
    tiles = ff // FF_TILE

    @pl.when(info[RUN] == 1)
    def _():
        micro = info[MICRO]
        get_g = fetch_either(info[SECTION] == 1, cot.at[micro], rec, g, sem_in.at[0])

        def get_up(j):
            cols = pl.ds(pl.multiple_of(j * FF_TILE, LANES), FF_TILE)
            return pltpu.make_async_copy(w_up.at[:, cols], wu.at[:, cols], sem_in.at[8 + j])

        def get_down(j):
            rows = pl.ds(pl.multiple_of(j * FF_TILE, LANES), FF_TILE)
            return pltpu.make_async_copy(w_down.at[rows, :], wd.at[rows, :], sem_in.at[8 + tiles + j])

        gets = [
            pltpu.make_async_copy(src.at[micro], dst, sem_in.at[1 + i])
            for i, (src, dst) in enumerate(
                ((n2_h, n2), (inv2_h, inv2), (d_act_h, d_act), (n1_h, n1), (inv1_h, inv1))
            )
        ]
        gets[0].start()
        gets[1].start()
        get_down(0).start()
        gets[2].start()
        for j in range(tiles):
            get_up(j).start()
            if j + 1 < tiles:
                get_down(j + 1).start()
        gets[3].start()
        gets[4].start()
        outs = Copies(sem_out)
        waits = []
        get_g.wait()
        gets[0].wait()
        gets[1].wait()
        zeros = jnp.zeros((8, width), F32)

        def back_two(i, carry):
            sum_g, sum_gn, sum_d = carry
            rows = pl.ds(pl.multiple_of(i * CHUNK, CHUNK), CHUNK)
            upstream = g[rows, :].astype(F32)
            normed = n2[rows, :]
            grad = norm_back(upstream, normed, inv2[rows, :1], small[GAIN_FFN : GAIN_FFN + 1, :])
            d_second[rows, :] = grad
            low = grad.astype(BF16)
            d_ffn[rows, :] = low
            return (
                sum_g + fold(upstream),
                sum_gn + fold(upstream * normed),
                sum_d + fold(low.astype(F32)),
            )

        sum_g, sum_gn, sum_d = lax.fori_loop(0, ROWS // CHUNK, back_two, (zeros, zeros, zeros))
        waits.append(outs.start(d_ffn, d_ffn_h.at[micro]))
        sums[1:2, :width] = jnp.sum(sum_d, axis=0, keepdims=True)
        sums[1:2, width : 2 * width] = jnp.sum(sum_gn, axis=0, keepdims=True)
        sums[1:2, 2 * width : 3 * width] = jnp.sum(sum_g, axis=0, keepdims=True)
        gets[2].wait()
        acc[...] = d_second[...]

        def first(j):
            cols = pl.ds(pl.multiple_of(j * FF_TILE, LANES), FF_TILE)
            get_down(j).wait()
            low = (dot_nt(d_ffn[...], wd[cols, :]) * d_act[:, cols].astype(F32)).astype(BF16)
            d_pre[:, cols] = low
            sums[0:1, cols] = jnp.sum(low.astype(F32), axis=0, keepdims=True)

        def second(j):
            cols = pl.ds(pl.multiple_of(j * FF_TILE, LANES), FF_TILE)
            get_up(j).wait()
            acc[...] += dot_nt(d_pre[:, cols], wu[:, cols])

        first(0)

        def ffn_step(j, carry):
            second(j - 1)
            first(j)
            return carry

        lax.fori_loop(1, tiles, ffn_step, 0)
        waits.append(outs.start(d_pre, d_pre_h.at[micro]))
        second(tiles - 1)
        gets[3].wait()
        gets[4].wait()

        def back_one(i, carry):
            sum_g, sum_gn, sum_d = carry
            rows = pl.ds(pl.multiple_of(i * CHUNK, CHUNK), CHUNK)
            upstream = acc[rows, :]
            normed = n1[rows, :]
            grad = norm_back(upstream, normed, inv1[rows, :1], small[GAIN_ATTN : GAIN_ATTN + 1, :])
            d_second[rows, :] = grad
            low = grad.astype(BF16)
            d_branch[rows, :] = low
            return (
                sum_g + fold(upstream),
                sum_gn + fold(upstream * normed),
                sum_d + fold(low.astype(F32)),
            )

        sum_g, sum_gn, sum_d = lax.fori_loop(0, ROWS // CHUNK, back_one, (zeros, zeros, zeros))
        sums[1:2, 3 * width :] = jnp.sum(sum_gn, axis=0, keepdims=True)
        sums[2:3, :width] = jnp.sum(sum_g, axis=0, keepdims=True)
        sums[2:3, width : 2 * width] = jnp.sum(sum_d, axis=0, keepdims=True)
        waits.append(outs.start(d_branch, d_branch_h.at[micro]))
        waits.append(outs.start(d_second, d_first_h))
        waits.append(outs.start(sums, sums_h.at[micro]))
        for copy in waits:
            copy.wait()


def ffn_back(info, cotangent, received, w_up, w_down, small, saved, held=None):
    width, ff = w_up.shape
    tiles = ff // FF_TILE
    n1, inv1, d_act, n2, inv2 = saved[4], saved[5], saved[8], saved[9], saved[10]
    shapes = (
        ((ROWS, width), BF16),
        ((ROWS, ff), BF16),
        ((ROWS, width), BF16),
        ((8, ff), F32),
    )
    aliased = [] if held is None else list(held)
    return pl.pallas_call(
        ffn_back_kernel,
        in_specs=[SCALARS, ANY, ANY, ANY, ANY, WHOLE] + [ANY] * (5 + len(aliased)),
        out_specs=[ANY] * 5,
        out_shape=hold(shapes) + [jax.ShapeDtypeStruct((ROWS, width), F32)],
        input_output_aliases={11 + i: i for i in range(len(aliased))},
        scratch_shapes=vmem(
            (
                ((ROWS, width), BF16),
                ((ROWS, width), F32),
                ((ROWS, LANES), F32),
                ((ROWS, ff), BF16),
                ((ROWS, width), F32),
                ((ROWS, LANES), F32),
            )
            + shapes
            + (
                ((ROWS, width), F32),
                ((width, ff), BF16),
                ((ff, width), BF16),
                ((ROWS, width), F32),
            )
        )
        + [pltpu.SemaphoreType.DMA((8 + 2 * tiles,)), pltpu.SemaphoreType.DMA((5,))],
        compiler_params=pltpu.CompilerParams(vmem_limit_bytes=VMEM_LIMIT),
        cost_estimate=pl.CostEstimate(
            flops=4 * ROWS * width * ff, bytes_accessed=20_000_000, transcendentals=0
        ),
        name="ffn_backward",
    )(info, cotangent, received, w_up, w_down, small, n1, inv1, d_act, n2, inv2, *aliased)


def attn_back_kernel(info, w_a, d_first_h, d_branch_h, qkv_h, lse_h, *refs):
    refs = refs[len(refs) - (4 + 13) :]
    d_qkv_h, grad_h, sums_h, produced = refs[:4]
    d_first, d_branch, qkv, lse, d_qkv, grad, sums, wa, d_context, bias, acc, sem_in, sem_out = refs[4:]
    width = grad.shape[1]

    @pl.when(info[RUN] == 1)
    def _():
        micro = info[MICRO]

        def get_a(j):
            cols = pl.ds(pl.multiple_of(j * width, LANES), width)
            return pltpu.make_async_copy(w_a.at[:, cols], wa.at[:, cols], sem_in.at[j])

        gets = [
            pltpu.make_async_copy(src, dst, sem_in.at[4 + i])
            for i, (src, dst) in enumerate(
                (
                    (d_branch_h.at[micro], d_branch),
                    (qkv_h.at[micro], qkv),
                    (lse_h.at[micro], lse),
                    (d_first_h, d_first),
                )
            )
        ]
        gets[0].start()
        get_a(3).start()
        gets[1].start()
        gets[2].start()
        for j in range(3):
            get_a(j).start()
        gets[3].start()
        outs = Copies(sem_out)
        waits = []
        gets[0].wait()
        get_a(3).wait()
        d_context[...] = dot_nt(d_branch[...], wa[:, 3 * width : 4 * width]).astype(BF16)
        gets[1].wait()
        gets[2].wait()
        attention_back(info, qkv, d_context, lse, bias, d_qkv)
        waits.append(outs.start(d_qkv, d_qkv_h.at[micro]))
        for row, at in ((0, 0), (1, 2 * width)):
            sums[row : row + 1, :] = jnp.sum(
                fold(d_qkv[:, at : at + width].astype(F32)), axis=0, keepdims=True
            )
        waits.append(outs.start(sums, sums_h.at[micro]))
        gets[3].wait()
        acc[...] = d_first[...]

        def project(j, carry):
            get_a(j).wait()
            cols = pl.ds(pl.multiple_of(j * width, LANES), width)
            acc[...] += dot_nt(d_qkv[:, cols], wa[:, cols])
            return carry

        lax.fori_loop(0, 3, project, 0)
        grad[...] = acc[...].astype(BF16)
        waits.append(outs.start(grad, produced))
        waits.append(outs.start(grad, grad_h.at[micro]))
        for copy in waits:
            copy.wait()


def attn_back(info, w_a, d_first, d_branch, saved, held=None):
    width = d_first.shape[1]
    shapes = (
        ((ROWS, 3 * width), BF16),
        ((ROWS, width), BF16),
        ((8, width), F32),
    )
    aliased = [] if held is None else list(held)
    flops = 2 * ROWS * width * 4 * width + 10 * ROWS * ROWS * width
    return pl.pallas_call(
        attn_back_kernel,
        in_specs=[SCALARS] + [ANY] * (5 + len(aliased)),
        out_specs=[ANY] * 4,
        out_shape=hold(shapes) + [jax.ShapeDtypeStruct((ROWS, width), BF16)],
        input_output_aliases={6 + i: i for i in range(len(aliased))},
        scratch_shapes=vmem(
            (
                ((ROWS, width), F32),
                ((ROWS, width), BF16),
                ((ROWS, 3 * width), BF16),
                ((HEADS, 8, 256), F32),
            )
            + shapes
            + (
                ((width, 4 * width), BF16),
                ((ROWS, width), BF16),
                ((3, 3 * SEGMENT, 3 * SEGMENT), F32),
                ((ROWS, width), F32),
            )
        )
        + [pltpu.SemaphoreType.DMA((8,)), pltpu.SemaphoreType.DMA((4,))],
        compiler_params=pltpu.CompilerParams(vmem_limit_bytes=VMEM_LIMIT),
        cost_estimate=pl.CostEstimate(flops=flops, bytes_accessed=15_000_000, transcendentals=0),
        name="attention_backward",
    )(info, w_a, d_first, d_branch, saved[1], saved[2], *aliased)


def weight_grad_kernel(a, b, out):
    out[...] = (dot_tn(a[0], b[0]) + dot_tn(a[1], b[1])).astype(BF16)


def weight_grad(a, b, name):
    rows, m = a.shape[1:]
    n = b.shape[2]
    tile = 256
    return pl.pallas_call(
        weight_grad_kernel,
        grid=(m // tile,),
        in_specs=[
            pl.BlockSpec((2, rows, tile), lambda i: (0, 0, i)),
            pl.BlockSpec((2, rows, n), lambda i: (0, 0, 0)),
        ],
        out_specs=pl.BlockSpec((tile, n), lambda i: (i, 0)),
        out_shape=jax.ShapeDtypeStruct((m, n), BF16),
        compiler_params=pltpu.CompilerParams(vmem_limit_bytes=VMEM_LIMIT),
        cost_estimate=pl.CostEstimate(
            flops=4 * rows * m * n, bytes_accessed=2 * m * n, transcendentals=0
        ),
        name=name,
    )(a, b)


def passed_along(block, axis, distance):
    devices = range(lax.axis_size(axis))
    route = [(i - distance, i) for i in devices if i - distance in devices]
    return lax.ppermute(block, axis, route)


def on_device(
    tokens,
    cotangent,
    bucket,
    lengths,
    w_qkv,
    bias_q,
    bias_v,
    w_out,
    bias_out,
    gain_attn,
    shift_attn,
    w_up,
    bias_up,
    w_down,
    bias_down,
    gain_ffn,
    shift_ffn,
):
    section = lax.axis_index("section")
    width = tokens.shape[2]
    ff = w_up.shape[2]
    share = bias_q.shape[1]
    n_dp = width // share
    vectors = (bias_q, bias_v, bias_out, gain_attn, shift_attn, bias_down, gain_ffn, shift_ffn)

    part_a = jnp.concatenate([w_qkv[0], w_out[0]], axis=1).astype(BF16)
    part_s = jnp.concatenate(vectors + (bias_up,), axis=1).astype(BF16)
    w_a = lax.all_gather(part_a, "dp", axis=0, tiled=True)
    smalls = lax.all_gather(part_s, "dp", axis=0, tiled=True)
    full_up = lax.all_gather(w_up[0].astype(BF16), "dp", axis=0, tiled=True)
    full_down = lax.all_gather(w_down[0].astype(BF16), "dp", axis=0, tiled=True)
    rows = smalls[:, : 8 * share].reshape(n_dp, 8, share).transpose(1, 0, 2).reshape(8, width)
    rows = rows.astype(F32)
    small = jnp.concatenate(
        [rows[:1], jnp.zeros((1, width), F32), rows[1:], jnp.zeros((7, width), F32)]
    )
    full_bias_up = smalls[:, 8 * share :].reshape(1, ff).astype(F32)

    def info(step, micro):
        picked = jnp.clip(micro, 0, 1)
        run = ((micro >= 0) & (micro <= 1)).astype(jnp.int32)
        head = jnp.stack([run, picked, section, lax.dynamic_index_in_dim(bucket, picked, 0, False)[0]])
        return jnp.concatenate([head, lax.dynamic_index_in_dim(lengths, picked, 0, False)])

    ahead = [info(step, step - section) for step in range(3)]
    back = [info(step, step - 1 + section) for step in range(3)]
    none = jnp.zeros((ROWS, width), BF16)

    weights = (w_a, full_up, full_down, small, full_bias_up)
    *saved, made = forward(ahead[0], tokens, none, *weights)
    got = passed_along(made, "section", 1)
    *saved, made = forward(ahead[1], tokens, got, *weights, saved=saved)
    got = passed_along(made, "section", 1)

    def backward(step, upstream, saved, held):
        ffn_held, attn_held = (None, None) if held is None else held
        *ffn_held, d_first = ffn_back(
            back[step], cotangent, upstream, full_up, full_down, small, saved, ffn_held
        )
        *attn_held, made = attn_back(back[step], w_a, d_first, ffn_held[2], saved, attn_held)
        return (ffn_held, attn_held), made

    held, made = backward(0, none, saved, None)
    sent = passed_along(made, "section", -1)
    *saved, made = forward(ahead[2], tokens, got, *weights, saved=saved)
    held, made = backward(1, sent, saved, held)
    sent = passed_along(made, "section", -1)
    (ffn_held, attn_held), made = backward(2, sent, saved, held)
    d_ffn, d_pre, d_branch, sums_ffn = ffn_held
    d_qkv, input_grads, sums_attn = attn_held

    g_down = weight_grad(saved[7], d_ffn, "grad_down")
    g_up = weight_grad(saved[6], d_pre, "grad_up")
    g_out = weight_grad(saved[3], d_branch, "grad_out")
    g_qkv = weight_grad(saved[0], d_qkv, "grad_qkv")
    total = sums_ffn[0] + sums_ffn[1]
    total_attn = sums_attn[0] + sums_attn[1]
    vector = [
        total_attn[0],
        total_attn[1],
        total[2, width : 2 * width],
        total[1, 3 * width :],
        total[2, :width],
        total[1, :width],
        total[1, width : 2 * width],
        total[1, 2 * width : 3 * width],
    ]
    table = jnp.stack(vector).reshape(8, n_dp, share).transpose(1, 0, 2).reshape(n_dp, 8 * share)
    table = jnp.concatenate([table, total[0].reshape(n_dp, ff // n_dp)], axis=1)

    def summed(values):
        return lax.psum_scatter(values, "dp", scatter_dimension=0, tiled=True).astype(F32)[None]

    g_down, g_up, g_out, g_qkv = (summed(g) for g in (g_down, g_up, g_out, g_qkv))
    table = summed(table)[0]
    g_vectors = [table[:, i * share : (i + 1) * share] for i in range(8)]
    g_bias_up = table[:, 8 * share :]
    (
        g_bias_q,
        g_bias_v,
        g_bias_out,
        g_gain_attn,
        g_shift_attn,
        g_bias_down,
        g_gain_ffn,
        g_shift_ffn,
    ) = g_vectors
    return (
        saved[11][None],
        input_grads[None],
        g_qkv,
        g_bias_q,
        g_bias_v,
        g_out,
        g_bias_out,
        g_gain_attn,
        g_shift_attn,
        g_up,
        g_bias_up,
        g_down,
        g_bias_down,
        g_gain_ffn,
        g_shift_ffn,
    )


def solution(mesh):
    matrix = P("section", "dp", None)
    vector = P("section", "dp")
    rows = P(None, "dp", None)
    outs = P("section", None, "dp", None)
    params = (
        matrix,
        vector,
        vector,
        matrix,
        vector,
        vector,
        vector,
        matrix,
        vector,
        matrix,
        vector,
        vector,
        vector,
    )
    return jax.shard_map(
        on_device,
        mesh=mesh,
        in_specs=(rows, rows, P(None, "dp"), P(None, "dp")) + params,
        out_specs=(outs, outs) + params,
        check_vma=False,
    )
```

```python
import functools

import jax
import jax.numpy as jnp
from jax import lax
from jax.experimental import pallas as pl
from jax.experimental.pallas import tpu as pltpu
from jax.sharding import PartitionSpec as P

HEADS = 12
SEGMENT = 64
PAIRS = 6
ROWS = 384
EPSILON = 1e-06
MASKED = -1000000000.0
LANES = 128
FF_TILE = 1024
LIMIT = 10
LIMIT_GRAD = 16
VMEM_LIMIT = 60 * 1024 * 1024
F32 = jnp.float32
BF16 = jnp.bfloat16

BIAS_Q, BIAS_K, BIAS_V, BIAS_OUT, GAIN_ATTN, SHIFT_ATTN, BIAS_DOWN, GAIN_FFN, SHIFT_FFN = range(9)
RUN, MICRO, SECTION, BUCKET, LENGTHS = range(5)
CORE, Y = LENGTHS + PAIRS, LENGTHS + PAIRS + 1

ANY = pl.BlockSpec(memory_space=pl.ANY)
WHOLE = pl.BlockSpec(memory_space=pltpu.VMEM)
SCALARS = pl.BlockSpec(memory_space=pltpu.SMEM)


def dot_nn(a, b):
    return lax.dot_general(a, b, (((1,), (0,)), ((), ())), preferred_element_type=F32)


def dot_nt(a, b):
    return lax.dot_general(a, b, (((1,), (1,)), ((), ())), preferred_element_type=F32)


def dot_tn(a, b):
    return lax.dot_general(a, b, (((0,), (0,)), ((), ())), preferred_element_type=F32)


class Row:
    def __init__(self, table, row):
        self.table, self.row = table, row

    def __getitem__(self, at):
        return self.table[self.row, at]


def fold(values):
    rows, n = values.shape
    return jnp.sum(values.reshape(rows // 8, 8, n), axis=0)


def write_bias(info, bias, block, count):
    segment = (info[BUCKET] + 1) * SEGMENT
    per_block = jnp.where(info[BUCKET] == 0, block // SEGMENT, 1)
    k_row = lax.broadcasted_iota(jnp.int32, (block, block), 0)
    q_row = lax.broadcasted_iota(jnp.int32, (block, block), 1)

    def pair_of(row):
        return (row >= segment).astype(jnp.int32) + (row >= 2 * segment).astype(jnp.int32)

    k_pair = pair_of(k_row)
    same = k_pair == pair_of(q_row)
    position = k_row - k_pair * segment
    for at in range(count):
        valid = [
            jnp.minimum(info[LENGTHS + jnp.minimum(at * per_block + i, PAIRS - 1)], segment)
            for i in range(3)
        ]
        length = jnp.where(k_pair == 0, valid[0], jnp.where(k_pair == 1, valid[1], valid[2]))
        bias[at, :block, :block] = jnp.where(same & (position < length), 0.0, MASKED)


def half_masks():
    lane = lax.broadcasted_iota(jnp.int32, (1, LANES), 1)
    low = (lane < LANES // 2).astype(F32)
    return low.astype(BF16), (1.0 - low).astype(BF16)


def by_block(info, body):
    @pl.when(info[BUCKET] == 1)
    def _():
        body(2 * SEGMENT, ROWS // (2 * SEGMENT))

    @pl.when(info[BUCKET] != 1)
    def _():
        body(3 * SEGMENT, ROWS // (3 * SEGMENT))


def attention(info, qkv, context, lse, bias):
    width = context.shape[1]
    low, high = half_masks()

    def body(block, count):
        write_bias(info, bias, block, count)

        def pair_step(pair, carry):
            at_q = pl.multiple_of(pair * LANES, LANES)
            at_k = pl.multiple_of(width + pair * LANES, LANES)
            at_v = pl.multiple_of(2 * width + pair * LANES, LANES)
            is_low = lax.broadcasted_iota(jnp.int32, (block, LANES), 1) < LANES // 2
            units = [(at, half) for at in range(count) for half in range(2)]
            rows = [pl.ds(at * block, block) for at in range(count)]
            q = [qkv[r, pl.ds(at_q, LANES)] for r in rows]
            k = [qkv[r, pl.ds(at_k, LANES)] for r in rows]
            v = [qkv[r, pl.ds(at_v, LANES)] for r in rows]
            scores = [
                dot_nt(k[at] * (low, high)[half], q[at]) + bias[at, :block, :block]
                for at, half in units
            ]
            tops = [jnp.max(x, axis=0, keepdims=True) for x in scores]
            weights = [jnp.exp(x - top) for x, top in zip(scores, tops)]
            totals = [jnp.sum(x, axis=0, keepdims=True) for x in weights]
            probs = [(x * (1.0 / total)).astype(BF16) for x, total in zip(weights, totals)]
            parts = [dot_tn(x, v[at]) for x, (at, half) in zip(probs, units)]
            for index, (at, half) in enumerate(units):
                lse[2 * pair + half, at : at + 1, :block] = tops[index] + jnp.log(
                    totals[index]
                )
            for at in range(count):
                context[rows[at], pl.ds(at_q, LANES)] = jnp.where(
                    is_low, parts[2 * at], parts[2 * at + 1]
                ).astype(BF16)
            return carry

        lax.fori_loop(0, HEADS // 2, pair_step, 0)

    by_block(info, body)


def attention_back(info, qkv, d_context, lse, bias, d_qkv):
    width = d_context.shape[1]
    low, high = half_masks()
    scale = (width // HEADS) ** -0.5

    def body(block, count):
        write_bias(info, bias, block, count)

        def pair_step(pair, carry):
            at_q = pl.multiple_of(pair * LANES, LANES)
            at_k = pl.multiple_of(width + pair * LANES, LANES)
            at_v = pl.multiple_of(2 * width + pair * LANES, LANES)
            is_low = lax.broadcasted_iota(jnp.int32, (block, LANES), 1) < LANES // 2
            units = [(at, half) for at in range(count) for half in range(2)]
            rows = [pl.ds(at * block, block) for at in range(count)]
            q = [qkv[r, pl.ds(at_q, LANES)] for r in rows]
            k = [qkv[r, pl.ds(at_k, LANES)] for r in rows]
            v = [qkv[r, pl.ds(at_v, LANES)] for r in rows]
            d_out = [d_context[r, pl.ds(at_q, LANES)] for r in rows]
            scores = [
                dot_nt(k[at] * (low, high)[half], q[at]) + bias[at, :block, :block]
                for at, half in units
            ]
            d_probs = [dot_nt(v[at] * (low, high)[half], d_out[at]) for at, half in units]
            probs = [
                jnp.exp(x - lse[2 * pair + half, at : at + 1, :block])
                for x, (at, half) in zip(scores, units)
            ]
            d_v = [dot_nn(x.astype(BF16), d_out[at]) for x, (at, half) in zip(probs, units)]
            inner = [jnp.sum(x * d_x, axis=0, keepdims=True) for x, d_x in zip(probs, d_probs)]
            d_scores = [
                (x * (d_x - total)).astype(BF16)
                for x, d_x, total in zip(probs, d_probs, inner)
            ]
            d_k = [dot_nn(x, q[at]) for x, (at, half) in zip(d_scores, units)]
            d_q = [dot_tn(x, k[at]) for x, (at, half) in zip(d_scores, units)]
            for at in range(count):
                one, two = 2 * at, 2 * at + 1
                r = rows[at]
                d_qkv[r, pl.ds(at_q, LANES)] = (
                    jnp.where(is_low, d_q[one], d_q[two]) * scale
                ).astype(BF16)
                d_qkv[r, pl.ds(at_k, LANES)] = jnp.where(
                    is_low, d_k[one], d_k[two]
                ).astype(BF16)
                d_qkv[r, pl.ds(at_v, LANES)] = jnp.where(
                    is_low, d_v[one], d_v[two]
                ).astype(BF16)
            return carry

        lax.fori_loop(0, HEADS // 2, pair_step, 0)

    by_block(info, body)


def norm(values):
    centered = values - jnp.mean(values, axis=-1, keepdims=True)
    inverse = lax.rsqrt(jnp.mean(centered * centered, axis=-1, keepdims=True) + EPSILON)
    return centered * inverse, inverse


def norm_back(upstream, normed, inverse, gain):
    scaled = upstream * gain
    return inverse * (
        scaled
        - jnp.mean(scaled, axis=-1, keepdims=True)
        - normed * jnp.mean(scaled * normed, axis=-1, keepdims=True)
    )


CHUNK = 64


def by_rows(step, carry=0):
    def body(i, carry):
        return step(pl.ds(pl.multiple_of(i * CHUNK, CHUNK), CHUNK), carry)

    return lax.fori_loop(0, ROWS // CHUNK, body, carry)


def carry_over(src, dst):
    if src.shape[0] == ROWS:

        def step(rows, carry):
            dst[rows, :] = src[rows, :]
            return carry

        by_rows(step)
    else:
        dst[...] = src[...]


def kernel_call(body, name, step, ins, out_shapes, held, after, scratch, flops, limit):
    held = [] if held is None else list(held)
    given = len(ins) - 1

    def kernel(table, *refs):
        info = Row(table, step)
        kept = refs[given : given + len(held)]
        outs = refs[given + len(held) + len(after) :]

        @pl.when(info[RUN] == 1)
        def _():
            body(info, *refs[:given], *outs)

        if held:

            @pl.when(info[RUN] != 1)
            def _():
                for src, dst in zip(kept, outs):
                    carry_over(src, dst)

    return pl.pallas_call(
        kernel,
        in_specs=[SCALARS] + [WHOLE] * (given + len(held)) + [ANY] * len(after),
        out_specs=[WHOLE] * len(out_shapes),
        out_shape=[jax.ShapeDtypeStruct(shape, kind) for shape, kind in out_shapes],
        input_output_aliases={1 + given + i: i for i in range(len(held))},
        scratch_shapes=scratch,
        compiler_params=pltpu.CompilerParams(vmem_limit_bytes=limit * 1024 * 1024),
        cost_estimate=pl.CostEstimate(flops=flops, bytes_accessed=0, transcendentals=0),
        name=name,
    )(*ins, *held, *after)


def forward_attn_body(info, tok, rec, w_a, small, x, qkv, lse, context, n1, inv1, hid, acc, bias):
    width = x.shape[1]

    micro = info[MICRO]

    @pl.when(info[SECTION] == 0)
    def _():
        x[...] = tok[micro]

    @pl.when(info[SECTION] != 0)
    def _():
        x[...] = rec[...]

    for j, (row, factor) in enumerate(
        ((BIAS_Q, (width // HEADS) ** -0.5), (BIAS_K, 1.0), (BIAS_V, 1.0))
    ):
        cols = slice(j * width, (j + 1) * width)
        part = dot_nn(x[...], w_a[:, cols]) + small[row : row + 1, :]
        qkv[:, cols] = (part * factor).astype(BF16)
    attention(info, qkv, context, lse, bias)
    acc[...] = dot_nn(context[...], w_a[:, 3 * width : 4 * width])

    def norm_one(rows, carry):
        total = x[rows, :].astype(F32) + acc[rows, :]
        normed, inverse = norm(total + small[BIAS_OUT : BIAS_OUT + 1, :])
        n1[rows, :] = normed
        inv1[rows, :] = jnp.broadcast_to(inverse, (CHUNK, LANES))
        hidden = normed * small[GAIN_ATTN : GAIN_ATTN + 1, :]
        hid[rows, :] = (hidden + small[SHIFT_ATTN : SHIFT_ATTN + 1, :]).astype(BF16)
        return carry

    by_rows(norm_one)


def forward_ffn_body(
    info, w_up, w_down, small, bias_up, n1, hid, act, d_act, n2, inv2, out, acc
):
    ff = act.shape[1]

    def up(j):
        cols = slice(j * FF_TILE, (j + 1) * FF_TILE)
        pre = dot_nn(hid[...], w_up[:, cols]) + bias_up[:, cols]
        below = 0.5 * (1.0 + lax.erf(pre * 0.7071067811865476))
        density = jnp.exp(pre * pre * -0.5) * 0.3989422804014327
        act[:, cols] = (pre * below).astype(BF16)
        d_act[:, cols] = (below + pre * density).astype(BF16)

    def down(j):
        cols = slice(j * FF_TILE, (j + 1) * FF_TILE)
        part = dot_nn(act[:, cols], w_down[cols, :])
        acc[...] = part if j == 0 else acc[...] + part

    up(0)
    for j in range(1, ff // FF_TILE):
        up(j)
        down(j - 1)
    down(ff // FF_TILE - 1)

    def norm_two(rows, carry):
        hidden = n1[rows, :] * small[GAIN_ATTN : GAIN_ATTN + 1, :]
        hidden = hidden + small[SHIFT_ATTN : SHIFT_ATTN + 1, :]
        normed, inverse = norm(hidden + acc[rows, :] + small[BIAS_DOWN : BIAS_DOWN + 1, :])
        n2[rows, :] = normed
        inv2[rows, :] = jnp.broadcast_to(inverse, (CHUNK, LANES))
        low = (
            normed * small[GAIN_FFN : GAIN_FFN + 1, :] + small[SHIFT_FFN : SHIFT_FFN + 1, :]
        ).astype(BF16)
        out[rows, :] = low
        return carry

    by_rows(norm_two)


def bias_scratch():
    return pltpu.VMEM((3, 3 * SEGMENT, 3 * SEGMENT), F32)


def forward_attn(step, info, tokens, received, w_a, small, held=None, after=()):
    width = small.shape[1]
    shapes = (
        ((ROWS, width), BF16),
        ((ROWS, 3 * width), BF16),
        ((HEADS, 8, 256), F32),
        ((ROWS, width), BF16),
        ((ROWS, width), F32),
        ((ROWS, LANES), F32),
        ((ROWS, width), BF16),
    )
    return kernel_call(
        forward_attn_body,
        "forward_attn",
        step,
        (info, tokens, received, w_a, small),
        shapes,
        held,
        after,
        [pltpu.VMEM((ROWS, width), F32), bias_scratch()],
        8 * ROWS * width * width + 4 * ROWS * ROWS * width,
        LIMIT,
    )


def forward_ffn(step, info, w_up, w_down, small, bias_up, n1, hid, held=None, after=()):
    width, ff = small.shape[1], bias_up.shape[1]
    shapes = (
        ((ROWS, ff), BF16),
        ((ROWS, ff), BF16),
        ((ROWS, width), F32),
        ((ROWS, LANES), F32),
        ((ROWS, width), BF16),
    )
    return kernel_call(
        forward_ffn_body,
        "forward_ffn",
        step,
        (info, w_up, w_down, small, bias_up, n1, hid),
        shapes,
        held,
        after,
        [pltpu.VMEM((ROWS, width), F32)],
        4 * ROWS * width * ff,
        LIMIT,
    )


def norm_back_rows(upstream, normed, inverse, gain, grad, low):
    zeros = jnp.zeros((8, grad.shape[1]), F32)

    def step(rows, carry):
        up, nm = upstream(rows), normed(rows)
        values = norm_back(up, nm, inverse(rows), gain)
        grad[rows, :] = values
        rounded = values.astype(BF16)
        low(rows, rounded)
        return (
            carry[0] + fold(up),
            carry[1] + fold(up * nm),
            carry[2] + fold(rounded.astype(F32)),
        )

    sums = by_rows(step, (zeros, zeros, zeros))
    return [jnp.sum(part, axis=0, keepdims=True) for part in sums]


def ffn_back_body(
    info,
    cot,
    rec,
    w_up,
    w_down,
    small,
    n1,
    inv1,
    d_act,
    n2,
    inv2,
    d_ffn,
    d_pre,
    d_branch,
    sums,
    d_first,
    acc,
):
    width = rec.shape[1]
    ff = d_pre.shape[1]
    tiles = ff // FF_TILE

    micro = info[MICRO]
    last = info[SECTION] == 1

    def upstream(rows):
        return jnp.where(last, cot[micro, rows, :], rec[rows, :]).astype(F32)

    def keep_ffn(rows, low):
        d_ffn[rows, :] = low

    sum_g, sum_gn, sum_d = norm_back_rows(
        upstream,
        lambda rows: n2[rows, :],
        lambda rows: inv2[rows, :1],
        small[GAIN_FFN : GAIN_FFN + 1, :],
        acc,
        keep_ffn,
    )
    sums[1:2, :width] = sum_d
    sums[1:2, width : 2 * width] = sum_gn
    sums[1:2, 2 * width : 3 * width] = sum_g

    def first(j):
        cols = slice(j * FF_TILE, (j + 1) * FF_TILE)
        part = dot_nt(d_ffn[...], w_down[cols, :]) * d_act[:, cols].astype(F32)
        low = part.astype(BF16)
        d_pre[:, cols] = low
        sums[0:1, cols] = jnp.sum(fold(low.astype(F32)), axis=0, keepdims=True)

    def second(j):
        cols = slice(j * FF_TILE, (j + 1) * FF_TILE)
        acc[...] += dot_nt(d_pre[:, cols], w_up[:, cols])

    first(0)
    for j in range(1, tiles):
        first(j)
        second(j - 1)
    second(tiles - 1)

    def keep_branch(rows, low):
        d_branch[rows, :] = low

    sum_g, sum_gn, sum_d = norm_back_rows(
        lambda rows: acc[rows, :],
        lambda rows: n1[rows, :],
        lambda rows: inv1[rows, :1],
        small[GAIN_ATTN : GAIN_ATTN + 1, :],
        d_first,
        keep_branch,
    )
    sums[1:2, 3 * width :] = sum_gn
    sums[2:3, :width] = sum_g
    sums[2:3, width : 2 * width] = sum_d


def ffn_back(step, info, cotangent, received, w_up, w_down, small, attn, ffn, held=None, after=()):
    width, ff = w_up.shape
    shapes = (
        ((ROWS, width), BF16),
        ((ROWS, ff), BF16),
        ((ROWS, width), BF16),
        ((8, ff), F32),
        ((ROWS, width), F32),
    )
    return kernel_call(
        ffn_back_body,
        "ffn_backward",
        step,
        (info, cotangent, received, w_up, w_down, small, attn[4], attn[5], ffn[1], ffn[2], ffn[3]),
        shapes,
        held,
        after,
        [pltpu.VMEM((ROWS, width), F32)],
        4 * ROWS * width * ff,
        LIMIT,
    )


def attn_back_body(
    info, w_a, d_first, d_branch, qkv, lse, d_qkv, grads, sums, d_context, bias
):
    width = d_first.shape[1]

    d_context[...] = dot_nt(d_branch[...], w_a[:, 3 * width : 4 * width]).astype(BF16)
    attention_back(info, qkv, d_context, lse, bias, d_qkv)
    grad = d_first[...] + dot_nt(d_qkv[...], w_a[:, : 3 * width])
    low = grad.astype(BF16)
    grads[...] = low
    for row, at in ((0, 0), (1, 2 * width)):
        sums[row : row + 1, :] = jnp.sum(
            fold(d_qkv[:, at : at + width].astype(F32)), axis=0, keepdims=True
        )


def attn_back(step, info, w_a, d_first, d_branch, attn, held=None, after=()):
    width = d_first.shape[1]
    shapes = (
        ((ROWS, 3 * width), BF16),
        ((ROWS, width), BF16),
        ((8, width), F32),
    )
    return kernel_call(
        attn_back_body,
        "attention_backward",
        step,
        (info, w_a, d_first, d_branch, attn[1], attn[2]),
        shapes,
        held,
        after,
        [pltpu.VMEM((ROWS, width), BF16), bias_scratch()],
        8 * ROWS * width * width + 10 * ROWS * ROWS * width,
        LIMIT,
    )


def split_blocks(values, place, mine, theirs, cols, first_z=0):
    share = mine.shape[2]
    core, y = place[0], place[1]
    zs = values.shape[0] // (4 * share)
    for z in range(zs):
        for yy in range(2):
            first = values[(z * 4 + yy * 2) * share : (z * 4 + yy * 2 + 1) * share].astype(BF16)
            second = values[(z * 4 + yy * 2 + 1) * share : (z * 4 + yy * 2 + 2) * share].astype(BF16)
            to = jnp.bitwise_xor(y, yy)

            @pl.when(core == 0)
            def _():
                mine[pl.ds(to, 1), first_z + z, :, cols] = first[None]
                theirs[pl.ds(to, 1), first_z + z, :, cols] = second[None]

            @pl.when(core == 1)
            def _():
                theirs[pl.ds(to, 1), first_z + z, :, cols] = first[None]
                mine[pl.ds(to, 1), first_z + z, :, cols] = second[None]


def both(refs, cols=slice(None)):
    return jnp.concatenate([ref[:, cols] for ref in refs], axis=0)


def grad_call(body, name, place, ins, share, n, after):
    shape = jax.ShapeDtypeStruct((2, 4, share, n), BF16)

    def kernel(place, *refs):
        body(place, *refs[: len(ins)], *refs[-2:])

    return pl.pallas_call(
        kernel,
        in_specs=[SCALARS] + [WHOLE] * len(ins) + [ANY] * len(after),
        out_specs=[WHOLE] * 2,
        out_shape=[shape, shape],
        compiler_params=pltpu.CompilerParams(vmem_limit_bytes=LIMIT_GRAD * 1024 * 1024),
        cost_estimate=pl.CostEstimate(
            flops=4 * ROWS * 16 * share * n, bytes_accessed=0, transcendentals=0
        ),
        name=name,
    )(place, *ins, *after)


def grad_by_rows_body(place, a, a2, b, b2, mine, theirs):
    rows = 4 * mine.shape[2]
    right = both((b, b2))
    for z in range(4):
        left = both((a, a2), slice(z * rows, (z + 1) * rows))
        split_blocks(dot_tn(left, right), place, mine, theirs, slice(None), z)


def grad_by_cols_body(place, a, a2, b, b2, mine, theirs):
    tile = 768
    left = both((a, a2))
    for at in range(0, b.shape[1], tile):
        cols = slice(at, at + tile)
        split_blocks(dot_tn(left, both((b, b2), cols)), place, mine, theirs, cols)


def grad_attn_body(
    place, x, x2, d_qkv, d_qkv2, context, context2, d_branch, d_branch2, table, mine, theirs
):
    width = x.shape[1]
    grad_by_cols_body(place, x, x2, d_qkv, d_qkv2, mine, theirs)
    values = dot_tn(both((context, context2)), both((d_branch, d_branch2)))
    split_blocks(values, place, mine, theirs, slice(3 * width, 4 * width))
    split_blocks(table[...], place, mine, theirs, slice(4 * width, 4 * width + LANES))


def grad_by_rows(place, a, b, name, after=()):
    share, n = a[0].shape[1] // 16, b[0].shape[1]
    return grad_call(grad_by_rows_body, name, place, (*a, *b), share, n, after)


def grad_by_cols(place, a, b, name, after=()):
    share, n = a[0].shape[1] // 16, b[0].shape[1]
    return grad_call(grad_by_cols_body, name, place, (*a, *b), share, n, after)


def grad_attn(place, x, d_qkv, context, d_branch, table, after=()):
    width = x[0].shape[1]
    ins = (*x, *d_qkv, *context, *d_branch, table)
    return grad_call(
        grad_attn_body, "grad_attn", place, ins, width // 16, 4 * width + LANES, after
    )


def join_body(place, own, other, own_sibling, other_sibling, out, sems):
    core, y = place[0], place[1]
    share = own.shape[1]
    copies = []
    for src, dy, dc in ((own, 0, 0), (other, 1, 0), (own_sibling, 0, 1), (other_sibling, 1, 1)):
        for z in range(4):
            at = z * 4 + jnp.bitwise_xor(y, dy) * 2 + jnp.bitwise_xor(core, dc)
            rows = pl.ds(pl.multiple_of(at * share, 16), share)
            copy = pltpu.make_async_copy(src.at[z], out.at[rows, :], sems.at[len(copies)])
            copy.start()
            copies.append(copy)
    for copy in copies:
        copy.wait()


def in_order(place, parts, name):
    z, share, n = parts[0].shape
    return pl.pallas_call(
        join_body,
        in_specs=[SCALARS] + [ANY] * 4,
        out_specs=WHOLE,
        out_shape=jax.ShapeDtypeStruct((4 * z * share, n), BF16),
        scratch_shapes=[pltpu.SemaphoreType.DMA((16,))],
        compiler_params=pltpu.CompilerParams(vmem_limit_bytes=24 * 1024 * 1024),
        cost_estimate=pl.CostEstimate(flops=0, bytes_accessed=32 * z * share * n, transcendentals=0),
        name=name,
    )(place, *parts)


def weight_grad(a, b):
    return sum(dot_tn(one, two) for one, two in zip(a, b)).astype(BF16)


def tie(value, *others):
    return lax.optimization_barrier((value, others))[0]


class Grid:
    def __init__(self):
        self.index = lax.axis_index("dp")
        self.z = self.index // 4
        self.y = (self.index // 2) % 2
        self.core = self.index % 2

    def swap_core(self, block):
        return lax.ppermute(block, "dp", [(i, i ^ 1) for i in range(16)])

    def swap_y(self, block):
        return lax.ppermute(block, "dp", [(i, i ^ 2) for i in range(16)])

    def shift(self, block, step, low, high):
        return lax.ppermute(
            block, "dp", [(i, i + 4 * step) for i in range(4 * low, 4 * high + 4)]
        )

    def near(self, block):
        return self.shift(block, 1, 0, 2), self.shift(block, -1, 1, 3)

    def far(self, got):
        up, down = got
        return (
            self.shift(up, 1, 1, 2),
            self.shift(down, -1, 1, 2),
            self.shift(up, 2, 1, 1),
            self.shift(down, -2, 2, 2),
        )

    def in_line(self, block, near, far):
        ups, downs = (near[0], far[0], far[2]), (near[1], far[1], far[3])

        def found(z, at):
            if z == at:
                return block
            return ups[z - at - 1] if z > at else downs[at - z - 1]

        picked = []
        for at in range(4):
            value = found(3, at)
            for z in range(3):
                value = jnp.where(self.z == z, found(z, at), value)
            picked.append(value)
        return jnp.stack(picked)

    def gather(self, part_a, part_up, part_down):
        near_a = self.near(part_a)
        down_other = self.swap_y(part_down)
        far_a = self.far(near_a)
        near_up = self.near(tie(part_up, *near_a))
        own_a = self.in_line(part_a, near_a, far_a)
        other_a = self.swap_y(own_a)
        far_up = self.far(tie(near_up, *far_a))
        down = tie(jnp.stack([part_down, down_other]), *far_a)
        near_down = self.near(down)
        own_up = self.in_line(part_up, near_up, far_up)
        other_up = self.swap_y(own_up)
        far_down = self.far(tie(near_down, *far_up))
        both = self.in_line(down, near_down, far_down)
        own_down, other_down = both[:, 0], both[:, 1]
        return tuple(
            (own, other, self.swap_core(own), self.swap_core(other))
            for own, other in ((own_a, other_a), (own_up, other_up), (own_down, other_down))
        )

    def ordered(self, pieces):
        own, other, own_sibling, other_sibling = pieces

        def by_y(one, two):
            first = self.y == 0
            return jnp.stack([jnp.where(first, one, two), jnp.where(first, two, one)], axis=1)

        mine, theirs = by_y(own, other), by_y(own_sibling, other_sibling)
        first = self.core == 0
        both = jnp.stack([jnp.where(first, mine, theirs), jnp.where(first, theirs, mine)], axis=2)
        return both.reshape((-1,) + both.shape[4:])

    def block(self, total, at):
        return lax.dynamic_index_in_dim(total, jnp.clip(at, 0, 3), 1, keepdims=False)

    def for_far(self, total):
        three_up, three_down = total[:, 3], total[:, 0]
        return tuple(
            part.astype(BF16)
            for part in (
                self.block(total, self.z + 2),
                self.block(total, self.z - 2),
                three_up,
                three_down,
            )
        )

    def send_far(self, sent):
        return (
            self.shift(sent[0], 1, 0, 1),
            self.shift(sent[1], -1, 2, 3),
            self.shift(sent[2], 2, 0, 0),
            self.shift(sent[3], -2, 3, 3),
        )

    def for_near(self, total, got):
        up, down, up_two, down_two = (part.astype(F32) for part in got)
        return (
            (self.block(total, self.z + 1) + up + up_two).astype(BF16),
            (self.block(total, self.z - 1) + down + down_two).astype(BF16),
        )

    def send_near(self, sent):
        return self.shift(sent[0], 1, 0, 2), self.shift(sent[1], -1, 1, 3)

    def line_end(self, total, got):
        return self.block(total, self.z) + got[0].astype(F32) + got[1].astype(F32)


def passed_along(block, axis, distance):
    devices = range(lax.axis_size(axis))
    route = [(i - distance, i) for i in devices if i - distance in devices]
    return lax.ppermute(block, axis, route)


def on_device(
    tokens,
    cotangent,
    bucket,
    lengths,
    w_qkv,
    bias_q,
    bias_v,
    w_out,
    bias_out,
    gain_attn,
    shift_attn,
    w_up,
    bias_up,
    w_down,
    bias_down,
    gain_ffn,
    shift_ffn,
):
    section = lax.axis_index("section")
    width = tokens.shape[2]
    ff = w_up.shape[2]
    share = bias_q.shape[1]
    n_dp = width // share
    vectors = (bias_q, bias_v, bias_out, gain_attn, shift_attn, bias_down, gain_ffn, shift_ffn)
    by_links = n_dp == 16 and share % 16 == 0
    low_up, low_down = w_up[0].astype(BF16), w_down[0].astype(BF16)
    columns = [v[0] for v in vectors] + list(bias_up[0].reshape(-1, share))
    table = jnp.stack(columns + [jnp.zeros((share,), F32)] * (LANES - len(columns)), axis=1)
    part_a = jnp.concatenate([w_qkv[0], w_out[0], table], axis=1).astype(BF16)
    if by_links:
        grid = Grid()
        place = jnp.stack([grid.core, grid.y])
        pieces = grid.gather(part_a, low_up, low_down)
        table = grid.ordered([piece[:, :, 4 * width :] for piece in pieces[0]]).astype(F32)
        w_a, full_up, full_down = (
            in_order(place, parts, name)
            for parts, name in zip(pieces, ("join_attn", "join_up", "join_down"))
        )
    else:
        place = jnp.zeros((2,), jnp.int32)
        w_a, full_up, full_down = (
            lax.all_gather(part, "dp", axis=0, tiled=True) for part in (part_a, low_up, low_down)
        )
        table = w_a[:, 4 * width :].astype(F32)
    rows = table[:, :8].T
    small = jnp.concatenate(
        [rows[:1], jnp.zeros((1, width), F32), rows[1:], jnp.zeros((7, width), F32)]
    )
    bias_columns = ff // width
    full_bias_up = table[:, 8 : 8 + bias_columns].reshape(n_dp, share, bias_columns)
    full_bias_up = full_bias_up.transpose(0, 2, 1).reshape(1, ff)

    def info(step, micro):
        picked = jnp.clip(micro, 0, 1)
        run = ((micro >= 0) & (micro <= 1)).astype(jnp.int32)
        head = jnp.stack([run, picked, section, lax.dynamic_index_in_dim(bucket, picked, 0, False)[0]])
        return jnp.concatenate([head, lax.dynamic_index_in_dim(lengths, picked, 0, False), place])

    steps = jnp.stack(
        [info(step, step - section) for step in range(3)]
        + [info(step, step - 1 + section) for step in range(3)]
    )
    none = jnp.zeros((ROWS, width), BF16)

    def ahead(step, received, held=None):
        attn_held, ffn_held = (None, None) if held is None else held
        attn = forward_attn(step, steps, tokens, received, w_a, small, attn_held)
        return attn, forward_ffn(
            step, steps, full_up, full_down, small, full_bias_up, attn[4], attn[6], ffn_held
        )

    def back_ffn(step, upstream, kept, held=None):
        return ffn_back(3 + step, steps, cotangent, upstream, full_up, full_down, small, *kept, held)

    outer = ahead(0, none)
    got = passed_along(outer[1][4], "section", 1)
    middle = ahead(1, got)
    got = passed_along(middle[1][4], "section", 1)
    back_outer = back_ffn(0, none, middle)
    back_attn_outer = attn_back(3, steps, w_a, back_outer[4], back_outer[2], middle[0])
    sent = passed_along(back_attn_outer[1], "section", -1)
    outer = ahead(2, got, outer)
    back_middle = back_ffn(1, sent, outer)
    back_attn_middle = attn_back(4, steps, w_a, back_middle[4], back_middle[2], outer[0])
    sent = passed_along(back_attn_middle[1], "section", -1)
    back_outer = back_ffn(2, sent, middle, back_outer)

    def last_attn_back(after=()):
        return attn_back(
            5, steps, w_a, back_outer[4], back_outer[2], middle[0], back_attn_outer, after
        )

    attn = tuple(zip(outer[0], middle[0]))
    ffn = tuple(zip(outer[1], middle[1]))
    d_ffn, d_pre, d_branch, sums_ffn, _ = zip(back_middle, back_outer)

    def by_micro(one, two):
        first = section == 0
        return jnp.stack([jnp.where(first, one, two), jnp.where(first, two, one)])[None]

    hidden_states = by_micro(*ffn[4])
    if by_links:
        mine, theirs = grad_by_rows(place, ffn[0], d_ffn, "grad_down")
        got_down = grid.swap_core(theirs)
        mine_up, theirs = grad_by_cols(place, attn[6], d_pre, "grad_up", after=(mine,))
        got_up = grid.swap_core(theirs)
        total_down = mine.astype(F32) + got_down.astype(F32)
        sent = grid.for_far(total_down)
        got_down = grid.send_far(sent)
        last = last_attn_back((mine_up,) + sent)
    else:
        last = last_attn_back()
    d_qkv, input_grads, sums_attn = zip(back_attn_middle, last)
    input_grads = by_micro(*input_grads)
    total = sums_ffn[0] + sums_ffn[1]
    total_attn = sums_attn[0] + sums_attn[1]
    vector = [
        total_attn[0],
        total_attn[1],
        total[2, width : 2 * width],
        total[1, 3 * width :],
        total[2, :width],
        total[1, :width],
        total[1, width : 2 * width],
        total[1, 2 * width : 3 * width],
    ]
    up_columns = total[0].reshape(n_dp, bias_columns, share).transpose(0, 2, 1)
    table = jnp.concatenate(
        [
            jnp.stack(vector, axis=1),
            up_columns.reshape(width, bias_columns),
            jnp.zeros((width, LANES - 8 - bias_columns), F32),
        ],
        axis=1,
    )
    if by_links:
        both_up = mine_up.astype(F32) + got_up.astype(F32)
        away_up = both_up[1].astype(BF16)
        sent = grid.for_near(total_down, got_down)
        got_down = grid.send_near(sent)
        got_up = grid.swap_y(away_up)
        mine_a, theirs = grad_attn(
            place, attn[0], d_qkv, attn[3], d_branch, table, after=sent + (away_up,)
        )
        got_a = grid.swap_core(theirs)
        both_a = mine_a.astype(F32) + got_a.astype(F32)
        got_a = grid.swap_y(both_a[1].astype(BF16))
        both_down = grid.line_end(total_down, got_down)
        got_down = grid.swap_y(both_down[1].astype(BF16))
        total_up = (both_up[0] + got_up.astype(F32))[None]
        got = grid.send_far(grid.for_far(total_up))
        got = grid.send_near(grid.for_near(total_up, got))
        g_up = grid.line_end(total_up, got)[0]
        g_down = both_down[0] + got_down.astype(F32)
        total_a = (both_a[0] + got_a.astype(F32))[None]
        got = grid.send_far(grid.for_far(total_a))
        got = grid.send_near(grid.for_near(total_a, got))
        g_a = grid.line_end(total_a, got)[0]
    else:

        def summed(values):
            return lax.psum_scatter(values, "dp", scatter_dimension=0, tiled=True).astype(F32)

        g_down = summed(weight_grad(ffn[0], d_ffn))
        g_up = summed(weight_grad(attn[6], d_pre))
        g_qkv = weight_grad(attn[0], d_qkv)
        g_out = weight_grad(attn[3], d_branch)
        g_a = summed(jnp.concatenate([g_qkv, g_out, table.astype(BF16)], axis=1))
    g_down, g_up = g_down[None], g_up[None]
    g_qkv, g_out = g_a[None, :, : 3 * width], g_a[None, :, 3 * width : 4 * width]
    g_vectors = [g_a[None, :, 4 * width + i] for i in range(8)]
    g_bias_up = g_a[:, 4 * width + 8 : 4 * width + 8 + bias_columns].T.reshape(1, ff // n_dp)
    (
        g_bias_q,
        g_bias_v,
        g_bias_out,
        g_gain_attn,
        g_shift_attn,
        g_bias_down,
        g_gain_ffn,
        g_shift_ffn,
    ) = g_vectors
    return (
        hidden_states,
        input_grads,
        g_qkv,
        g_bias_q,
        g_bias_v,
        g_out,
        g_bias_out,
        g_gain_attn,
        g_shift_attn,
        g_up,
        g_bias_up,
        g_down,
        g_bias_down,
        g_gain_ffn,
        g_shift_ffn,
    )


def solution(mesh):
    matrix = P("section", "dp", None)
    vector = P("section", "dp")
    rows = P(None, "dp", None)
    outs = P("section", None, "dp", None)
    params = (
        matrix,
        vector,
        vector,
        matrix,
        vector,
        vector,
        vector,
        matrix,
        vector,
        matrix,
        vector,
        vector,
        vector,
    )
    return jax.shard_map(
        on_device,
        mesh=mesh,
        in_specs=(rows, rows, P(None, "dp"), P(None, "dp")) + params,
        out_specs=(outs, outs) + params,
        check_vma=False,
    )
```

```python
import functools

import jax
import jax.numpy as jnp
from jax import lax
from jax.experimental import pallas as pl
from jax.experimental.pallas import tpu as pltpu
from jax.sharding import PartitionSpec as P

HEADS = 12
SEGMENT = 64
PAIRS = 6
ROWS = 384
EPSILON = 1e-06
MASKED = -1000000000.0
LANES = 128
FF_TILE = 1024
LIMIT = 4
LIMIT_GRAD = 6
VMEM_LIMIT = 60 * 1024 * 1024
F32 = jnp.float32
BF16 = jnp.bfloat16

BIAS_Q, BIAS_K, BIAS_V, BIAS_OUT, GAIN_ATTN, SHIFT_ATTN, BIAS_DOWN, GAIN_FFN, SHIFT_FFN = range(9)
RUN, MICRO, SECTION, BUCKET, LENGTHS = range(5)
CORE, Y = LENGTHS + PAIRS, LENGTHS + PAIRS + 1

ANY = pl.BlockSpec(memory_space=pl.ANY)
WHOLE = pl.BlockSpec(memory_space=pltpu.VMEM)
SCALARS = pl.BlockSpec(memory_space=pltpu.SMEM)
FAR = pl.BlockSpec(memory_space=pltpu.HBM)
COST = pl.CostEstimate(flops=1, bytes_accessed=1, transcendentals=0)


def in_hbm(arrays):
    return [pltpu.with_memory_space_constraint(array, pltpu.HBM) for array in arrays]


def dot_nn(a, b):
    return lax.dot_general(a, b, (((1,), (0,)), ((), ())), preferred_element_type=F32)


def dot_nt(a, b):
    return lax.dot_general(a, b, (((1,), (1,)), ((), ())), preferred_element_type=F32)


def dot_tn(a, b):
    return lax.dot_general(a, b, (((0,), (0,)), ((), ())), preferred_element_type=F32)


class Row:
    def __init__(self, table, row):
        self.table, self.row = table, row

    def __getitem__(self, at):
        return self.table[self.row, at]


def fold(values):
    rows, n = values.shape
    return jnp.sum(values.reshape(rows // 8, 8, n), axis=0)


def write_bias(info, bias, block, count):
    segment = (info[BUCKET] + 1) * SEGMENT
    per_block = jnp.where(info[BUCKET] == 0, block // SEGMENT, 1)
    k_row = lax.broadcasted_iota(jnp.int32, (block, block), 0)
    q_row = lax.broadcasted_iota(jnp.int32, (block, block), 1)

    def pair_of(row):
        return (row >= segment).astype(jnp.int32) + (row >= 2 * segment).astype(jnp.int32)

    k_pair = pair_of(k_row)
    same = k_pair == pair_of(q_row)
    position = k_row - k_pair * segment
    for at in range(count):
        valid = [
            jnp.minimum(info[LENGTHS + jnp.minimum(at * per_block + i, PAIRS - 1)], segment)
            for i in range(3)
        ]
        length = jnp.where(k_pair == 0, valid[0], jnp.where(k_pair == 1, valid[1], valid[2]))
        bias[at, :block, :block] = jnp.where(same & (position < length), 0.0, MASKED)


def half_masks():
    lane = lax.broadcasted_iota(jnp.int32, (1, LANES), 1)
    low = (lane < LANES // 2).astype(F32)
    return low.astype(BF16), (1.0 - low).astype(BF16)


def by_block(info, body):
    @pl.when(info[BUCKET] == 1)
    def _():
        body(2 * SEGMENT, ROWS // (2 * SEGMENT))

    @pl.when(info[BUCKET] != 1)
    def _():
        body(3 * SEGMENT, ROWS // (3 * SEGMENT))


def attention(info, qkv, context, lse, bias):
    width = context.shape[1]
    low, high = half_masks()

    def body(block, count):
        write_bias(info, bias, block, count)

        def pair_step(pair, carry):
            at_q = pl.multiple_of(pair * LANES, LANES)
            at_k = pl.multiple_of(width + pair * LANES, LANES)
            at_v = pl.multiple_of(2 * width + pair * LANES, LANES)
            is_low = lax.broadcasted_iota(jnp.int32, (block, LANES), 1) < LANES // 2
            units = [(at, half) for at in range(count) for half in range(2)]
            rows = [pl.ds(at * block, block) for at in range(count)]
            q = [qkv[r, pl.ds(at_q, LANES)] for r in rows]
            k = [qkv[r, pl.ds(at_k, LANES)] for r in rows]
            v = [qkv[r, pl.ds(at_v, LANES)] for r in rows]
            scores = [
                dot_nt(k[at] * (low, high)[half], q[at]) + bias[at, :block, :block]
                for at, half in units
            ]
            tops = [jnp.max(x, axis=0, keepdims=True) for x in scores]
            weights = [jnp.exp(x - top) for x, top in zip(scores, tops)]
            totals = [jnp.sum(x, axis=0, keepdims=True) for x in weights]
            probs = [(x * (1.0 / total)).astype(BF16) for x, total in zip(weights, totals)]
            parts = [dot_tn(x, v[at]) for x, (at, half) in zip(probs, units)]
            for index, (at, half) in enumerate(units):
                lse[2 * pair + half, at : at + 1, :block] = tops[index] + jnp.log(
                    totals[index]
                )
            for at in range(count):
                context[rows[at], pl.ds(at_q, LANES)] = jnp.where(
                    is_low, parts[2 * at], parts[2 * at + 1]
                ).astype(BF16)
            return carry

        lax.fori_loop(0, HEADS // 2, pair_step, 0)

    by_block(info, body)


def attention_back(info, qkv, d_context, lse, bias, d_qkv):
    width = d_context.shape[1]
    low, high = half_masks()
    scale = (width // HEADS) ** -0.5

    def body(block, count):
        write_bias(info, bias, block, count)

        def pair_step(pair, carry):
            at_q = pl.multiple_of(pair * LANES, LANES)
            at_k = pl.multiple_of(width + pair * LANES, LANES)
            at_v = pl.multiple_of(2 * width + pair * LANES, LANES)
            is_low = lax.broadcasted_iota(jnp.int32, (block, LANES), 1) < LANES // 2
            units = [(at, half) for at in range(count) for half in range(2)]
            rows = [pl.ds(at * block, block) for at in range(count)]
            q = [qkv[r, pl.ds(at_q, LANES)] for r in rows]
            k = [qkv[r, pl.ds(at_k, LANES)] for r in rows]
            v = [qkv[r, pl.ds(at_v, LANES)] for r in rows]
            d_out = [d_context[r, pl.ds(at_q, LANES)] for r in rows]
            scores = [
                dot_nt(k[at] * (low, high)[half], q[at]) + bias[at, :block, :block]
                for at, half in units
            ]
            d_probs = [dot_nt(v[at] * (low, high)[half], d_out[at]) for at, half in units]
            probs = [
                jnp.exp(x - lse[2 * pair + half, at : at + 1, :block])
                for x, (at, half) in zip(scores, units)
            ]
            d_v = [dot_nn(x.astype(BF16), d_out[at]) for x, (at, half) in zip(probs, units)]
            inner = [jnp.sum(x * d_x, axis=0, keepdims=True) for x, d_x in zip(probs, d_probs)]
            d_scores = [
                (x * (d_x - total)).astype(BF16)
                for x, d_x, total in zip(probs, d_probs, inner)
            ]
            d_k = [dot_nn(x, q[at]) for x, (at, half) in zip(d_scores, units)]
            d_q = [dot_tn(x, k[at]) for x, (at, half) in zip(d_scores, units)]
            for at in range(count):
                one, two = 2 * at, 2 * at + 1
                r = rows[at]
                d_qkv[r, pl.ds(at_q, LANES)] = (
                    jnp.where(is_low, d_q[one], d_q[two]) * scale
                ).astype(BF16)
                d_qkv[r, pl.ds(at_k, LANES)] = jnp.where(
                    is_low, d_k[one], d_k[two]
                ).astype(BF16)
                d_qkv[r, pl.ds(at_v, LANES)] = jnp.where(
                    is_low, d_v[one], d_v[two]
                ).astype(BF16)
            return carry

        lax.fori_loop(0, HEADS // 2, pair_step, 0)

    by_block(info, body)


def norm(values):
    centered = values - jnp.mean(values, axis=-1, keepdims=True)
    inverse = lax.rsqrt(jnp.mean(centered * centered, axis=-1, keepdims=True) + EPSILON)
    return centered * inverse, inverse


def norm_back(upstream, normed, inverse, gain):
    scaled = upstream * gain
    return inverse * (
        scaled
        - jnp.mean(scaled, axis=-1, keepdims=True)
        - normed * jnp.mean(scaled * normed, axis=-1, keepdims=True)
    )


CHUNK = 64


def by_rows(step, carry=0):
    def body(i, carry):
        return step(pl.ds(pl.multiple_of(i * CHUNK, CHUNK), CHUNK), carry)

    return lax.fori_loop(0, ROWS // CHUNK, body, carry)


def carry_over(src, dst):
    if src.shape[0] == ROWS:

        def step(rows, carry):
            dst[rows, :] = src[rows, :]
            return carry

        by_rows(step)
    else:
        dst[...] = src[...]


def kernel_call(body, name, step, ins, out_shapes, held, after, scratch, limit, far=()):
    held = [] if held is None else list(held)
    given = len(ins) - 1
    count = len(out_shapes)
    spec = [FAR if i in far else WHOLE for i in range(count)]

    def kernel(table, *refs):
        info = Row(table, step)
        kept = refs[given : given + len(held)]
        outs = refs[given + len(held) + len(after) :][:count]
        own = refs[given + len(held) + len(after) + count :]

        @pl.when(info[RUN] == 1)
        def _():
            copies = []

            def flush(index, ref):
                copy = pltpu.make_async_copy(ref, outs[index], own[-1].at[len(copies)])
                copy.start()
                copies.append(copy)

            near = [out for i, out in enumerate(outs) if i not in far]
            body(info, flush, *refs[:given], *near, *own[: len(scratch)])
            for copy in copies:
                copy.wait()

        if held:

            @pl.when(info[RUN] != 1)
            def _():
                for i, (src, dst) in enumerate(zip(kept, outs)):
                    if i not in far:
                        carry_over(src, dst)

    return pl.pallas_call(
        kernel,
        in_specs=[SCALARS] + [WHOLE] * given + spec[: len(held)] + [FAR] * len(after),
        out_specs=spec,
        out_shape=[
            pltpu.HBM(shape, kind) if i in far else jax.ShapeDtypeStruct(shape, kind)
            for i, (shape, kind) in enumerate(out_shapes)
        ],
        input_output_aliases={1 + given + i: i for i in range(len(held))},
        scratch_shapes=scratch + ([pltpu.SemaphoreType.DMA((len(far),))] if far else []),
        compiler_params=pltpu.CompilerParams(vmem_limit_bytes=int(limit * 1024 * 1024)),
        cost_estimate=COST,
        name=name,
    )(*ins, *(in_hbm([x])[0] if i in far else x for i, x in enumerate(held)), *in_hbm(after))


def forward_attn_body(
    info, flush, tok, rec, w_a, small, qkv, lse, n1, inv1, hid, n1_low, x, context, acc, bias
):
    width = x.shape[1]

    @pl.when(info[SECTION] == 0)
    def _():
        x[...] = tok[...]

    @pl.when(info[SECTION] != 0)
    def _():
        x[...] = rec[...]

    flush(6, x)
    for j, (row, factor) in enumerate(
        ((BIAS_Q, (width // HEADS) ** -0.5), (BIAS_K, 1.0), (BIAS_V, 1.0))
    ):
        cols = slice(j * width, (j + 1) * width)
        part = dot_nn(x[...], w_a[:, cols]) + small[row : row + 1, :]
        qkv[:, cols] = (part * factor).astype(BF16)
    attention(info, qkv, context, lse, bias)
    flush(7, context)
    acc[...] = dot_nn(context[...], w_a[:, 3 * width : 4 * width])

    def norm_one(rows, carry):
        total = x[rows, :].astype(F32) + acc[rows, :]
        normed, inverse = norm(total + small[BIAS_OUT : BIAS_OUT + 1, :])
        n1[rows, :] = normed
        n1_low[rows, :] = normed.astype(BF16)
        inv1[rows, :] = jnp.broadcast_to(inverse, (CHUNK, LANES))
        hidden = normed * small[GAIN_ATTN : GAIN_ATTN + 1, :]
        hid[rows, :] = (hidden + small[SHIFT_ATTN : SHIFT_ATTN + 1, :]).astype(BF16)
        return carry

    by_rows(norm_one)
    flush(8, hid)


def up_tile(j, hid, w_up, bias_up, act, d_act):
    cols = slice(j * FF_TILE, (j + 1) * FF_TILE)
    pre = dot_nn(hid[...], w_up[:, cols]) + bias_up[:, cols]
    below = 0.5 * (1.0 + lax.erf(pre * 0.7071067811865476))
    density = jnp.exp(pre * pre * -0.5) * 0.3989422804014327
    act[:, cols] = (pre * below).astype(BF16)
    d_act[:, cols] = (below + pre * density).astype(BF16)


def down_tile(j, act, w_down, acc):
    cols = slice(j * FF_TILE, (j + 1) * FF_TILE)
    part = dot_nn(act[:, cols], w_down[cols, :])
    acc[...] = part if j == 0 else acc[...] + part


def layer_end(small, n1, n2, inv2, out, acc):
    def norm_two(rows, carry):
        hidden = n1[rows, :] * small[GAIN_ATTN : GAIN_ATTN + 1, :]
        hidden = hidden + small[SHIFT_ATTN : SHIFT_ATTN + 1, :]
        normed, inverse = norm(hidden + acc[rows, :] + small[BIAS_DOWN : BIAS_DOWN + 1, :])
        n2[rows, :] = normed.astype(BF16)
        inv2[rows, :] = jnp.broadcast_to(inverse, (CHUNK, LANES))
        out[rows, :] = (
            normed * small[GAIN_FFN : GAIN_FFN + 1, :] + small[SHIFT_FFN : SHIFT_FFN + 1, :]
        ).astype(BF16)
        return carry

    by_rows(norm_two)


def forward_ffn_body(
    info, flush, w_up, w_down, small, bias_up, n1, hid, d_act, n2, inv2, out, act, acc
):
    tiles = act.shape[1] // FF_TILE
    up_tile(0, hid, w_up, bias_up, act, d_act)
    for j in range(1, tiles):
        up_tile(j, hid, w_up, bias_up, act, d_act)
        down_tile(j - 1, act, w_down, acc)
    flush(4, act)
    down_tile(tiles - 1, act, w_down, acc)
    layer_end(small, n1, n2, inv2, out, acc)


def forward_up_body(info, flush, w_up, bias_up, hid, d_act, act):
    for j in range(act.shape[1] // FF_TILE):
        up_tile(j, hid, w_up, bias_up, act, d_act)
    flush(2, act)


def forward_down_body(info, flush, w_down, small, n1, act, n2, inv2, out, acc):
    for j in range(act.shape[1] // FF_TILE):
        down_tile(j, act, w_down, acc)
    layer_end(small, n1, n2, inv2, out, acc)


def bias_scratch():
    return pltpu.VMEM((3, 3 * SEGMENT, 3 * SEGMENT), F32)


def forward_attn(step, info, tokens, received, w_a, small, held=None, after=()):
    width = small.shape[1]
    rows = ((ROWS, width), BF16)
    shapes = (
        ((ROWS, 3 * width), BF16),
        ((HEADS, 8, 256), F32),
        ((ROWS, width), F32),
        ((ROWS, LANES), F32),
        rows,
        rows,
        rows,
        rows,
        rows,
    )
    return kernel_call(
        forward_attn_body,
        "forward_attn",
        step,
        (info, tokens, received, w_a, small),
        shapes,
        held,
        after,
        [pltpu.VMEM(*rows)] * 2 + [pltpu.VMEM((ROWS, width), F32), bias_scratch()],
        LIMIT + 1.2,
        far=(6, 7, 8),
    )


def forward_ffn(step, info, w_up, w_down, small, bias_up, n1, hid, held=None):
    width, ff = small.shape[1], bias_up.shape[1]
    return kernel_call(
        forward_ffn_body,
        "forward_ffn",
        step,
        (info, w_up, w_down, small, bias_up, n1, hid),
        (
            ((ROWS, ff), BF16),
            ((ROWS, width), BF16),
            ((ROWS, LANES), F32),
            ((ROWS, width), BF16),
            ((ROWS, ff), BF16),
        ),
        held,
        (),
        [pltpu.VMEM((ROWS, ff), BF16), pltpu.VMEM((ROWS, width), F32)],
        LIMIT + 2.4,
        far=(4,),
    )


def forward_up(step, info, w_up, bias_up, hid, after=()):
    ff = w_up.shape[1]
    return kernel_call(
        forward_up_body,
        "forward_up",
        step,
        (info, w_up, bias_up, hid),
        [((ROWS, ff), BF16)] * 3,
        None,
        after,
        [],
        LIMIT,
        far=(2,),
    )


def forward_down(step, info, w_down, small, n1, act, after=()):
    width = w_down.shape[1]
    return kernel_call(
        forward_down_body,
        "forward_down",
        step,
        (info, w_down, small, n1, act),
        (((ROWS, width), BF16), ((ROWS, LANES), F32), ((ROWS, width), BF16)),
        None,
        after,
        [pltpu.VMEM((ROWS, width), F32)],
        LIMIT,
    )


def norm_back_rows(upstream, normed, inverse, gain, grad, low):
    zeros = jnp.zeros((8, grad.shape[1]), F32)

    def step(rows, carry):
        up, nm = upstream(rows), normed(rows)
        values = norm_back(up, nm, inverse(rows), gain)
        grad[rows, :] = values
        rounded = values.astype(BF16)
        low(rows, rounded)
        return (
            carry[0] + fold(up),
            carry[1] + fold(up * nm),
            carry[2] + fold(rounded.astype(F32)),
        )

    sums = by_rows(step, (zeros, zeros, zeros))
    return [jnp.sum(part, axis=0, keepdims=True) for part in sums]


def ffn_back_body(
    far,
    info,
    flush,
    cot,
    rec,
    w_up,
    w_down,
    small,
    n1,
    inv1,
    d_act,
    n2,
    inv2,
    d_branch,
    sums,
    d_first,
    d_ffn,
    d_pre,
    acc,
):
    if not far:

        def flush(index, ref):
            pass

    width = rec.shape[1]
    ff = d_pre.shape[1]
    tiles = ff // FF_TILE

    last = info[SECTION] == 1

    def upstream(rows):
        return jnp.where(last, cot[rows, :], rec[rows, :]).astype(F32)

    def keep_ffn(rows, low):
        d_ffn[rows, :] = low

    sum_g, sum_gn, sum_d = norm_back_rows(
        upstream,
        lambda rows: n2[rows, :].astype(F32),
        lambda rows: inv2[rows, :1],
        small[GAIN_FFN : GAIN_FFN + 1, :],
        acc,
        keep_ffn,
    )
    flush(3, d_ffn)
    sums[1:2, :width] = sum_d
    sums[1:2, width : 2 * width] = sum_gn
    sums[1:2, 2 * width : 3 * width] = sum_g

    def first(j):
        cols = slice(j * FF_TILE, (j + 1) * FF_TILE)
        part = dot_nt(d_ffn[...], w_down[cols, :]) * d_act[:, cols].astype(F32)
        low = part.astype(BF16)
        d_pre[:, cols] = low
        sums[0:1, cols] = jnp.sum(fold(low.astype(F32)), axis=0, keepdims=True)

    def second(j):
        cols = slice(j * FF_TILE, (j + 1) * FF_TILE)
        acc[...] += dot_nt(d_pre[:, cols], w_up[:, cols])

    first(0)
    for j in range(1, tiles):
        first(j)
        second(j - 1)
    flush(4, d_pre)
    second(tiles - 1)

    def keep_branch(rows, low):
        d_branch[rows, :] = low

    sum_g, sum_gn, sum_d = norm_back_rows(
        lambda rows: acc[rows, :],
        lambda rows: n1[rows, :].astype(F32),
        lambda rows: inv1[rows, :1],
        small[GAIN_ATTN : GAIN_ATTN + 1, :],
        d_first,
        keep_branch,
    )
    flush(5, d_branch)
    sums[1:2, 3 * width :] = sum_gn
    sums[2:3, :width] = sum_g
    sums[2:3, width : 2 * width] = sum_d


def ffn_back(step, info, cotangent, received, w_up, w_down, small, attn, ffn, held=None, far=False):
    width, ff = w_up.shape
    rows, wide = ((ROWS, width), BF16), ((ROWS, ff), BF16)
    shapes = (rows, ((8, ff), F32), ((ROWS, width), F32), rows, wide) + ((rows,) if far else ())
    scratch = [pltpu.VMEM(*rows), pltpu.VMEM(*wide)] if far else []
    return kernel_call(
        functools.partial(ffn_back_body, far),
        "ffn_backward",
        step,
        (info, cotangent, received, w_up, w_down, small, attn[5], attn[3], ffn[0], ffn[1], ffn[2]),
        shapes,
        held,
        (),
        scratch + [pltpu.VMEM((ROWS, width), F32)],
        LIMIT + (3 if far else 0),
        far=(3, 4, 5) if far else (),
    )


def attn_back_body(
    far, info, flush, w_a, d_first, d_branch, qkv, lse, grads, sums, d_qkv, d_context, bias
):
    if not far:

        def flush(index, ref):
            pass

    width = d_first.shape[1]

    d_context[...] = dot_nt(d_branch[...], w_a[:, 3 * width : 4 * width]).astype(BF16)
    attention_back(info, qkv, d_context, lse, bias, d_qkv)
    flush(2, d_qkv)
    grad = d_first[...] + dot_nt(d_qkv[...], w_a[:, : 3 * width])
    low = grad.astype(BF16)
    grads[...] = low
    for row, at in ((0, 0), (1, 2 * width)):
        sums[row : row + 1, :] = jnp.sum(
            fold(d_qkv[:, at : at + width].astype(F32)), axis=0, keepdims=True
        )


def attn_back(step, info, w_a, d_first, d_branch, attn, held=None, after=(), far=False):
    width = d_first.shape[1]
    rows, wide = ((ROWS, width), BF16), ((ROWS, 3 * width), BF16)
    return kernel_call(
        functools.partial(attn_back_body, far),
        "attention_backward",
        step,
        (info, w_a, d_first, d_branch, attn[0], attn[1]),
        (rows, ((8, width), F32), wide),
        held,
        after,
        ([pltpu.VMEM(*wide)] if far else []) + [pltpu.VMEM(*rows), bias_scratch()],
        LIMIT + (1.8 if far else 0),
        far=(2,) if far else (),
    )


def split_blocks(values, place, mine, theirs, cols, first_z=0):
    share = mine.shape[3]
    core, y, pair = place[0], place[1], place[2]
    for index in range(values.shape[0] // (4 * share)):
        z = first_z + index
        for yy in range(2):
            at = (index * 4 + yy * 2) * share
            first = values[at : at + share].astype(BF16)[None]
            second = values[at + share : at + 2 * share].astype(BF16)[None]
            to_y, to_pair = jnp.bitwise_xor(y, yy), jnp.bitwise_xor(pair, z // 2)

            @pl.when(core == 0)
            def _():
                mine[to_y, pl.ds(to_pair, 1), z % 2, :, cols] = first
                theirs[to_y, pl.ds(to_pair, 1), z % 2, :, cols] = second

            @pl.when(core == 1)
            def _():
                theirs[to_y, pl.ds(to_pair, 1), z % 2, :, cols] = first
                mine[to_y, pl.ds(to_pair, 1), z % 2, :, cols] = second


def grad_call(body, name, place, far, near, share, n, cuts):
    shape = (2, 2, 2, share, n)
    total = sum(cuts)

    def kernel(place, *refs):
        sources, refs = refs[: len(far)], refs[len(far) :]
        kept, refs = refs[: len(near)], refs[len(near) :]
        mine_out, theirs_out, mine, theirs, *held, sems = refs
        copies = []
        for src, dst, cut in zip(sources, held, cuts):
            size = src.shape[1] // cut
            group = []
            for i in range(cut):
                cols = slice(i * size, (i + 1) * size)
                sem = sems.at[sum(map(len, copies)) + i]
                group.append(pltpu.make_async_copy(src.at[:, cols], dst.at[:, cols], sem))
            copies.append(group)
        for i in range(max(cuts)):
            for group in copies:
                if i < len(group):
                    group[i].start()
        done = set()

        def wait(index, part=0):
            if (index, part) not in done:
                done.add((index, part))
                copies[index][part].wait()

        body(place, wait, held, kept, mine, theirs)
        copies = [
            pltpu.make_async_copy(src, dst, sems.at[total + i])
            for i, (src, dst) in enumerate(((theirs, theirs_out), (mine, mine_out)))
        ]
        for copy in copies:
            copy.start()
        for copy in copies:
            copy.wait()

    scratch = [pltpu.VMEM(shape, BF16)] * 2 + [pltpu.VMEM(x.shape, x.dtype) for x in far]
    size = sum(x.size * 2 for x in far) + 32 * share * n
    return pl.pallas_call(
        kernel,
        in_specs=[SCALARS] + [FAR] * len(far) + [WHOLE] * len(near),
        out_specs=[FAR] * 2,
        out_shape=[pltpu.HBM(shape, BF16)] * 2,
        scratch_shapes=scratch + [pltpu.SemaphoreType.DMA((total + 2,))],
        compiler_params=pltpu.CompilerParams(vmem_limit_bytes=size + LIMIT_GRAD * 1024 * 1024),
        cost_estimate=COST,
        name=name,
    )(place, *in_hbm(far), *near)


def stacked(one, two, cols=slice(None)):
    return jnp.concatenate([one[:, cols], two[:, cols]], axis=0)


def grad_down_body(place, wait, held, kept, mine, theirs):
    d_middle, act, act2 = held
    wait(0)
    right = stacked(d_middle, kept[0])
    rows = 4 * mine.shape[3]
    for z in range(4):
        wait(1, z)
        wait(2, z)
        left = stacked(act, act2, slice(z * rows, (z + 1) * rows))
        split_blocks(dot_tn(left, right), place, mine, theirs, slice(None), z)


def grad_up_body(place, wait, held, kept, mine, theirs):
    hid, hid2, d_middle = held
    wait(0)
    wait(1)
    left = stacked(hid, hid2)
    tile = d_middle.shape[1] // 4
    for i in range(4):
        wait(2, i)
        cols = slice(i * tile, (i + 1) * tile)
        split_blocks(dot_tn(left, stacked(d_middle, kept[0], cols)), place, mine, theirs, cols)


def grad_attn_body(place, wait, held, kept, mine, theirs):
    x, x2, d_middle, context, context2, d_branch = held
    width = x.shape[1]
    wait(0)
    wait(1)
    left = stacked(x, x2)
    for i in range(3):
        wait(2, i)
        cols = slice(i * width, (i + 1) * width)
        split_blocks(dot_tn(left, stacked(d_middle, kept[0], cols)), place, mine, theirs, cols)
    for i in range(3, 6):
        wait(i)
    values = dot_tn(stacked(context, context2), stacked(d_branch, kept[1]))
    split_blocks(values, place, mine, theirs, slice(3 * width, 4 * width))
    split_blocks(kept[2][...], place, mine, theirs, slice(4 * width, 4 * width + LANES))


def join_body(place, *refs):
    pieces, (out, sems) = refs[:-2], refs[-2:]
    core, y, pair, low = (place[i] for i in range(4))
    near = (pair * 2 + low, pair * 2 + 1 - low)
    far = (jnp.where(pair == 0, 2, 1), jnp.where(pair == 0, 3, 0))
    share = out.shape[0] // 16
    copies = []
    for index in range(8):
        dc, dy, away = index // 4, (index // 2) % 2, index % 2
        for i, z in enumerate(far if away else near):
            src = pieces[index].at[i]
            at = z * 4 + jnp.bitwise_xor(y, dy) * 2 + jnp.bitwise_xor(core, dc)
            rows = pl.ds(pl.multiple_of(at * share, 16), share)
            copy = pltpu.make_async_copy(src, out.at[rows, :], sems.at[len(copies)])
            copy.start()
            copies.append(copy)
    for copy in copies:
        copy.wait()


def in_order(place, pieces, name):
    share, n = pieces[0].shape[-2:]
    return pl.pallas_call(
        join_body,
        in_specs=[SCALARS] + [FAR] * len(pieces),
        out_specs=WHOLE,
        out_shape=jax.ShapeDtypeStruct((16 * share, n), BF16),
        scratch_shapes=[pltpu.SemaphoreType.DMA((16,))],
        compiler_params=pltpu.CompilerParams(vmem_limit_bytes=4 * 1024 * 1024),
        cost_estimate=COST,
        name=name,
    )(place, *in_hbm(pieces))


def weight_grad(a, b):
    return sum(dot_tn(one, two) for one, two in zip(a, b)).astype(BF16)


def tie(value, *others):
    return lax.optimization_barrier((value, others))[0]


def after(before, *values):
    return lax.optimization_barrier((values, tuple(before)))[0]


class Grid:
    def __init__(self):
        index = lax.axis_index("dp")
        self.core = index % 2
        self.y = (index // 2) % 2
        self.low = (index // 4) % 2
        self.pair = index // 8
        self.is_middle = self.low != self.pair

    def move(self, block, route):
        return lax.ppermute(block, "dp", route)

    def swap_core(self, block):
        return self.move(block, [(i, i ^ 1) for i in range(16)])

    def swap_y(self, block):
        return self.move(block, [(i, i ^ 2) for i in range(16)])

    def swap_near(self, block):
        return self.move(block, [(i, i ^ 4) for i in range(16)])

    def swap_middle(self, block):
        return self.move(block, [(i, i ^ 12) for i in range(4, 12)])

    def send_out(self, block):
        return self.move(block, [(i, i ^ 4) for i in range(4, 12)])

    def send_in(self, block):
        return self.move(block, [(i, i ^ 4) for i in range(16) if not 4 <= i < 12])

    def low_first(self, first, second):
        return jnp.where(self.low == 0, first, second)

    def picked(self, blocks, at, axis):
        return lax.dynamic_index_in_dim(blocks, at, axis, keepdims=False)

    def ordered(self, pieces):
        near, far = (self.pair * 2 + self.low, self.pair * 2 + 1 - self.low), (
            jnp.where(self.pair == 0, 2, 1),
            jnp.where(self.pair == 0, 3, 0),
        )
        places = []
        for index in range(8):
            dc, dy, away = index // 4, (index // 2) % 2, index % 2
            for z in far if away else near:
                places.append(z * 4 + (self.y ^ dy) * 2 + (self.core ^ dc))
        return jnp.zeros_like(jnp.concatenate(pieces)).at[jnp.stack(places)].set(
            jnp.concatenate(pieces)
        )


def passed_along(block, axis, distance):
    devices = range(lax.axis_size(axis))
    route = [(i - distance, i) for i in devices if i - distance in devices]
    return lax.ppermute(block, axis, route)


def on_device(
    tokens,
    cotangent,
    bucket,
    lengths,
    w_qkv,
    bias_q,
    bias_v,
    w_out,
    bias_out,
    gain_attn,
    shift_attn,
    w_up,
    bias_up,
    w_down,
    bias_down,
    gain_ffn,
    shift_ffn,
):
    section = lax.axis_index("section")
    width = tokens.shape[2]
    ff = w_up.shape[2]
    share = bias_q.shape[1]
    n_dp = width // share
    vectors = (bias_q, bias_v, bias_out, gain_attn, shift_attn, bias_down, gain_ffn, shift_ffn)
    by_links = n_dp == 16 and share % 16 == 0
    shares = ff // width
    count = len(vectors) + shares
    row_table = jnp.concatenate(vectors + (bias_up.reshape(shares, share),))
    row_table = lax.optimization_barrier(row_table).astype(BF16)
    part_a = jnp.concatenate([w_qkv[0], w_out[0]], axis=1).astype(BF16)
    part_up, part_down = w_up[0].astype(BF16), w_down[0].astype(BF16)
    if by_links:
        grid = Grid()
        place = jnp.stack([grid.core, grid.y, grid.pair, grid.low])
        padded = jnp.pad(row_table, ((0, share - count), (0, LANES - share)))
        part_a = jnp.concatenate([part_a, padded], axis=1)
        got_a, got_up = grid.swap_near(part_a), grid.swap_near(part_up)
        down_other = grid.swap_y(part_down)
        ended = (got_a, got_up, down_other)
        near_a, near_up = jnp.stack([part_a, got_a]), jnp.stack([part_up, got_up])

        near_a, both_down = after(ended, near_a, jnp.stack([part_down, down_other]))
        middle_a, got_down = grid.swap_middle(near_a), grid.swap_near(both_down)
        near_a_y = grid.swap_y(near_a)
        ended = (middle_a, got_down, near_a_y)
        near_down = jnp.stack([part_down, got_down[0]])
        near_down_y = jnp.stack([down_other, got_down[1]])

        middle_a, near_up = after(ended, middle_a, near_up)
        out_a, middle_up = grid.send_out(middle_a), grid.swap_middle(near_up)
        near_up_y = grid.swap_y(near_up)
        ended = (out_a, middle_up, near_up_y)
        far_a = jnp.where(grid.is_middle, middle_a, out_a)

        middle_up, near_down, far_a = after(ended, middle_up, near_down, far_a)
        out_up, middle_down = grid.send_out(middle_up), grid.swap_middle(near_down)
        far_a_y = grid.swap_y(far_a)
        ended = (out_up, middle_down, far_a_y)
        far_up = jnp.where(grid.is_middle, middle_up, out_up)

        middle_down, near_down_y, far_up, near_a, far_a, near_a_y, far_a_y = after(
            ended, middle_down, near_down_y, far_up, near_a, far_a, near_a_y, far_a_y
        )
        out_down, middle_down_y = grid.send_out(middle_down), grid.swap_middle(near_down_y)
        far_up_y = grid.swap_y(far_up)
        ended = (out_down, middle_down_y, far_up_y)
        far_down = jnp.where(grid.is_middle, middle_down, out_down)

        def with_siblings(pieces):
            return pieces + tuple(grid.swap_core(piece) for piece in pieces)

        pieces_a = with_siblings((near_a, far_a, near_a_y, far_a_y))
        table = grid.ordered([piece[:, :, 4 * width :] for piece in pieces_a])
        table = table[:, :count, :share]
        w_a = in_order(place, pieces_a, "join_attn")
    else:
        place = jnp.zeros((4,), jnp.int32)
        w_a, full_up, full_down = (
            lax.all_gather(part, "dp", axis=0, tiled=True) for part in (part_a, part_up, part_down)
        )
        table = lax.all_gather(row_table[None], "dp", axis=0, tiled=True)
    table = table.astype(F32).transpose(1, 0, 2)
    rows = table[:8].reshape(8, width)
    small = jnp.concatenate(
        [rows[:1], jnp.zeros((1, width), F32), rows[1:], jnp.zeros((7, width), F32)]
    )
    full_bias_up = table[8:].transpose(1, 0, 2).reshape(1, ff)

    def info(step, micro):
        picked = jnp.clip(micro, 0, 1)
        run = ((micro >= 0) & (micro <= 1)).astype(jnp.int32)
        head = jnp.stack([run, picked, section, lax.dynamic_index_in_dim(bucket, picked, 0, False)[0]])
        return jnp.concatenate([head, lax.dynamic_index_in_dim(lengths, picked, 0, False), place])

    steps = jnp.stack(
        [info(step, step - section) for step in range(3)]
        + [info(step, step - 1 + section) for step in range(3)]
    )
    none = jnp.zeros((ROWS, width), BF16)

    def ahead(step, received, held=None):
        attn_held, ffn_held = (None, None) if held is None else held
        own = tokens[min(step, 1)]
        attn = forward_attn(step, steps, own, received, w_a, small, attn_held)
        return attn, forward_ffn(
            step, steps, full_up, full_down, small, full_bias_up, attn[2], attn[4], ffn_held
        )

    def back_ffn(step, upstream, kept, held=None, far=False):
        return ffn_back(
            3 + step, steps, cotangent[min(step, 1)], upstream, full_up, full_down, small, *kept, held, far
        )

    if by_links:
        attn = forward_attn(0, steps, tokens[0], none, w_a, small)
        middle_down_y, near_up, far_up, near_up_y, far_up_y = after(
            ended + (attn[1],), middle_down_y, near_up, far_up, near_up_y, far_up_y
        )
        out_down_y = grid.send_out(middle_down_y)
        pieces_up = with_siblings((near_up, far_up, near_up_y, far_up_y))
        full_up = in_order(place, pieces_up, "join_up")
        up = forward_up(0, steps, full_up, full_bias_up, attn[4])
        siblings = tuple(grid.swap_core(x) for x in (near_down, far_down, near_down_y))
        far_down_y = jnp.where(grid.is_middle, middle_down_y, tie(out_down_y, up[0]))
        pieces_down = (near_down, far_down, near_down_y, far_down_y) + siblings
        pieces_down += (grid.swap_core(far_down_y),)
        full_down = in_order(place, pieces_down, "join_down")
        end = forward_down(0, steps, full_down, small, attn[2], up[1])
        outer = (attn, (up[0], *end, up[2]))
    else:
        outer = ahead(0, none)
    got = passed_along(outer[1][3], "section", 1)
    middle = ahead(1, got)
    got = passed_along(middle[1][3], "section", 1)
    back_outer = back_ffn(0, none, middle)
    back_attn_outer = attn_back(3, steps, w_a, back_outer[2], back_outer[0], middle[0])
    sent = passed_along(back_attn_outer[0], "section", -1)
    outer = ahead(2, got, outer)
    back_middle = back_ffn(1, sent, outer, far=by_links)
    back_attn_middle = attn_back(
        4, steps, w_a, back_middle[2], back_middle[0], outer[0], far=by_links
    )
    sent = passed_along(back_attn_middle[0], "section", -1)
    back_outer = back_ffn(2, sent, middle, back_outer)

    def last_attn_back(steps):
        return attn_back(5, steps, w_a, back_outer[2], back_outer[0], middle_attn, back_attn_outer)

    middle_attn = middle[0]
    x, context, hid = zip(outer[0][6:], middle[0][6:])
    act, outputs = (outer[1][4], middle[1][4]), (outer[1][3], middle[1][3])
    sums_ffn = back_middle[1], back_outer[1]
    d_ffn, d_pre = zip(back_middle[3:5], back_outer[3:5])
    d_branch = back_middle[-1 if by_links else 0], back_outer[0]

    def by_micro(one, two):
        first = section == 0
        return jnp.stack([jnp.where(first, one, two), jnp.where(first, two, one)])[None]

    hidden_states = by_micro(*outputs)
    if by_links:
        def plus(one, two):
            return one.astype(F32) + two.astype(F32)

        mine_down, theirs = grad_call(
            grad_down_body,
            "grad_down",
            place,
            (d_ffn[0], *act),
            (d_ffn[1],),
            ff // 16,
            width,
            (1, 4, 4),
        )
        got_down = grid.swap_core(theirs)
        mine_up, theirs = grad_call(
            grad_up_body,
            "grad_up",
            place,
            (tie(hid[0], mine_down), hid[1], d_pre[0]),
            (d_pre[1],),
            share,
            ff,
            (1, 1, 4),
        )
        far_down = [plus(mine_down[i, 1], got_down[i, 1]) for i in range(2)]

        out, theirs, table = after((got_down, mine_up), far_down[0].astype(BF16), theirs, steps)
        got_out_down, got_up = grid.send_in(out), grid.swap_core(theirs)
        last = last_attn_back(table)
        ended = (got_out_down, got_up, last[1])
        middle = (far_down[0] + got_out_down.astype(F32)).astype(BF16)

        away, middle, out, first_x = after(
            ended,
            plus(mine_up[1, 1], got_up[1, 1]).astype(BF16),
            middle,
            far_down[1].astype(BF16),
            x[0],
        )
        far_up_y, got_middle_down = grid.swap_y(away), grid.swap_middle(middle)
        got_out_down_y = grid.send_in(out)
        ended = (far_up_y, got_middle_down, got_out_down_y)
    else:
        last = last_attn_back(steps)
    input_grads, sums_attn, d_qkv = zip(back_attn_middle, last)
    input_grads = by_micro(*input_grads)
    total = sums_ffn[0] + sums_ffn[1]
    total_attn = sums_attn[0] + sums_attn[1]
    vector_rows = jnp.stack(
        [
            total_attn[0],
            total_attn[1],
            total[2, width : 2 * width],
            total[1, 3 * width :],
            total[2, :width],
            total[1, :width],
            total[1, width : 2 * width],
            total[1, 2 * width : 3 * width],
        ]
    ).reshape(8, n_dp, share)
    table = jnp.concatenate(
        [vector_rows.transpose(1, 0, 2), total[0].reshape(n_dp, shares, share)], axis=1
    )
    if by_links:
        padded = jnp.pad(table, ((0, 0), (0, share - count), (0, LANES - share)))
        mine_a, theirs = grad_call(
            grad_attn_body,
            "grad_attn",
            place,
            (first_x, x[1], d_qkv[0], *context, d_branch[0]),
            (d_qkv[1], d_branch[1], padded.reshape(width, LANES)),
            share,
            4 * width + LANES,
            (1, 1, 3, 1, 1, 1),
        )
        far_up = plus(mine_up[0, 1], got_up[0, 1]) + far_up_y.astype(F32)
        middle = (far_down[1] + got_out_down_y.astype(F32)).astype(BF16)

        theirs, out, middle, away = after(
            ended + (mine_a,),
            theirs,
            far_up.astype(BF16),
            middle,
            plus(mine_up[1, 0], got_up[1, 0]).astype(BF16),
        )
        got_a, got_out_up = grid.swap_core(theirs), grid.send_in(out)
        got_middle_down_y, near_up_y = grid.swap_middle(middle), grid.swap_y(away)
        ended = (got_a, got_out_up, got_middle_down_y, near_up_y)
        middle = (far_up + got_out_up.astype(F32)).astype(BF16)
        near_down = plus(mine_down[:, 0], got_down[:, 0]) + jnp.stack(
            [got_middle_down, got_middle_down_y]
        ).astype(F32)

        away, middle, near = after(
            ended,
            plus(mine_a[1, 1], got_a[1, 1]).astype(BF16),
            middle,
            grid.picked(near_down, 1 - grid.low, 1).astype(BF16),
        )
        far_a_y, got_middle_up = grid.swap_y(away), grid.swap_middle(middle)
        got_near_down = grid.swap_near(near)
        ended = (far_a_y, got_middle_up, got_near_down)
        far_a = plus(mine_a[0, 1], got_a[0, 1]) + far_a_y.astype(F32)

        out, away = after(
            ended, far_a.astype(BF16), plus(mine_a[1, 0], got_a[1, 0]).astype(BF16)
        )
        got_out_a, near_a_y = grid.send_in(out), grid.swap_y(away)
        ended = (got_out_a, near_a_y)
        middle = (far_a + got_out_a.astype(F32)).astype(BF16)
        near_up = plus(mine_up[0, 0], got_up[0, 0]) + plus(near_up_y, got_middle_up)
        both_down = grid.picked(near_down, grid.low, 1) + got_near_down.astype(F32)

        middle, near, away = after(
            ended,
            middle,
            grid.picked(near_up, 1 - grid.low, 0).astype(BF16),
            both_down[1].astype(BF16),
        )
        got_middle_a, got_near_up = grid.swap_middle(middle), grid.swap_near(near)
        got_down_y = grid.swap_y(away)
        ended = (got_middle_a, got_near_up, got_down_y)
        near_a = plus(mine_a[0, 0], got_a[0, 0]) + plus(near_a_y, got_middle_a)
        (near,) = after(ended, grid.picked(near_a, 1 - grid.low, 0).astype(BF16))
        got_near_a = grid.swap_near(near)
        g_down = both_down[0] + got_down_y.astype(F32)
        g_up = grid.picked(near_up, grid.low, 0) + got_near_up.astype(F32)
        g_a = grid.picked(near_a, grid.low, 0) + got_near_a.astype(F32)
        table = g_a[:count, 4 * width : 4 * width + share]
    else:

        def summed(values):
            return lax.psum_scatter(values, "dp", scatter_dimension=0, tiled=True).astype(F32)

        g_down = summed(weight_grad(act, d_ffn))
        g_up = summed(weight_grad(hid, d_pre))
        g_qkv = weight_grad(x, d_qkv)
        g_out = weight_grad(context, d_branch)
        g_a = summed(jnp.concatenate([g_qkv, g_out], axis=1))
        table = summed(table)[0]
    g_down, g_up = g_down[None], g_up[None]
    g_qkv, g_out = g_a[None, :, : 3 * width], g_a[None, :, 3 * width : 4 * width]
    g_vectors = [table[i : i + 1] for i in range(8)]
    g_bias_up = table[8:].reshape(1, ff // n_dp)
    (
        g_bias_q,
        g_bias_v,
        g_bias_out,
        g_gain_attn,
        g_shift_attn,
        g_bias_down,
        g_gain_ffn,
        g_shift_ffn,
    ) = g_vectors
    return (
        hidden_states,
        input_grads,
        g_qkv,
        g_bias_q,
        g_bias_v,
        g_out,
        g_bias_out,
        g_gain_attn,
        g_shift_attn,
        g_up,
        g_bias_up,
        g_down,
        g_bias_down,
        g_gain_ffn,
        g_shift_ffn,
    )


def solution(mesh):
    matrix = P("section", "dp", None)
    vector = P("section", "dp")
    rows = P(None, "dp", None)
    outs = P("section", None, "dp", None)
    params = (
        matrix,
        vector,
        vector,
        matrix,
        vector,
        vector,
        vector,
        matrix,
        vector,
        matrix,
        vector,
        vector,
        vector,
    )
    return jax.shard_map(
        on_device,
        mesh=mesh,
        in_specs=(rows, rows, P(None, "dp"), P(None, "dp")) + params,
        out_specs=(outs, outs) + params,
        check_vma=False,
    )
```

```python
import functools

import jax
import jax.numpy as jnp
from jax import lax
from jax.experimental import pallas as pl
from jax.experimental.pallas import tpu as pltpu
from jax.sharding import PartitionSpec as P

HEADS = 12
SEGMENT = 64
PAIRS = 6
ROWS = 384
EPSILON = 1e-06
MASKED = -1000000000.0
LANES = 128
FF_TILE = 1024
LIMIT = 4
LIMIT_GRAD = 6
VMEM_LIMIT = 60 * 1024 * 1024
F32 = jnp.float32
BF16 = jnp.bfloat16

BIAS_Q, BIAS_K, BIAS_V, BIAS_OUT, GAIN_ATTN, SHIFT_ATTN, BIAS_DOWN, GAIN_FFN, SHIFT_FFN = range(9)
RUN, MICRO, SECTION, BUCKET, LENGTHS = range(5)
CORE, Y, PAIR, LOW = range(LENGTHS + PAIRS, LENGTHS + PAIRS + 4)

ANY = pl.BlockSpec(memory_space=pl.ANY)
WHOLE = pl.BlockSpec(memory_space=pltpu.VMEM)
SCALARS = pl.BlockSpec(memory_space=pltpu.SMEM)
FAR = pl.BlockSpec(memory_space=pltpu.HBM)
COST = pl.CostEstimate(flops=1, bytes_accessed=1, transcendentals=0)


def in_hbm(arrays):
    return [pltpu.with_memory_space_constraint(array, pltpu.HBM) for array in arrays]


def dot_nn(a, b):
    return lax.dot_general(a, b, (((1,), (0,)), ((), ())), preferred_element_type=F32)


def dot_nt(a, b):
    return lax.dot_general(a, b, (((1,), (1,)), ((), ())), preferred_element_type=F32)


def dot_tn(a, b):
    return lax.dot_general(a, b, (((0,), (0,)), ((), ())), preferred_element_type=F32)


class Row:
    def __init__(self, table, row):
        self.table, self.row = table, row

    def __getitem__(self, at):
        return self.table[self.row, at]


def fold(values):
    rows, n = values.shape
    return jnp.sum(values.reshape(rows // 8, 8, n), axis=0)


def write_bias(info, bias, block, count):
    segment = (info[BUCKET] + 1) * SEGMENT
    per_block = jnp.where(info[BUCKET] == 0, block // SEGMENT, 1)
    k_row = lax.broadcasted_iota(jnp.int32, (block, block), 0)
    q_row = lax.broadcasted_iota(jnp.int32, (block, block), 1)

    def pair_of(row):
        return (row >= segment).astype(jnp.int32) + (row >= 2 * segment).astype(jnp.int32)

    k_pair = pair_of(k_row)
    same = k_pair == pair_of(q_row)
    position = k_row - k_pair * segment
    for at in range(count):
        valid = [
            jnp.minimum(info[LENGTHS + jnp.minimum(at * per_block + i, PAIRS - 1)], segment)
            for i in range(3)
        ]
        length = jnp.where(k_pair == 0, valid[0], jnp.where(k_pair == 1, valid[1], valid[2]))
        bias[at, :block, :block] = jnp.where(same & (position < length), 0.0, MASKED)


def half_masks():
    lane = lax.broadcasted_iota(jnp.int32, (1, LANES), 1)
    low = (lane < LANES // 2).astype(F32)
    return low.astype(BF16), (1.0 - low).astype(BF16)


def by_block(info, body):
    @pl.when(info[BUCKET] == 1)
    def _():
        body(2 * SEGMENT, ROWS // (2 * SEGMENT))

    @pl.when(info[BUCKET] != 1)
    def _():
        body(3 * SEGMENT, ROWS // (3 * SEGMENT))


def attention(info, qkv, context, lse, bias):
    width = context.shape[1]
    low, high = half_masks()

    def body(block, count):
        write_bias(info, bias, block, count)

        def pair_step(pair, carry):
            at_q = pl.multiple_of(pair * LANES, LANES)
            at_k = pl.multiple_of(width + pair * LANES, LANES)
            at_v = pl.multiple_of(2 * width + pair * LANES, LANES)
            is_low = lax.broadcasted_iota(jnp.int32, (block, LANES), 1) < LANES // 2
            units = [(at, half) for at in range(count) for half in range(2)]
            rows = [pl.ds(at * block, block) for at in range(count)]
            q = [qkv[r, pl.ds(at_q, LANES)] for r in rows]
            k = [qkv[r, pl.ds(at_k, LANES)] for r in rows]
            v = [qkv[r, pl.ds(at_v, LANES)] for r in rows]
            scores = [
                dot_nt(k[at] * (low, high)[half], q[at]) + bias[at, :block, :block]
                for at, half in units
            ]
            tops = [jnp.max(x, axis=0, keepdims=True) for x in scores]
            weights = [jnp.exp(x - top) for x, top in zip(scores, tops)]
            totals = [jnp.sum(x, axis=0, keepdims=True) for x in weights]
            probs = [(x * (1.0 / total)).astype(BF16) for x, total in zip(weights, totals)]
            parts = [dot_tn(x, v[at]) for x, (at, half) in zip(probs, units)]
            for index, (at, half) in enumerate(units):
                lse[2 * pair + half, at : at + 1, :block] = tops[index] + jnp.log(
                    totals[index]
                )
            for at in range(count):
                context[rows[at], pl.ds(at_q, LANES)] = jnp.where(
                    is_low, parts[2 * at], parts[2 * at + 1]
                ).astype(BF16)
            return carry

        lax.fori_loop(0, HEADS // 2, pair_step, 0)

    by_block(info, body)


def attention_back(info, qkv, d_context, lse, bias, d_qkv):
    width = d_context.shape[1]
    low, high = half_masks()
    scale = (width // HEADS) ** -0.5

    def body(block, count):
        write_bias(info, bias, block, count)

        def pair_step(pair, carry):
            at_q = pl.multiple_of(pair * LANES, LANES)
            at_k = pl.multiple_of(width + pair * LANES, LANES)
            at_v = pl.multiple_of(2 * width + pair * LANES, LANES)
            is_low = lax.broadcasted_iota(jnp.int32, (block, LANES), 1) < LANES // 2
            units = [(at, half) for at in range(count) for half in range(2)]
            rows = [pl.ds(at * block, block) for at in range(count)]
            q = [qkv[r, pl.ds(at_q, LANES)] for r in rows]
            k = [qkv[r, pl.ds(at_k, LANES)] for r in rows]
            v = [qkv[r, pl.ds(at_v, LANES)] for r in rows]
            d_out = [d_context[r, pl.ds(at_q, LANES)] for r in rows]
            scores = [
                dot_nt(k[at] * (low, high)[half], q[at]) + bias[at, :block, :block]
                for at, half in units
            ]
            d_probs = [dot_nt(v[at] * (low, high)[half], d_out[at]) for at, half in units]
            probs = [
                jnp.exp(x - lse[2 * pair + half, at : at + 1, :block])
                for x, (at, half) in zip(scores, units)
            ]
            d_v = [dot_nn(x.astype(BF16), d_out[at]) for x, (at, half) in zip(probs, units)]
            inner = [jnp.sum(x * d_x, axis=0, keepdims=True) for x, d_x in zip(probs, d_probs)]
            d_scores = [
                (x * (d_x - total)).astype(BF16)
                for x, d_x, total in zip(probs, d_probs, inner)
            ]
            d_k = [dot_nn(x, q[at]) for x, (at, half) in zip(d_scores, units)]
            d_q = [dot_tn(x, k[at]) for x, (at, half) in zip(d_scores, units)]
            for at in range(count):
                one, two = 2 * at, 2 * at + 1
                r = rows[at]
                d_qkv[r, pl.ds(at_q, LANES)] = (
                    jnp.where(is_low, d_q[one], d_q[two]) * scale
                ).astype(BF16)
                d_qkv[r, pl.ds(at_k, LANES)] = jnp.where(
                    is_low, d_k[one], d_k[two]
                ).astype(BF16)
                d_qkv[r, pl.ds(at_v, LANES)] = jnp.where(
                    is_low, d_v[one], d_v[two]
                ).astype(BF16)
            return carry

        lax.fori_loop(0, HEADS // 2, pair_step, 0)

    by_block(info, body)


def norm(values):
    centered = values - jnp.mean(values, axis=-1, keepdims=True)
    inverse = lax.rsqrt(jnp.mean(centered * centered, axis=-1, keepdims=True) + EPSILON)
    return centered * inverse, inverse


def norm_back(upstream, normed, inverse, gain):
    scaled = upstream * gain
    return inverse * (
        scaled
        - jnp.mean(scaled, axis=-1, keepdims=True)
        - normed * jnp.mean(scaled * normed, axis=-1, keepdims=True)
    )


CHUNK = 64


def by_rows(step, carry=0):
    def body(i, carry):
        return step(pl.ds(pl.multiple_of(i * CHUNK, CHUNK), CHUNK), carry)

    return lax.fori_loop(0, ROWS // CHUNK, body, carry)


def carry_over(src, dst):
    if src.shape[0] == ROWS:

        def step(rows, carry):
            dst[rows, :] = src[rows, :]
            return carry

        by_rows(step)
    else:
        dst[...] = src[...]


def join_copies(info, pieces, out, sems):
    core, y, pair, low = (info[i] for i in (CORE, Y, PAIR, LOW))
    near = (pair * 2 + low, pair * 2 + 1 - low)
    far = (jnp.where(pair == 0, 2, 1), jnp.where(pair == 0, 3, 0))
    share = pieces[0].shape[1]
    copies = []
    for index, piece in enumerate(pieces):
        dc, dy, away = index // 4, (index // 2) % 2, index % 2
        for i, z in enumerate(far if away else near):
            at = z * 4 + jnp.bitwise_xor(y, dy) * 2 + jnp.bitwise_xor(core, dc)
            rows = pl.ds(pl.multiple_of(at * share, 16), share)
            copies.append(pltpu.make_async_copy(piece.at[i], out.at[rows, :], sems.at[len(copies)]))
    return copies


def kernel_call(body, name, step, ins, out_shapes, held, scratch, limit, far=(), pieces=(), far_ins=()):
    held = [] if held is None else list(held)
    given = len(ins) - 1
    count = len(out_shapes)
    spec = [FAR if i in far else WHOLE for i in range(count)]

    def kernel(table, *refs):
        info = Row(table, step)
        blocks, refs = refs[: len(pieces)], refs[len(pieces) :]
        kept = refs[given : given + len(held)]
        outs = refs[given + len(held) :][:count]
        own = refs[given + len(held) + count :]
        if pieces:
            joins = join_copies(info, blocks, outs[-1], own[len(scratch)])
            for copy in joins:
                copy.start()
            for copy in joins:
                copy.wait()

        @pl.when(info[RUN] == 1)
        def _():
            copies = []

            def flush(index, ref):
                copy = pltpu.make_async_copy(ref, outs[index], own[-1].at[len(copies)])
                copy.start()
                copies.append(copy)

            near = [out for i, out in enumerate(outs) if i not in far]
            body(info, flush, *refs[:given], *near, *own[: len(scratch)])
            for copy in copies:
                copy.wait()

        if held:

            @pl.when(info[RUN] != 1)
            def _():
                for i, (src, dst) in enumerate(zip(kept, outs)):
                    if i not in far:
                        carry_over(src, dst)

    return pl.pallas_call(
        kernel,
        in_specs=[SCALARS]
        + [FAR] * len(pieces)
        + [FAR if i in far_ins else WHOLE for i in range(given)]
        + spec[: len(held)],
        out_specs=spec,
        out_shape=[
            pltpu.HBM(shape, kind) if i in far else jax.ShapeDtypeStruct(shape, kind)
            for i, (shape, kind) in enumerate(out_shapes)
        ],
        input_output_aliases={1 + given + i: i for i in range(len(held))},
        scratch_shapes=scratch
        + ([pltpu.SemaphoreType.DMA((16,))] if pieces else [])
        + ([pltpu.SemaphoreType.DMA((len(far),))] if far else []),
        compiler_params=pltpu.CompilerParams(vmem_limit_bytes=int(limit * 1024 * 1024)),
        cost_estimate=COST,
        name=name,
    )(
        ins[0],
        *in_hbm(pieces),
        *(in_hbm([x])[0] if i in far_ins else x for i, x in enumerate(ins[1:])),
        *(in_hbm([x])[0] if i in far else x for i, x in enumerate(held)),
    )


def forward_attn_body(
    info, flush, tok, rec, w_a, small, qkv, lse, n1, inv1, hid, n1_low, x, context, acc, bias, sem
):
    width = x.shape[1]

    @pl.when(info[SECTION] == 0)
    def _():
        copy = pltpu.make_async_copy(tok.at[info[MICRO]], x, sem)
        copy.start()
        copy.wait()

    @pl.when(info[SECTION] != 0)
    def _():
        x[...] = rec[...]

    flush(6, x)
    for j, (row, factor) in enumerate(
        ((BIAS_Q, (width // HEADS) ** -0.5), (BIAS_K, 1.0), (BIAS_V, 1.0))
    ):
        cols = slice(j * width, (j + 1) * width)
        part = dot_nn(x[...], w_a[:, cols]) + small[row : row + 1, :]
        qkv[:, cols] = (part * factor).astype(BF16)
    attention(info, qkv, context, lse, bias)
    flush(7, context)
    acc[...] = dot_nn(context[...], w_a[:, 3 * width : 4 * width])

    def norm_one(rows, carry):
        total = x[rows, :].astype(F32) + acc[rows, :]
        normed, inverse = norm(total + small[BIAS_OUT : BIAS_OUT + 1, :])
        n1[rows, :] = normed
        n1_low[rows, :] = normed.astype(BF16)
        inv1[rows, :] = jnp.broadcast_to(inverse, (CHUNK, LANES))
        hidden = normed * small[GAIN_ATTN : GAIN_ATTN + 1, :]
        hid[rows, :] = (hidden + small[SHIFT_ATTN : SHIFT_ATTN + 1, :]).astype(BF16)
        return carry

    by_rows(norm_one)
    flush(8, hid)


def up_tile(j, hid, w_up, bias_up, act, d_act):
    cols = slice(j * FF_TILE, (j + 1) * FF_TILE)
    pre = dot_nn(hid[...], w_up[:, cols]) + bias_up[:, cols]
    below = 0.5 * (1.0 + lax.erf(pre * 0.7071067811865476))
    density = jnp.exp(pre * pre * -0.5) * 0.3989422804014327
    act[:, cols] = (pre * below).astype(BF16)
    d_act[:, cols] = (below + pre * density).astype(BF16)


def down_tile(j, act, w_down, acc):
    cols = slice(j * FF_TILE, (j + 1) * FF_TILE)
    part = dot_nn(act[:, cols], w_down[cols, :])
    acc[...] = part if j == 0 else acc[...] + part


def layer_end(small, n1, n2, inv2, out, acc):
    def norm_two(rows, carry):
        hidden = n1[rows, :] * small[GAIN_ATTN : GAIN_ATTN + 1, :]
        hidden = hidden + small[SHIFT_ATTN : SHIFT_ATTN + 1, :]
        normed, inverse = norm(hidden + acc[rows, :] + small[BIAS_DOWN : BIAS_DOWN + 1, :])
        n2[rows, :] = normed.astype(BF16)
        inv2[rows, :] = jnp.broadcast_to(inverse, (CHUNK, LANES))
        out[rows, :] = (
            normed * small[GAIN_FFN : GAIN_FFN + 1, :] + small[SHIFT_FFN : SHIFT_FFN + 1, :]
        ).astype(BF16)
        return carry

    by_rows(norm_two)


def forward_ffn_body(
    info, flush, w_up, w_down, small, bias_up, n1, hid, d_act, n2, inv2, out, act, acc
):
    tiles = act.shape[1] // FF_TILE
    up_tile(0, hid, w_up, bias_up, act, d_act)
    for j in range(1, tiles):
        up_tile(j, hid, w_up, bias_up, act, d_act)
        down_tile(j - 1, act, w_down, acc)
    flush(4, act)
    down_tile(tiles - 1, act, w_down, acc)
    layer_end(small, n1, n2, inv2, out, acc)


def forward_up_body(info, flush, w_up, bias_up, hid, d_act, act):
    for j in range(act.shape[1] // FF_TILE):
        up_tile(j, hid, w_up, bias_up, act, d_act)
    flush(2, act)


def forward_down_body(info, flush, w_down, small, n1, act, n2, inv2, out, acc):
    for j in range(act.shape[1] // FF_TILE):
        down_tile(j, act, w_down, acc)
    layer_end(small, n1, n2, inv2, out, acc)


def bias_scratch():
    return pltpu.VMEM((3, 3 * SEGMENT, 3 * SEGMENT), F32)


def joined_shape(pieces):
    share, n = pieces[0].shape[-2:]
    return (((16 * share, n), BF16),)


def forward_attn(step, info, tokens, received, w_a, small, held=None, pieces=()):
    width = small.shape[1]
    rows = ((ROWS, width), BF16)
    shapes = (
        ((ROWS, 3 * width), BF16),
        ((HEADS, 8, 256), F32),
        ((ROWS, width), F32),
        ((ROWS, LANES), F32),
    ) + (rows,) * 5
    if pieces:

        def body(info, flush, tok, rec, small, qkv, lse, n1, inv1, hid, n1_low, w_a, *rest):
            outs = (qkv, lse, n1, inv1, hid, n1_low)
            forward_attn_body(info, flush, tok, rec, w_a, small, *outs, *rest)

        ins = (info, tokens, received, small)
        shapes += joined_shape(pieces)
    else:
        body = forward_attn_body
        ins = (info, tokens, received, w_a, small)
    return kernel_call(
        body,
        "forward_attn",
        step,
        ins,
        shapes,
        held,
        [pltpu.VMEM(*rows)] * 2
        + [pltpu.VMEM((ROWS, width), F32), bias_scratch(), pltpu.SemaphoreType.DMA],
        LIMIT + 1.2,
        far=(6, 7, 8),
        pieces=pieces,
        far_ins=(0,),
    )


def forward_ffn(step, info, w_up, w_down, small, bias_up, n1, hid, held=None):
    width, ff = small.shape[1], bias_up.shape[1]
    return kernel_call(
        forward_ffn_body,
        "forward_ffn",
        step,
        (info, w_up, w_down, small, bias_up, n1, hid),
        (
            ((ROWS, ff), BF16),
            ((ROWS, width), BF16),
            ((ROWS, LANES), F32),
            ((ROWS, width), BF16),
            ((ROWS, ff), BF16),
        ),
        held,
        [pltpu.VMEM((ROWS, ff), BF16), pltpu.VMEM((ROWS, width), F32)],
        LIMIT + 2.4,
        far=(4,),
    )


def forward_up(step, info, pieces, bias_up, hid):
    ff = bias_up.shape[1]

    def body(info, flush, bias_up, hid, d_act, act, w_up):
        forward_up_body(info, flush, w_up, bias_up, hid, d_act, act)

    return kernel_call(
        body,
        "forward_up",
        step,
        (info, bias_up, hid),
        (((ROWS, ff), BF16),) * 3 + joined_shape(pieces),
        None,
        [],
        LIMIT,
        far=(2,),
        pieces=pieces,
    )


def forward_down(step, info, pieces, small, n1, act):
    width = small.shape[1]

    def body(info, flush, small, n1, act, n2, inv2, out, w_down, acc):
        forward_down_body(info, flush, w_down, small, n1, act, n2, inv2, out, acc)

    shapes = (((ROWS, width), BF16), ((ROWS, LANES), F32), ((ROWS, width), BF16))
    return kernel_call(
        body,
        "forward_down",
        step,
        (info, small, n1, act),
        shapes + joined_shape(pieces),
        None,
        [pltpu.VMEM((ROWS, width), F32)],
        LIMIT,
        pieces=pieces,
    )


def norm_back_rows(upstream, normed, inverse, gain, grad, low):
    zeros = jnp.zeros((8, grad.shape[1]), F32)

    def step(rows, carry):
        up, nm = upstream(rows), normed(rows)
        values = norm_back(up, nm, inverse(rows), gain)
        grad[rows, :] = values
        rounded = values.astype(BF16)
        low(rows, rounded)
        return (
            carry[0] + fold(up),
            carry[1] + fold(up * nm),
            carry[2] + fold(rounded.astype(F32)),
        )

    sums = by_rows(step, (zeros, zeros, zeros))
    return [jnp.sum(part, axis=0, keepdims=True) for part in sums]


def ffn_back_body(
    far,
    info,
    flush,
    cot,
    rec,
    w_up,
    w_down,
    small,
    n1,
    inv1,
    d_act,
    n2,
    inv2,
    d_branch,
    sums,
    d_first,
    d_ffn,
    d_pre,
    acc,
):
    if not far:

        def flush(index, ref):
            pass

    width = rec.shape[1]
    ff = d_pre.shape[1]
    tiles = ff // FF_TILE

    last = info[SECTION] == 1

    def upstream(rows):
        return jnp.where(last, cot[rows, :], rec[rows, :]).astype(F32)

    def keep_ffn(rows, low):
        d_ffn[rows, :] = low

    sum_g, sum_gn, sum_d = norm_back_rows(
        upstream,
        lambda rows: n2[rows, :].astype(F32),
        lambda rows: inv2[rows, :1],
        small[GAIN_FFN : GAIN_FFN + 1, :],
        acc,
        keep_ffn,
    )
    flush(3, d_ffn)
    sums[1:2, :width] = sum_d
    sums[1:2, width : 2 * width] = sum_gn
    sums[1:2, 2 * width : 3 * width] = sum_g

    def first(j):
        cols = slice(j * FF_TILE, (j + 1) * FF_TILE)
        part = dot_nt(d_ffn[...], w_down[cols, :]) * d_act[:, cols].astype(F32)
        low = part.astype(BF16)
        d_pre[:, cols] = low
        sums[0:1, cols] = jnp.sum(fold(low.astype(F32)), axis=0, keepdims=True)

    def second(j):
        cols = slice(j * FF_TILE, (j + 1) * FF_TILE)
        acc[...] += dot_nt(d_pre[:, cols], w_up[:, cols])

    first(0)
    for j in range(1, tiles):
        first(j)
        second(j - 1)
    flush(4, d_pre)
    second(tiles - 1)

    def keep_branch(rows, low):
        d_branch[rows, :] = low

    sum_g, sum_gn, sum_d = norm_back_rows(
        lambda rows: acc[rows, :],
        lambda rows: n1[rows, :].astype(F32),
        lambda rows: inv1[rows, :1],
        small[GAIN_ATTN : GAIN_ATTN + 1, :],
        d_first,
        keep_branch,
    )
    flush(5, d_branch)
    sums[1:2, 3 * width :] = sum_gn
    sums[2:3, :width] = sum_g
    sums[2:3, width : 2 * width] = sum_d


def ffn_back(step, info, cotangent, received, w_up, w_down, small, attn, ffn, held=None, far=False):
    width, ff = w_up.shape
    rows, wide = ((ROWS, width), BF16), ((ROWS, ff), BF16)
    shapes = (rows, ((8, ff), F32), ((ROWS, width), F32), rows, wide) + ((rows,) if far else ())
    scratch = [pltpu.VMEM(*rows), pltpu.VMEM(*wide)] if far else []
    return kernel_call(
        functools.partial(ffn_back_body, far),
        "ffn_backward",
        step,
        (info, cotangent, received, w_up, w_down, small, attn[5], attn[3], ffn[0], ffn[1], ffn[2]),
        shapes,
        held,
        scratch + [pltpu.VMEM((ROWS, width), F32)],
        LIMIT + (3 if far else 0),
        far=(3, 4, 5) if far else (),
    )


def attn_back_body(
    far, info, flush, w_a, d_first, d_branch, qkv, lse, grads, sums, d_qkv, d_context, bias
):
    if not far:

        def flush(index, ref):
            pass

    width = d_first.shape[1]

    d_context[...] = dot_nt(d_branch[...], w_a[:, 3 * width : 4 * width]).astype(BF16)
    attention_back(info, qkv, d_context, lse, bias, d_qkv)
    flush(2, d_qkv)
    grad = d_first[...] + dot_nt(d_qkv[...], w_a[:, : 3 * width])
    low = grad.astype(BF16)
    grads[...] = low
    for row, at in ((0, 0), (1, 2 * width)):
        sums[row : row + 1, :] = jnp.sum(
            fold(d_qkv[:, at : at + width].astype(F32)), axis=0, keepdims=True
        )


def attn_back(step, info, w_a, d_first, d_branch, attn, held=None, far=False):
    width = d_first.shape[1]
    rows, wide = ((ROWS, width), BF16), ((ROWS, 3 * width), BF16)
    return kernel_call(
        functools.partial(attn_back_body, far),
        "attention_backward",
        step,
        (info, w_a, d_first, d_branch, attn[0], attn[1]),
        (rows, ((8, width), F32), wide),
        held,
        ([pltpu.VMEM(*wide)] if far else []) + [pltpu.VMEM(*rows), bias_scratch()],
        LIMIT + (1.8 if far else 0),
        far=(2,) if far else (),
    )


def split_blocks(values, place, halves, cols, first_z=0):
    share = halves.shape[4]
    core, y, pair = place[0], place[1], place[2]
    for index in range(values.shape[0] // (4 * share)):
        z = first_z + index
        for yy in range(2):
            for cc in range(2):
                at = (index * 4 + yy * 2 + cc) * share
                part = values[at : at + share].astype(BF16)
                to = [jnp.bitwise_xor(core, cc), jnp.bitwise_xor(y, yy), jnp.bitwise_xor(pair, z // 2)]
                halves[(*to, z % 2, slice(None), cols)] = part


def grad_call(body, name, place, far, near, share, n, cuts, fetch=True):
    shape = (2, 2, 2, share, n)
    total = sum(cuts)

    def kernel(place, *refs):
        sources, refs = refs[: len(far)], refs[len(far) :]
        kept, refs = refs[: len(near)], refs[len(near) :]
        if not fetch:
            refs = (*refs[:3], *sources, refs[-1])
        mine_out, theirs_out, halves, *held, sems = refs
        copies = []
        for src, dst, cut in zip(sources, held, cuts):
            size = src.shape[1] // cut
            group = []
            for i in range(cut):
                cols = slice(i * size, (i + 1) * size)
                sem = sems.at[sum(map(len, copies)) + i]
                group.append(pltpu.make_async_copy(src.at[:, cols], dst.at[:, cols], sem))
            copies.append(group)
        for i in range(max(cuts) if fetch else 0):
            for group in copies:
                if i < len(group):
                    group[i].start()
        done = set()

        def wait(index, part=0):
            if fetch and (index, part) not in done:
                done.add((index, part))
                copies[index][part].wait()

        sent = []

        def flush(*at):
            for core, dst in ((1, theirs_out), (0, mine_out)):
                src = halves.at[(core, *at)]
                copy = pltpu.make_async_copy(src, dst.at[at], sems.at[total + len(sent)])
                copy.start()
                sent.append(copy)

        body(place, wait, flush, held, kept, halves)
        for copy in sent:
            copy.wait()

    held = far if fetch else ()
    scratch = [pltpu.VMEM((2, *shape), BF16)] + [pltpu.VMEM(x.shape, x.dtype) for x in held]
    size = sum(x.size * 2 for x in held) + 32 * share * n
    return pl.pallas_call(
        kernel,
        in_specs=[SCALARS] + [FAR if fetch else WHOLE] * len(far) + [WHOLE] * len(near),
        out_specs=[FAR] * 2,
        out_shape=[pltpu.HBM(shape, BF16)] * 2,
        scratch_shapes=scratch + [pltpu.SemaphoreType.DMA((total + 8,))],
        compiler_params=pltpu.CompilerParams(vmem_limit_bytes=size + LIMIT_GRAD * 1024 * 1024),
        cost_estimate=COST,
        name=name,
    )(place, *(in_hbm(far) if fetch else far), *near)


def stacked(one, two, cols=slice(None)):
    return jnp.concatenate([one[:, cols], two[:, cols]], axis=0)


def grad_down_body(place, wait, flush, held, kept, halves):
    d_middle, act, act2 = held
    wait(0)
    right = stacked(d_middle, kept[0])
    rows = 4 * halves.shape[4]
    for z in range(4):
        wait(1, z)
        wait(2, z)
        left = stacked(act, act2, slice(z * rows, (z + 1) * rows))
        split_blocks(dot_tn(left, right), place, halves, slice(None), z)
        if z % 2:
            pair = pl.ds(jnp.bitwise_xor(place[2], z // 2), 1)
            flush(slice(None), pair)


def grad_up_body(place, wait, flush, held, kept, halves):
    hid, hid2, d_middle = held
    wait(0)
    wait(1)
    left = stacked(hid, hid2)
    tile = d_middle.shape[1] // 4
    for i in range(4):
        wait(2, i)
        cols = slice(i * tile, (i + 1) * tile)
        split_blocks(dot_tn(left, stacked(d_middle, kept[0], cols)), place, halves, cols)
        flush(slice(None), slice(None), slice(None), slice(None), cols)


def write_table(place, sums, halves, first):
    share = halves.shape[4]
    width, wide = sums[2].shape[1], sums[0].shape[1]
    ffn, attn = sums[0][...] + sums[1][...], sums[2][...] + sums[3][...]
    vectors = [attn[0:1], attn[1:2], ffn[2:3, width : 2 * width], ffn[1:2, 3 * width : 4 * width]]
    vectors += [ffn[2:3, :width]] + [ffn[1:2, i * width : (i + 1) * width] for i in range(3)]
    vectors = jnp.concatenate(vectors, axis=0)
    core, y, pair = place[0], place[1], place[2]
    count = wide // width
    for at in range(16):
        z, yy, cc = at // 4, (at // 2) % 2, at % 2
        rows = [vectors[:, at * share : (at + 1) * share]]
        for i in range(count):
            begin = (at * count + i) * share
            rows.append(ffn[0:1, begin : begin + share])
        rows.append(jnp.zeros((share - 8 - count, share), F32))
        part = jnp.concatenate(rows, axis=0)
        part = jnp.concatenate([part, jnp.zeros((share, LANES - share), F32)], axis=1)
        to = [jnp.bitwise_xor(core, cc), jnp.bitwise_xor(y, yy), jnp.bitwise_xor(pair, z // 2)]
        halves[(*to, z % 2, slice(None), slice(first, first + LANES))] = part.astype(BF16)


def grad_attn_body(place, wait, flush, held, kept, halves):
    x, x2, d_middle, context, context2, d_branch = held
    width = x.shape[1]
    wait(0)
    wait(1)
    left = stacked(x, x2)
    for i in range(3):
        wait(2, i)
        cols = slice(i * width, (i + 1) * width)
        split_blocks(dot_tn(left, stacked(d_middle, kept[0], cols)), place, halves, cols)
        flush(slice(None), slice(None), slice(None), slice(None), cols)
    for i in range(3, 6):
        wait(i)
    values = dot_tn(stacked(context, context2), stacked(d_branch, kept[1]))
    split_blocks(values, place, halves, slice(3 * width, 4 * width))
    write_table(place, kept[2:], halves, 4 * width)
    cols = slice(3 * width, 4 * width + LANES)
    flush(slice(None), slice(None), slice(None), slice(None), cols)


def weight_grad(a, b):
    return sum(dot_tn(one, two) for one, two in zip(a, b)).astype(BF16)


def tie(value, *others):
    return lax.optimization_barrier((value, others))[0]


def after(before, *values):
    return lax.optimization_barrier((values, tuple(before)))[0]


class Grid:
    def __init__(self):
        index = lax.axis_index("dp")
        self.core = index % 2
        self.y = (index // 2) % 2
        self.low = (index // 4) % 2
        self.pair = index // 8
        self.is_middle = self.low != self.pair

    def move(self, block, route):
        return lax.ppermute(block, "dp", route)

    def swap_core(self, block):
        return self.move(block, [(i, i ^ 1) for i in range(16)])

    def swap_y(self, block):
        return self.move(block, [(i, i ^ 2) for i in range(16)])

    def swap_near(self, block):
        return self.move(block, [(i, i ^ 4) for i in range(16)])

    def swap_middle(self, block):
        return self.move(block, [(i, i ^ 12) for i in range(4, 12)])

    def send_out(self, block):
        return self.move(block, [(i, i ^ 4) for i in range(4, 12)])

    def send_in(self, block):
        return self.move(block, [(i, i ^ 4) for i in range(16) if not 4 <= i < 12])

    def skip_out(self, block):
        return self.move(block, [(i, i ^ 8) for i in range(4, 12)])

    def skip_in(self, block):
        return self.move(block, [(i, i ^ 8) for i in range(16) if not 4 <= i < 12])

    def picked(self, blocks, at, axis):
        return lax.dynamic_index_in_dim(blocks, at, axis, keepdims=False)

    def ordered(self, pieces):
        near, far = (self.pair * 2 + self.low, self.pair * 2 + 1 - self.low), (
            jnp.where(self.pair == 0, 2, 1),
            jnp.where(self.pair == 0, 3, 0),
        )
        places = []
        for index in range(8):
            dc, dy, away = index // 4, (index // 2) % 2, index % 2
            for z in far if away else near:
                places.append(z * 4 + (self.y ^ dy) * 2 + (self.core ^ dc))
        return jnp.zeros_like(jnp.concatenate(pieces)).at[jnp.stack(places)].set(
            jnp.concatenate(pieces)
        )


def passed_along(block, axis, distance):
    devices = range(lax.axis_size(axis))
    route = [(i - distance, i) for i in devices if i - distance in devices]
    return lax.ppermute(block, axis, route)


def on_device(
    tokens,
    cotangent,
    bucket,
    lengths,
    w_qkv,
    bias_q,
    bias_v,
    w_out,
    bias_out,
    gain_attn,
    shift_attn,
    w_up,
    bias_up,
    w_down,
    bias_down,
    gain_ffn,
    shift_ffn,
):
    section = lax.axis_index("section")
    width = tokens.shape[2]
    ff = w_up.shape[2]
    share = bias_q.shape[1]
    n_dp = width // share
    vectors = (bias_q, bias_v, bias_out, gain_attn, shift_attn, bias_down, gain_ffn, shift_ffn)
    by_links = n_dp == 16 and share % 16 == 0
    shares = ff // width
    count = len(vectors) + shares
    row_table = jnp.concatenate(vectors + (bias_up.reshape(shares, share),))
    row_table = lax.optimization_barrier(row_table).astype(BF16)
    part_a = jnp.concatenate([w_qkv[0], w_out[0]], axis=1).astype(BF16)
    part_up, part_down = w_up[0].astype(BF16), w_down[0].astype(BF16)
    if by_links:
        grid = Grid()
        place = jnp.stack([grid.core, grid.y, grid.pair, grid.low])
        padded = jnp.pad(row_table, ((0, share - count), (0, LANES - share)))
        part_a = jnp.concatenate([part_a, padded], axis=1)
        got_a, got_up = grid.swap_near(part_a), grid.swap_near(part_up)
        down_other = grid.swap_y(part_down)
        ended = (got_a, got_up, down_other)
        near_a, near_up = jnp.stack([part_a, got_a]), jnp.stack([part_up, got_up])

        near_a, both_down = after(ended, near_a, jnp.stack([part_down, down_other]))
        middle_a, got_down = grid.swap_middle(near_a), grid.swap_near(both_down)
        near_a_y = grid.swap_y(near_a)
        ended = (middle_a, got_down, near_a_y)
        near_down = jnp.stack([part_down, got_down[0]])
        near_down_y = jnp.stack([down_other, got_down[1]])

        middle_a, near_up = after(ended, middle_a, near_up)
        out_a, middle_up = grid.send_out(middle_a), grid.swap_middle(near_up)
        near_up_y = grid.swap_y(near_up)
        ended = (out_a, middle_up, near_up_y)
        far_a = jnp.where(grid.is_middle, middle_a, out_a)

        middle_up, near_down, far_a, near_a, near_a_y = after(
            ended, middle_up, near_down, far_a, near_a, near_a_y
        )
        out_up, middle_down = grid.send_out(middle_up), grid.swap_middle(near_down)
        far_a_y = grid.swap_y(far_a)
        near_a_c, near_a_yc = grid.swap_core(near_a), grid.swap_core(near_a_y)
        ended = (out_up, middle_down, far_a_y, near_a_c, near_a_yc)
        far_up = jnp.where(grid.is_middle, middle_up, out_up)

        middle_down, near_down_y, far_up, far_a, far_a_y = after(
            ended, middle_down, near_down_y, far_up, far_a, far_a_y
        )
        out_down, middle_down_y = grid.send_out(middle_down), grid.swap_middle(near_down_y)
        far_up_y = grid.swap_y(far_up)
        far_a_c, far_a_yc = grid.swap_core(far_a), grid.swap_core(far_a_y)
        pieces_a = (near_a, far_a, near_a_y, far_a_y, near_a_c, far_a_c, near_a_yc, far_a_yc)
        table = grid.ordered([piece[:, :, 4 * width :] for piece in pieces_a])
        table = table[:, :count, :share]
    else:
        place = jnp.zeros((4,), jnp.int32)
        w_a, full_up, full_down = (
            lax.all_gather(part, "dp", axis=0, tiled=True) for part in (part_a, part_up, part_down)
        )
        table = lax.all_gather(row_table[None], "dp", axis=0, tiled=True)
    table = table.astype(F32).transpose(1, 0, 2)
    rows = table[:8].reshape(8, width)
    small = jnp.concatenate(
        [rows[:1], jnp.zeros((1, width), F32), rows[1:], jnp.zeros((7, width), F32)]
    )
    full_bias_up = table[8:].transpose(1, 0, 2).reshape(1, ff)

    def info(step, micro):
        picked = jnp.clip(micro, 0, 1)
        run = ((micro >= 0) & (micro <= 1)).astype(jnp.int32)
        head = jnp.stack([run, picked, section, lax.dynamic_index_in_dim(bucket, picked, 0, False)[0]])
        return jnp.concatenate([head, lax.dynamic_index_in_dim(lengths, picked, 0, False), place])

    steps = jnp.stack(
        [info(step, step - section) for step in range(3)]
        + [info(step, step - 1 + section) for step in range(3)]
    )
    none = jnp.zeros((ROWS, width), BF16)

    def ahead(step, received, held=None):
        attn_held, ffn_held = (None, None) if held is None else held
        attn = forward_attn(step, steps, tokens, received, w_a, small, attn_held)
        return attn, forward_ffn(
            step, steps, full_up, full_down, small, full_bias_up, attn[2], attn[4], ffn_held
        )

    def back_ffn(step, upstream, kept, held=None, far=False):
        return ffn_back(
            3 + step, steps, cotangent[min(step, 1)], upstream, full_up, full_down, small, *kept, held, far
        )

    if by_links:
        *attn, w_a = forward_attn(0, steps, tokens, none, None, small, pieces=pieces_a)
        ended = after((attn[1],), out_down, middle_down_y, far_up_y)
        out_down, middle_down_y, far_up_y = ended
        far_down = jnp.where(grid.is_middle, middle_down, out_down)
        middle_down_y, near_up, far_up, near_up_y, far_up_y = after(
            ended, middle_down_y, near_up, far_up, near_up_y, far_up_y
        )
        out_down_y = grid.send_out(middle_down_y)
        pieces = (near_up, far_up, near_up_y, far_up_y)
        pieces += tuple(grid.swap_core(x) for x in pieces)
        *up, full_up = forward_up(0, steps, pieces, full_bias_up, attn[4])
        siblings = [grid.swap_core(x) for x in (near_down, far_down, near_down_y)]
        far_down_y = jnp.where(grid.is_middle, middle_down_y, tie(out_down_y, up[0]))
        pieces = (near_down, far_down, near_down_y, far_down_y, *siblings)
        pieces += (grid.swap_core(far_down_y),)
        *end, full_down = forward_down(0, steps, pieces, small, attn[2], up[1])
        outer = (attn, (up[0], *end, up[2]))
    else:
        outer = ahead(0, none)
    got = passed_along(outer[1][3], "section", 1)
    middle = ahead(1, got)
    got = passed_along(middle[1][3], "section", 1)
    back_outer = back_ffn(0, none, middle)
    back_attn_outer = attn_back(3, steps, w_a, back_outer[2], back_outer[0], middle[0])
    sent = passed_along(back_attn_outer[0], "section", -1)
    outer = ahead(2, got, outer)
    back_middle = back_ffn(1, sent, outer, far=by_links)
    back_attn_middle = attn_back(
        4, steps, w_a, back_middle[2], back_middle[0], outer[0], far=by_links
    )
    sent = passed_along(back_attn_middle[0], "section", -1)
    back_outer = back_ffn(2, sent, middle, back_outer)

    def last_attn_back(steps):
        return attn_back(5, steps, w_a, back_outer[2], back_outer[0], middle_attn, back_attn_outer)

    middle_attn = middle[0]
    x, context, hid = zip(outer[0][6:], middle[0][6:])
    act, outputs = (outer[1][4], middle[1][4]), (outer[1][3], middle[1][3])
    sums_ffn = back_middle[1], back_outer[1]
    d_ffn, d_pre = zip(back_middle[3:5], back_outer[3:5])
    d_branch = back_middle[-1 if by_links else 0], back_outer[0]

    def by_micro(one, two):
        first = section == 0
        return jnp.stack([jnp.where(first, one, two), jnp.where(first, two, one)])[None]

    if by_links:
        def plus(one, two):
            return one.astype(F32) + two.astype(F32)

        mine_down, theirs = grad_call(
            grad_down_body,
            "grad_down",
            place,
            (d_ffn[0], *act),
            (d_ffn[1],),
            ff // 16,
            width,
            (1, 4, 4),
            fetch=False,
        )
        got_down = grid.swap_core(theirs)
        mine_up, theirs = grad_call(
            grad_up_body,
            "grad_up",
            place,
            (tie(hid[0], mine_down), hid[1], d_pre[0]),
            (d_pre[1],),
            share,
            ff,
            (1, 1, 4),
            fetch=False,
        )

        def low_sum(*parts):
            return sum(part.astype(F32) for part in parts).astype(BF16)

        down_parts = [(mine_down[i, 1], got_down[i, 1]) for i in range(2)]
        out, out_y = (low_sum(*parts) for parts in down_parts)
        out, out_y, theirs, table = after((got_down, mine_up), out, out_y, theirs, steps)
        got_out, got_up = grid.send_in(out), grid.swap_core(theirs)
        last = last_attn_back(table)
        (got_out,) = after((last[1],), got_out)

        out_y, early_up, early_got = after((got_out,), out_y, mine_up, got_up)
        away_up, away_near = (low_sum(early_up[1, i], early_got[1, i]) for i in (1, 0))
        middle = low_sum(out, got_out)
        far_up_y, got_out_y = grid.swap_y(away_up), grid.send_in(out_y)
        got_middle = grid.swap_middle(middle)
        (first_x,) = after((middle, away_up, away_near), x[0])
    else:
        last = last_attn_back(steps)
    input_grads, sums_attn, d_qkv = zip(back_attn_middle, last)
    total = sums_ffn[0] + sums_ffn[1]
    total_attn = sums_attn[0] + sums_attn[1]
    vector_rows = jnp.stack(
        [
            total_attn[0],
            total_attn[1],
            total[2, width : 2 * width],
            total[1, 3 * width :],
            total[2, :width],
            total[1, :width],
            total[1, width : 2 * width],
            total[1, 2 * width : 3 * width],
        ]
    ).reshape(8, n_dp, share)
    table = jnp.concatenate(
        [vector_rows.transpose(1, 0, 2), total[0].reshape(n_dp, shares, share)], axis=1
    )
    if by_links:
        mine_a, theirs = grad_call(
            grad_attn_body,
            "grad_attn",
            place,
            (first_x, x[1], d_qkv[0], *context, d_branch[0]),
            (d_qkv[1], d_branch[1], *sums_ffn, *sums_attn),
            share,
            4 * width + LANES,
            (1, 1, 3, 1, 1, 1),
        )
        far_up_y, got_out_y, got_middle = after((mine_a,), far_up_y, got_out_y, got_middle)
        mine_up, got_up, mine_down, got_down = after(
            (mine_a,), mine_up, got_up, mine_down, got_down
        )

        theirs, away_up = after((far_up_y, got_out_y, got_middle), theirs, away_near)
        got_a, near_up_y = grid.swap_core(theirs), grid.swap_y(away_up)
        far_up = low_sum(mine_up[0, 1], got_up[0, 1], far_up_y)
        got_out_up = grid.send_in(far_up)
        got_middle_y = grid.swap_middle(low_sum(out_y, got_out_y))
        away_a, away_a_near = (low_sum(mine_a[1, i], got_a[1, i]) for i in (1, 0))
        got_out_up, got_middle_y, near_up_y = after(
            (away_a, away_a_near), got_out_up, got_middle_y, near_up_y
        )

        def down_sum(at, i):
            parts = (mine_down[i, 0], got_down[i, 0], (got_middle, got_middle_y)[i])
            return sum(grid.picked(part, at, 0).astype(F32) for part in parts)

        def up_sum(at):
            parts = (mine_up[0, 0], got_up[0, 0], near_up_y, got_middle_up)
            return sum(grid.picked(part, at, 0).astype(F32) for part in parts)

        def a_sum(at):
            parts = (mine_a[0, 0], got_a[0, 0], near_a_y)
            return sum(grid.picked(part, at, 0).astype(F32) for part in parts)

        (away_a,) = after((got_out_up, got_middle_y, near_up_y), away_a)
        far_a_y = grid.swap_y(away_a)
        got_middle_up = grid.swap_middle(low_sum(far_up, got_out_up))
        away = [down_sum(1 - grid.low, i).astype(BF16) for i in range(2)]
        got_near_down = grid.swap_near(jnp.stack(away))

        (away_a,) = after((far_a_y, got_middle_up, got_near_down), away_a_near)
        parts = (mine_a[0, 1], got_a[0, 1], far_a_y)
        one, other = (
            low_sum(*(grid.picked(part, at, 0) for part in parts)) for at in (grid.low, 1 - grid.low)
        )
        got_in, got_over, got_skip = grid.send_in(one), grid.swap_middle(one), grid.skip_in(other)
        near_a_y = grid.swap_y(away_a)
        both_down = [down_sum(grid.low, i) + got_near_down[i].astype(F32) for i in range(2)]
        away_down, away_up = both_down[1].astype(BF16), up_sum(1 - grid.low).astype(BF16)
        got_in, got_over, got_skip, near_a_y = after(
            (away_down, away_up), got_in, got_over, got_skip, near_a_y
        )

        away_down, away_up = after((got_in, got_over, got_skip, near_a_y), away_down, away_up)
        away = a_sum(1 - grid.low) + got_over.astype(F32) + got_skip.astype(F32)
        outputs, input_grads = after((got_in, got_over), outputs, input_grads)
        got_near_a = grid.swap_near(away.astype(BF16))
        got_middle_a = grid.swap_middle(low_sum(other, got_in))
        got_near_up, got_down_y = grid.swap_near(away_up), grid.swap_y(away_down)
        g_down = both_down[0] + got_down_y.astype(F32)
        g_up = up_sum(grid.low) + got_near_up.astype(F32)
        g_a = a_sum(grid.low) + got_near_a.astype(F32) + got_middle_a.astype(F32)
        table = g_a[:count, 4 * width : 4 * width + share]
    else:

        def summed(values):
            return lax.psum_scatter(values, "dp", scatter_dimension=0, tiled=True).astype(F32)

        g_down = summed(weight_grad(act, d_ffn))
        g_up = summed(weight_grad(hid, d_pre))
        g_qkv = weight_grad(x, d_qkv)
        g_out = weight_grad(context, d_branch)
        g_a = summed(jnp.concatenate([g_qkv, g_out], axis=1))
        table = summed(table)[0]
    hidden_states, input_grads = by_micro(*outputs), by_micro(*input_grads)
    g_down, g_up = g_down[None], g_up[None]
    g_qkv, g_out = g_a[None, :, : 3 * width], g_a[None, :, 3 * width : 4 * width]
    g_vectors = [table[i : i + 1] for i in range(8)]
    g_bias_up = table[8:].reshape(1, ff // n_dp)
    (
        g_bias_q,
        g_bias_v,
        g_bias_out,
        g_gain_attn,
        g_shift_attn,
        g_bias_down,
        g_gain_ffn,
        g_shift_ffn,
    ) = g_vectors
    return (
        hidden_states,
        input_grads,
        g_qkv,
        g_bias_q,
        g_bias_v,
        g_out,
        g_bias_out,
        g_gain_attn,
        g_shift_attn,
        g_up,
        g_bias_up,
        g_down,
        g_bias_down,
        g_gain_ffn,
        g_shift_ffn,
    )


def solution(mesh):
    matrix = P("section", "dp", None)
    vector = P("section", "dp")
    rows = P(None, "dp", None)
    outs = P("section", None, "dp", None)
    params = (
        matrix,
        vector,
        vector,
        matrix,
        vector,
        vector,
        vector,
        matrix,
        vector,
        matrix,
        vector,
        vector,
        vector,
    )
    return jax.shard_map(
        on_device,
        mesh=mesh,
        in_specs=(rows, rows, P(None, "dp"), P(None, "dp")) + params,
        out_specs=(outs, outs) + params,
        check_vma=False,
    )
```

```python
import functools

import jax
import jax.numpy as jnp
from jax import lax
from jax.experimental import pallas as pl
from jax.experimental.pallas import tpu as pltpu
from jax.sharding import PartitionSpec as P

HEADS = 12
SEGMENT = 64
PAIRS = 6
ROWS = 384
EPSILON = 1e-06
MASKED = -1000000000.0
LANES = 128
FF_TILE = 1024
LIMIT = 4
LIMIT_GRAD = 6
VMEM_LIMIT = 60 * 1024 * 1024
F32 = jnp.float32
BF16 = jnp.bfloat16

BIAS_Q, BIAS_K, BIAS_V, BIAS_OUT, GAIN_ATTN, SHIFT_ATTN, BIAS_DOWN, GAIN_FFN, SHIFT_FFN = range(9)
RUN, MICRO, SECTION, BUCKET, LENGTHS = range(5)
CORE, Y, PAIR, LOW = range(LENGTHS + PAIRS, LENGTHS + PAIRS + 4)

ANY = pl.BlockSpec(memory_space=pl.ANY)
WHOLE = pl.BlockSpec(memory_space=pltpu.VMEM)
SCALARS = pl.BlockSpec(memory_space=pltpu.SMEM)
FAR = pl.BlockSpec(memory_space=pltpu.HBM)
COST = pl.CostEstimate(flops=1, bytes_accessed=1, transcendentals=0)


def in_hbm(arrays):
    return [pltpu.with_memory_space_constraint(array, pltpu.HBM) for array in arrays]


def dot_nn(a, b):
    return lax.dot_general(a, b, (((1,), (0,)), ((), ())), preferred_element_type=F32)


def dot_nt(a, b):
    return lax.dot_general(a, b, (((1,), (1,)), ((), ())), preferred_element_type=F32)


def dot_tn(a, b):
    return lax.dot_general(a, b, (((0,), (0,)), ((), ())), preferred_element_type=F32)


class Row:
    def __init__(self, table, row):
        self.table, self.row = table, row

    def __getitem__(self, at):
        return self.table[self.row, at]


def fold(values):
    rows, n = values.shape
    return jnp.sum(values.reshape(rows // 8, 8, n), axis=0)


def write_bias(info, bias, block, count):
    segment = (info[BUCKET] + 1) * SEGMENT
    per_block = jnp.where(info[BUCKET] == 0, block // SEGMENT, 1)
    k_row = lax.broadcasted_iota(jnp.int32, (block, block), 0)
    q_row = lax.broadcasted_iota(jnp.int32, (block, block), 1)

    def pair_of(row):
        return (row >= segment).astype(jnp.int32) + (row >= 2 * segment).astype(jnp.int32)

    k_pair = pair_of(k_row)
    same = k_pair == pair_of(q_row)
    position = k_row - k_pair * segment
    for at in range(count):
        valid = [
            jnp.minimum(info[LENGTHS + jnp.minimum(at * per_block + i, PAIRS - 1)], segment)
            for i in range(3)
        ]
        length = jnp.where(k_pair == 0, valid[0], jnp.where(k_pair == 1, valid[1], valid[2]))
        bias[at, :block, :block] = jnp.where(same & (position < length), 0.0, MASKED)


def half_masks():
    lane = lax.broadcasted_iota(jnp.int32, (1, LANES), 1)
    low = (lane < LANES // 2).astype(F32)
    return low.astype(BF16), (1.0 - low).astype(BF16)


def by_block(info, body):
    @pl.when(info[BUCKET] == 1)
    def _():
        body(2 * SEGMENT, ROWS // (2 * SEGMENT))

    @pl.when(info[BUCKET] != 1)
    def _():
        body(3 * SEGMENT, ROWS // (3 * SEGMENT))


def attention(info, qkv, context, lse, bias):
    width = context.shape[1]
    low, high = half_masks()

    def both_heads(values):
        return jnp.concatenate([values * low, values * high], axis=0)

    def body(block, count):
        write_bias(info, bias, block, count)

        def pair_step(pair, carry):
            at_q = pl.multiple_of(pair * LANES, LANES)
            at_k = pl.multiple_of(width + pair * LANES, LANES)
            at_v = pl.multiple_of(2 * width + pair * LANES, LANES)
            rows = [pl.ds(at * block, block) for at in range(count)]
            q = [qkv[r, pl.ds(at_q, LANES)] for r in rows]
            k = [both_heads(qkv[r, pl.ds(at_k, LANES)]) for r in rows]
            v = [both_heads(qkv[r, pl.ds(at_v, LANES)]) for r in rows]
            masks = [bias[at, :block, :block] for at in range(count)]
            scores = [
                dot_nt(k[at], q[at]).reshape(2, block, block) + masks[at][None]
                for at in range(count)
            ]
            tops = [jnp.max(x, axis=1, keepdims=True) for x in scores]
            weights = [jnp.exp(x - top) for x, top in zip(scores, tops)]
            totals = [jnp.sum(x, axis=1, keepdims=True) for x in weights]
            probs = [
                (x * (1.0 / total)).astype(BF16).reshape(2 * block, block)
                for x, total in zip(weights, totals)
            ]
            parts = [dot_tn(x, values) for x, values in zip(probs, v)]
            for at in range(count):
                ends = tops[at] + jnp.log(totals[at])
                for half in range(2):
                    lse[2 * pair + half, at : at + 1, :block] = ends[half]
                context[rows[at], pl.ds(at_q, LANES)] = parts[at].astype(BF16)
            return carry

        def steps(i, carry):
            for sub in range(3):
                pair_step(i * 3 + sub, carry)
            return carry

        lax.fori_loop(0, HEADS // 2 // 3, steps, 0)

    by_block(info, body)


def attention_back(info, qkv, d_context, lse, bias, d_qkv):
    width = d_context.shape[1]
    low, high = half_masks()
    scale = (width // HEADS) ** -0.5

    def both_heads(values):
        return jnp.concatenate([values * low, values * high], axis=0)

    def flat(values):
        return values.astype(BF16).reshape(2 * values.shape[1], values.shape[2])

    def body(block, count):
        write_bias(info, bias, block, count)

        def pair_step(pair, carry):
            at_q = pl.multiple_of(pair * LANES, LANES)
            at_k = pl.multiple_of(width + pair * LANES, LANES)
            at_v = pl.multiple_of(2 * width + pair * LANES, LANES)
            is_low = lax.broadcasted_iota(jnp.int32, (block, LANES), 1) < LANES // 2
            rows = [pl.ds(at * block, block) for at in range(count)]
            q = [qkv[r, pl.ds(at_q, LANES)] for r in rows]
            k = [both_heads(qkv[r, pl.ds(at_k, LANES)]) for r in rows]
            v = [both_heads(qkv[r, pl.ds(at_v, LANES)]) for r in rows]
            d_out = [d_context[r, pl.ds(at_q, LANES)] for r in rows]
            masks = [bias[at, :block, :block] for at in range(count)]
            scores = [
                dot_nt(k[at], q[at]).reshape(2, block, block) + masks[at][None]
                for at in range(count)
            ]
            d_probs = [dot_nt(v[at], d_out[at]).reshape(2, block, block) for at in range(count)]
            ends = [
                jnp.stack([lse[2 * pair + half, at : at + 1, :block] for half in range(2)])
                for at in range(count)
            ]
            probs = [jnp.exp(x - end) for x, end in zip(scores, ends)]
            d_v = [dot_nn(flat(x), d_out[at]) for at, x in enumerate(probs)]
            inner = [jnp.sum(x * d_x, axis=1, keepdims=True) for x, d_x in zip(probs, d_probs)]
            d_scores = [
                flat(x * (d_x - total)) for x, d_x, total in zip(probs, d_probs, inner)
            ]
            d_k = [dot_nn(x, q[at]) for at, x in enumerate(d_scores)]
            d_q = [dot_tn(x, k[at]) for at, x in enumerate(d_scores)]
            for at, r in enumerate(rows):
                d_qkv[r, pl.ds(at_q, LANES)] = (d_q[at] * scale).astype(BF16)
                for to, part in ((at_k, d_k[at]), (at_v, d_v[at])):
                    part = jnp.where(is_low, part[:block], part[block:])
                    d_qkv[r, pl.ds(to, LANES)] = part.astype(BF16)
            return carry

        def steps(i, carry):
            for sub in range(3):
                pair_step(i * 3 + sub, carry)
            return carry

        lax.fori_loop(0, HEADS // 2 // 3, steps, 0)

    by_block(info, body)


def norm(values):
    centered = values - jnp.mean(values, axis=-1, keepdims=True)
    inverse = lax.rsqrt(jnp.mean(centered * centered, axis=-1, keepdims=True) + EPSILON)
    return centered * inverse, inverse


def norm_back(upstream, normed, inverse, gain):
    scaled = upstream * gain
    return inverse * (
        scaled
        - jnp.mean(scaled, axis=-1, keepdims=True)
        - normed * jnp.mean(scaled * normed, axis=-1, keepdims=True)
    )


CHUNK = 64


def by_rows(step, carry=0):
    def body(i, carry):
        return step(pl.ds(pl.multiple_of(i * CHUNK, CHUNK), CHUNK), carry)

    return lax.fori_loop(0, ROWS // CHUNK, body, carry)


def carry_over(src, dst):
    if src.shape[0] == ROWS:

        def step(rows, carry):
            dst[rows, :] = src[rows, :]
            return carry

        by_rows(step)
    else:
        dst[...] = src[...]


def join_copies(info, pieces, out, sems):
    core, y, pair, low = (info[i] for i in (CORE, Y, PAIR, LOW))
    near = (pair * 2 + low, pair * 2 + 1 - low)
    far = (jnp.where(pair == 0, 2, 1), jnp.where(pair == 0, 3, 0))
    share = pieces[0].shape[1]
    copies = []
    for index, piece in enumerate(pieces):
        dc, dy, away = index // 4, (index // 2) % 2, index % 2
        for i, z in enumerate(far if away else near):
            at = z * 4 + jnp.bitwise_xor(y, dy) * 2 + jnp.bitwise_xor(core, dc)
            rows = pl.ds(pl.multiple_of(at * share, 16), share)
            copies.append(pltpu.make_async_copy(piece.at[i], out.at[rows, :], sems.at[len(copies)]))
    return copies


def kernel_call(body, name, step, ins, out_shapes, held, scratch, limit, far=(), pieces=(), far_ins=()):
    held = [] if held is None else list(held)
    given = len(ins) - 1
    count = len(out_shapes)
    spec = [FAR if i in far else WHOLE for i in range(count)]

    def kernel(table, *refs):
        info = Row(table, step)
        blocks, refs = refs[: 8 * len(pieces)], refs[8 * len(pieces) :]
        kept = refs[given : given + len(held)]
        outs = refs[given + len(held) :][:count]
        own = refs[given + len(held) + count :]
        joins = [
            join_copies(
                info, blocks[8 * i : 8 * i + 8], outs[count - len(pieces) + i], own[len(scratch)].at[i]
            )
            for i in range(len(pieces))
        ]
        for copy in sum(joins, []):
            copy.start()

        def wait_for(join):
            def wait():
                for copy in join:
                    copy.wait()

            return wait

        waits = [wait_for(join) for join in joins]

        @pl.when(info[RUN] == 1)
        def _():
            copies = []

            def flush(index, ref):
                copy = pltpu.make_async_copy(ref, outs[index], own[-1].at[len(copies)])
                copy.start()
                copies.append(copy)

            near = [out for i, out in enumerate(outs) if i not in far]
            given_waits = (waits,) if pieces else ()
            body(info, flush, *given_waits, *refs[:given], *near, *own[: len(scratch)])
            for copy in copies:
                copy.wait()

        if held or pieces:

            @pl.when(info[RUN] != 1)
            def _():
                for wait in waits:
                    wait()
                for i, (src, dst) in enumerate(zip(kept, outs)):
                    if i not in far:
                        carry_over(src, dst)

    return pl.pallas_call(
        kernel,
        in_specs=[SCALARS]
        + [FAR] * (8 * len(pieces))
        + [FAR if i in far_ins else WHOLE for i in range(given)]
        + spec[: len(held)],
        out_specs=spec,
        out_shape=[
            pltpu.HBM(shape, kind) if i in far else jax.ShapeDtypeStruct(shape, kind)
            for i, (shape, kind) in enumerate(out_shapes)
        ],
        input_output_aliases={1 + given + i: i for i in range(len(held))},
        scratch_shapes=scratch
        + ([pltpu.SemaphoreType.DMA((len(pieces), 16))] if pieces else [])
        + ([pltpu.SemaphoreType.DMA((len(far),))] if far else []),
        compiler_params=pltpu.CompilerParams(vmem_limit_bytes=int(limit * 1024 * 1024)),
        cost_estimate=COST,
        name=name,
    )(
        ins[0],
        *in_hbm([piece for group in pieces for piece in group]),
        *(in_hbm([x])[0] if i in far_ins else x for i, x in enumerate(ins[1:])),
        *(in_hbm([x])[0] if i in far else x for i, x in enumerate(held)),
    )


def forward_attn_body(
    info, flush, tok, rec, w_a, small, qkv, lse, n1, inv1, hid, n1_low, x, context, acc, bias, sem, ready=None
):
    width = x.shape[1]

    @pl.when(info[SECTION] == 0)
    def _():
        copy = pltpu.make_async_copy(tok.at[info[MICRO]], x, sem)
        copy.start()
        copy.wait()

    @pl.when(info[SECTION] != 0)
    def _():
        x[...] = rec[...]

    flush(6, x)
    if ready is not None:
        ready()
    for j, (row, factor) in enumerate(
        ((BIAS_Q, (width // HEADS) ** -0.5), (BIAS_K, 1.0), (BIAS_V, 1.0))
    ):
        cols = slice(j * width, (j + 1) * width)
        part = dot_nn(x[...], w_a[:, cols]) + small[row : row + 1, :]
        qkv[:, cols] = (part * factor).astype(BF16)
    attention(info, qkv, context, lse, bias)
    flush(7, context)
    acc[...] = dot_nn(context[...], w_a[:, 3 * width : 4 * width])

    def norm_one(rows, carry):
        total = x[rows, :].astype(F32) + acc[rows, :]
        normed, inverse = norm(total + small[BIAS_OUT : BIAS_OUT + 1, :])
        n1[rows, :] = normed
        n1_low[rows, :] = normed.astype(BF16)
        inv1[rows, :] = jnp.broadcast_to(inverse, (CHUNK, LANES))
        hidden = normed * small[GAIN_ATTN : GAIN_ATTN + 1, :]
        hid[rows, :] = (hidden + small[SHIFT_ATTN : SHIFT_ATTN + 1, :]).astype(BF16)
        return carry

    by_rows(norm_one)


def up_tile(j, hid, w_up, bias_up, act, d_act):
    cols = slice(j * FF_TILE, (j + 1) * FF_TILE)
    pre = dot_nn(hid[...], w_up[:, cols]) + bias_up[:, cols]
    below = 0.5 * (1.0 + lax.erf(pre * 0.7071067811865476))
    density = jnp.exp(pre * pre * -0.5) * 0.3989422804014327
    act[:, cols] = (pre * below).astype(BF16)
    d_act[:, cols] = (below + pre * density).astype(BF16)


def down_tile(j, act, w_down, acc):
    cols = slice(j * FF_TILE, (j + 1) * FF_TILE)
    part = dot_nn(act[:, cols], w_down[cols, :])
    acc[...] = part if j == 0 else acc[...] + part


def layer_end(small, n1, n2, inv2, out, acc):
    def norm_two(rows, carry):
        hidden = n1[rows, :] * small[GAIN_ATTN : GAIN_ATTN + 1, :]
        hidden = hidden + small[SHIFT_ATTN : SHIFT_ATTN + 1, :]
        normed, inverse = norm(hidden + acc[rows, :] + small[BIAS_DOWN : BIAS_DOWN + 1, :])
        n2[rows, :] = normed.astype(BF16)
        inv2[rows, :] = jnp.broadcast_to(inverse, (CHUNK, LANES))
        out[rows, :] = (
            normed * small[GAIN_FFN : GAIN_FFN + 1, :] + small[SHIFT_FFN : SHIFT_FFN + 1, :]
        ).astype(BF16)
        return carry

    by_rows(norm_two)


def forward_ffn_body(
    info, flush, w_up, w_down, small, bias_up, n1, hid, d_act, n2, inv2, out, act, acc
):
    tiles = act.shape[1] // FF_TILE
    flush(5, hid)
    up_tile(0, hid, w_up, bias_up, act, d_act)
    for j in range(1, tiles):
        up_tile(j, hid, w_up, bias_up, act, d_act)
        down_tile(j - 1, act, w_down, acc)
    flush(4, act)
    down_tile(tiles - 1, act, w_down, acc)
    layer_end(small, n1, n2, inv2, out, acc)


def forward_down_body(info, flush, w_down, small, n1, act, n2, inv2, out, acc):
    for j in range(act.shape[1] // FF_TILE):
        down_tile(j, act, w_down, acc)
    layer_end(small, n1, n2, inv2, out, acc)


def bias_scratch():
    return pltpu.VMEM((3, 3 * SEGMENT, 3 * SEGMENT), F32)


def joined_shape(pieces):
    share, n = pieces[0].shape[-2:]
    return (((16 * share, n), BF16),)


def forward_attn(step, info, tokens, received, w_a, small, held=None):
    width = small.shape[1]
    rows = ((ROWS, width), BF16)
    return kernel_call(
        forward_attn_body,
        "forward_attn",
        step,
        (info, tokens, received, w_a, small),
        attn_shapes(width) + (rows, rows),
        held,
        [pltpu.VMEM(*rows)] * 2
        + [pltpu.VMEM((ROWS, width), F32), bias_scratch(), pltpu.SemaphoreType.DMA],
        LIMIT + 1.2,
        far=(6, 7),
        far_ins=(0,),
    )


def attn_shapes(width):
    rows = ((ROWS, width), BF16)
    return (
        ((ROWS, 3 * width), BF16),
        ((HEADS, 8, 256), F32),
        ((ROWS, width), F32),
        ((ROWS, LANES), F32),
        rows,
        rows,
    )


def forward_first_body(info, flush, waits, tok, rec, small, bias_up, *refs):
    attn_refs, (d_act, act, w_a, w_up), (x, context, acc, bias, sem) = refs[:6], refs[6:10], refs[10:]

    def flush_attn(index, ref):
        flush(index + 2, ref)

    forward_attn_body(
        info, flush_attn, tok, rec, w_a, small, *attn_refs, x, context, acc, bias, sem, waits[0]
    )
    hid = attn_refs[4]
    flush(10, hid)
    waits[1]()
    for j in range(act.shape[1] // FF_TILE):
        up_tile(j, hid, w_up, bias_up, act, d_act)
    flush(11, act)


def forward_first(step, info, tokens, received, small, bias_up, pieces):
    width, ff = small.shape[1], bias_up.shape[1]
    rows, wide = ((ROWS, width), BF16), ((ROWS, ff), BF16)
    return kernel_call(
        forward_first_body,
        "forward_first",
        step,
        (info, tokens, received, small, bias_up),
        attn_shapes(width)
        + (wide, wide, rows, rows, rows, wide)
        + joined_shape(pieces[0])
        + joined_shape(pieces[1]),
        None,
        [pltpu.VMEM(*rows)] * 2
        + [pltpu.VMEM((ROWS, width), F32), bias_scratch(), pltpu.SemaphoreType.DMA],
        LIMIT + 1.2,
        far=(8, 9, 10, 11),
        pieces=pieces,
        far_ins=(0,),
    )


def forward_ffn(step, info, w_up, w_down, small, bias_up, n1, hid, held=None):
    width, ff = small.shape[1], bias_up.shape[1]
    rows, wide = ((ROWS, width), BF16), ((ROWS, ff), BF16)
    return kernel_call(
        forward_ffn_body,
        "forward_ffn",
        step,
        (info, w_up, w_down, small, bias_up, n1, hid),
        (wide, rows, ((ROWS, LANES), F32), rows, wide, rows),
        held,
        [pltpu.VMEM((ROWS, ff), BF16), pltpu.VMEM((ROWS, width), F32)],
        LIMIT + 2.4,
        far=(4, 5),
    )


def forward_down(step, info, pieces, small, n1, act):
    width = small.shape[1]

    def body(info, flush, waits, small, n1, act, n2, inv2, out, w_down, acc):
        waits[0]()
        forward_down_body(info, flush, w_down, small, n1, act, n2, inv2, out, acc)

    shapes = (((ROWS, width), BF16), ((ROWS, LANES), F32), ((ROWS, width), BF16))
    return kernel_call(
        body,
        "forward_down",
        step,
        (info, small, n1, act),
        shapes + joined_shape(pieces),
        None,
        [pltpu.VMEM((ROWS, width), F32)],
        LIMIT,
        pieces=(pieces,),
    )


def norm_back_rows(upstream, normed, inverse, gain, grad, low):
    zeros = jnp.zeros((8, grad.shape[1]), F32)

    def step(rows, carry):
        up, nm = upstream(rows), normed(rows)
        values = norm_back(up, nm, inverse(rows), gain)
        grad[rows, :] = values
        rounded = values.astype(BF16)
        low(rows, rounded)
        return (
            carry[0] + fold(up),
            carry[1] + fold(up * nm),
            carry[2] + fold(rounded.astype(F32)),
        )

    sums = by_rows(step, (zeros, zeros, zeros))
    return [jnp.sum(part, axis=0, keepdims=True) for part in sums]


def ffn_back_body(
    far,
    info,
    flush,
    cot,
    rec,
    w_up,
    w_down,
    small,
    n1,
    inv1,
    d_act,
    n2,
    inv2,
    d_branch,
    sums,
    d_first,
    d_ffn,
    d_pre,
    acc,
):
    if not far:

        def flush(index, ref):
            pass

    width = rec.shape[1]
    ff = d_pre.shape[1]
    tiles = ff // FF_TILE

    last = info[SECTION] == 1

    def upstream(rows):
        return jnp.where(last, cot[rows, :], rec[rows, :]).astype(F32)

    def keep_ffn(rows, low):
        d_ffn[rows, :] = low

    sum_g, sum_gn, sum_d = norm_back_rows(
        upstream,
        lambda rows: n2[rows, :].astype(F32),
        lambda rows: inv2[rows, :1],
        small[GAIN_FFN : GAIN_FFN + 1, :],
        acc,
        keep_ffn,
    )
    flush(3, d_ffn)
    sums[1:2, :width] = sum_d
    sums[1:2, width : 2 * width] = sum_gn
    sums[1:2, 2 * width : 3 * width] = sum_g

    def first(j):
        cols = slice(j * FF_TILE, (j + 1) * FF_TILE)
        part = dot_nt(d_ffn[...], w_down[cols, :]) * d_act[:, cols].astype(F32)
        low = part.astype(BF16)
        d_pre[:, cols] = low
        sums[0:1, cols] = jnp.sum(fold(low.astype(F32)), axis=0, keepdims=True)

    def second(j):
        cols = slice(j * FF_TILE, (j + 1) * FF_TILE)
        acc[...] += dot_nt(d_pre[:, cols], w_up[:, cols])

    first(0)
    for j in range(1, tiles):
        first(j)
        second(j - 1)
    flush(4, d_pre)
    second(tiles - 1)

    def keep_branch(rows, low):
        d_branch[rows, :] = low

    sum_g, sum_gn, sum_d = norm_back_rows(
        lambda rows: acc[rows, :],
        lambda rows: n1[rows, :].astype(F32),
        lambda rows: inv1[rows, :1],
        small[GAIN_ATTN : GAIN_ATTN + 1, :],
        d_first,
        keep_branch,
    )
    sums[1:2, 3 * width :] = sum_gn
    sums[2:3, :width] = sum_g
    sums[2:3, width : 2 * width] = sum_d


def ffn_back(step, info, cotangent, received, w_up, w_down, small, attn, ffn, held=None, far=False):
    width, ff = w_up.shape
    rows, wide = ((ROWS, width), BF16), ((ROWS, ff), BF16)
    shapes = (rows, ((8, ff), F32), ((ROWS, width), F32), rows, wide)
    scratch = [pltpu.VMEM(*rows), pltpu.VMEM(*wide)] if far else []
    return kernel_call(
        functools.partial(ffn_back_body, far),
        "ffn_backward",
        step,
        (info, cotangent, received, w_up, w_down, small, attn[5], attn[3], ffn[0], ffn[1], ffn[2]),
        shapes,
        held,
        scratch + [pltpu.VMEM((ROWS, width), F32)],
        LIMIT + (3 if far else 0),
        far=(3, 4) if far else (),
    )


def attn_back_body(
    far, info, flush, w_a, d_first, d_branch, qkv, lse, grads, sums, d_qkv, d_context, bias
):
    if not far:

        def flush(index, ref):
            pass

    flush(3, d_branch)
    width = d_first.shape[1]

    d_context[...] = dot_nt(d_branch[...], w_a[:, 3 * width : 4 * width]).astype(BF16)
    attention_back(info, qkv, d_context, lse, bias, d_qkv)
    flush(2, d_qkv)
    grad = d_first[...] + dot_nt(d_qkv[...], w_a[:, : 3 * width])
    low = grad.astype(BF16)
    grads[...] = low
    for row, at in ((0, 0), (1, 2 * width)):
        sums[row : row + 1, :] = jnp.sum(
            fold(d_qkv[:, at : at + width].astype(F32)), axis=0, keepdims=True
        )


def attn_back(step, info, w_a, d_first, d_branch, attn, held=None, far=False):
    width = d_first.shape[1]
    rows, wide = ((ROWS, width), BF16), ((ROWS, 3 * width), BF16)
    return kernel_call(
        functools.partial(attn_back_body, far),
        "attention_backward",
        step,
        (info, w_a, d_first, d_branch, attn[0], attn[1]),
        (rows, ((8, width), F32), wide) + ((rows,) if far else ()),
        held,
        ([pltpu.VMEM(*wide)] if far else []) + [pltpu.VMEM(*rows), bias_scratch()],
        LIMIT + (1.8 if far else 0),
        far=(2, 3) if far else (),
    )


def split_blocks(values, place, halves, cols, first_z=0):
    share = halves.shape[4]
    core, y, pair = place[0], place[1], place[2]
    for index in range(values.shape[0] // (4 * share)):
        z = first_z + index
        for yy in range(2):
            for cc in range(2):
                at = (index * 4 + yy * 2 + cc) * share
                part = values[at : at + share].astype(BF16)
                to = [jnp.bitwise_xor(core, cc), jnp.bitwise_xor(y, yy), jnp.bitwise_xor(pair, z // 2)]
                halves[(*to, z % 2, slice(None), cols)] = part


def grad_call(body, name, place, far, near, share, n, cuts, fetch=True):
    shape = (2, 2, 2, share, n)
    total = sum(cuts)

    def kernel(place, *refs):
        sources, refs = refs[: len(far)], refs[len(far) :]
        kept, refs = refs[: len(near)], refs[len(near) :]
        if not fetch:
            refs = (*refs[:3], *sources, refs[-1])
        mine_out, theirs_out, halves, *held, sems = refs
        copies = []
        for src, dst, cut in zip(sources, held, cuts) if fetch else ():
            size = src.shape[1] // cut
            group = []
            for i in range(cut):
                cols = slice(i * size, (i + 1) * size)
                sem = sems.at[sum(map(len, copies)) + i]
                group.append(pltpu.make_async_copy(src.at[:, cols], dst.at[:, cols], sem))
            copies.append(group)
        for i in range(max(cuts)):
            for group in copies:
                if i < len(group):
                    group[i].start()
        done = set()

        def wait(index, part=0):
            if fetch and (index, part) not in done:
                done.add((index, part))
                copies[index][part].wait()

        sent = []

        def flush(*at):
            for core, dst in ((1, theirs_out), (0, mine_out)):
                src = halves.at[(core, *at)]
                copy = pltpu.make_async_copy(src, dst.at[at], sems.at[total + len(sent)])
                copy.start()
                sent.append(copy)

        body(place, wait, flush, held, kept, halves)
        for copy in sent:
            copy.wait()

    held = far if fetch else ()
    scratch = [pltpu.VMEM((2, *shape), BF16)] + [pltpu.VMEM(x.shape, x.dtype) for x in held]
    size = sum(x.size * 2 for x in held) + 32 * share * n
    return pl.pallas_call(
        kernel,
        in_specs=[SCALARS] + [FAR if fetch else WHOLE] * len(far) + [WHOLE] * len(near),
        out_specs=[FAR] * 2,
        out_shape=[pltpu.HBM(shape, BF16)] * 2,
        scratch_shapes=scratch + [pltpu.SemaphoreType.DMA((total + 8,))],
        compiler_params=pltpu.CompilerParams(vmem_limit_bytes=size + LIMIT_GRAD * 1024 * 1024),
        cost_estimate=COST,
        name=name,
    )(place, *(in_hbm(far) if fetch else far), *near)


def stacked(one, two, cols=slice(None)):
    return jnp.concatenate([one[:, cols], two[:, cols]], axis=0)


def grad_down_body(place, wait, flush, held, kept, halves):
    d_middle, act, act2 = held
    wait(0)
    right = stacked(d_middle, kept[0])
    rows = 4 * halves.shape[4]
    for z in range(4):
        wait(1, z)
        wait(2, z)
        left = stacked(act, act2, slice(z * rows, (z + 1) * rows))
        split_blocks(dot_tn(left, right), place, halves, slice(None), z)
        if z % 2:
            pair = pl.ds(jnp.bitwise_xor(place[2], z // 2), 1)
            flush(slice(None), pair)


def grad_up_body(place, wait, flush, held, kept, halves):
    hid, hid2, d_middle = held
    wait(0)
    wait(1)
    left = stacked(hid, hid2)
    tile = d_middle.shape[1] // 4
    for i in range(4):
        wait(2, i)
        cols = slice(i * tile, (i + 1) * tile)
        split_blocks(dot_tn(left, stacked(d_middle, kept[0], cols)), place, halves, cols)
        flush(slice(None), slice(None), slice(None), slice(None), cols)


def write_table(place, sums, halves, first):
    share = halves.shape[4]
    width, wide = sums[2].shape[1], sums[0].shape[1]
    ffn, attn = sums[0][...] + sums[1][...], sums[2][...] + sums[3][...]
    vectors = [attn[0:1], attn[1:2], ffn[2:3, width : 2 * width], ffn[1:2, 3 * width : 4 * width]]
    vectors += [ffn[2:3, :width]] + [ffn[1:2, i * width : (i + 1) * width] for i in range(3)]
    vectors = jnp.concatenate(vectors, axis=0)
    core, y, pair = place[0], place[1], place[2]
    count = wide // width
    for at in range(16):
        z, yy, cc = at // 4, (at // 2) % 2, at % 2
        rows = [vectors[:, at * share : (at + 1) * share]]
        for i in range(count):
            begin = (at * count + i) * share
            rows.append(ffn[0:1, begin : begin + share])
        rows.append(jnp.zeros((share - 8 - count, share), F32))
        part = jnp.concatenate(rows, axis=0)
        part = jnp.concatenate([part, jnp.zeros((share, LANES - share), F32)], axis=1)
        to = [jnp.bitwise_xor(core, cc), jnp.bitwise_xor(y, yy), jnp.bitwise_xor(pair, z // 2)]
        halves[(*to, z % 2, slice(None), slice(first, first + LANES))] = part.astype(BF16)


def grad_attn_body(place, wait, flush, held, kept, halves):
    x, x2, d_middle, context, context2, d_branch = held
    width = x.shape[1]
    wait(0)
    wait(1)
    left = stacked(x, x2)
    for i in range(3):
        wait(2, i)
        cols = slice(i * width, (i + 1) * width)
        split_blocks(dot_tn(left, stacked(d_middle, kept[0], cols)), place, halves, cols)
        flush(slice(None), slice(None), slice(None), slice(None), cols)
    for i in range(3, 6):
        wait(i)
    values = dot_tn(stacked(context, context2), stacked(d_branch, kept[1]))
    split_blocks(values, place, halves, slice(3 * width, 4 * width))
    write_table(place, kept[2:], halves, 4 * width)
    cols = slice(3 * width, 4 * width + LANES)
    flush(slice(None), slice(None), slice(None), slice(None), cols)


def weight_grad(a, b):
    return sum(dot_tn(one, two) for one, two in zip(a, b)).astype(BF16)


def tie(value, *others):
    return lax.optimization_barrier((value, others))[0]


def after(before, *values):
    return lax.optimization_barrier((values, tuple(before)))[0]


class Grid:
    def __init__(self):
        index = lax.axis_index("dp")
        self.core = index % 2
        self.y = (index // 2) % 2
        self.low = (index // 4) % 2
        self.pair = index // 8
        self.is_middle = self.low != self.pair

    def move(self, block, route):
        return lax.ppermute(block, "dp", route)

    def swap_core(self, block):
        return self.move(block, [(i, i ^ 1) for i in range(16)])

    def swap_y(self, block):
        return self.move(block, [(i, i ^ 2) for i in range(16)])

    def swap_near(self, block):
        return self.move(block, [(i, i ^ 4) for i in range(16)])

    def swap_middle(self, block):
        return self.move(block, [(i, i ^ 12) for i in range(4, 12)])

    def send_out(self, block):
        return self.move(block, [(i, i ^ 4) for i in range(4, 12)])

    def send_in(self, block):
        return self.move(block, [(i, i ^ 4) for i in range(16) if not 4 <= i < 12])

    def skip_out(self, block):
        return self.move(block, [(i, i ^ 8) for i in range(4, 12)])

    def skip_in(self, block):
        return self.move(block, [(i, i ^ 8) for i in range(16) if not 4 <= i < 12])

    def picked(self, blocks, at, axis):
        return lax.dynamic_index_in_dim(blocks, at, axis, keepdims=False)

    def ordered(self, pieces):
        near, far = (self.pair * 2 + self.low, self.pair * 2 + 1 - self.low), (
            jnp.where(self.pair == 0, 2, 1),
            jnp.where(self.pair == 0, 3, 0),
        )
        places = []
        for index in range(8):
            dc, dy, away = index // 4, (index // 2) % 2, index % 2
            for z in far if away else near:
                places.append(z * 4 + (self.y ^ dy) * 2 + (self.core ^ dc))
        return jnp.zeros_like(jnp.concatenate(pieces)).at[jnp.stack(places)].set(
            jnp.concatenate(pieces)
        )


def passed_along(block, axis, distance):
    devices = range(lax.axis_size(axis))
    route = [(i - distance, i) for i in devices if i - distance in devices]
    return lax.ppermute(block, axis, route)


def on_device(
    tokens,
    cotangent,
    bucket,
    lengths,
    w_qkv,
    bias_q,
    bias_v,
    w_out,
    bias_out,
    gain_attn,
    shift_attn,
    w_up,
    bias_up,
    w_down,
    bias_down,
    gain_ffn,
    shift_ffn,
):
    section = lax.axis_index("section")
    width = tokens.shape[2]
    ff = w_up.shape[2]
    share = bias_q.shape[1]
    n_dp = width // share
    vectors = (bias_q, bias_v, bias_out, gain_attn, shift_attn, bias_down, gain_ffn, shift_ffn)
    by_links = n_dp == 16 and share % 16 == 0
    shares = ff // width
    count = len(vectors) + shares
    row_table = jnp.concatenate(vectors + (bias_up.reshape(shares, share),))
    row_table = lax.optimization_barrier(row_table).astype(BF16)
    part_a = jnp.concatenate([w_qkv[0], w_out[0]], axis=1).astype(BF16)
    part_up, part_down = w_up[0].astype(BF16), w_down[0].astype(BF16)
    grid = Grid() if by_links else None
    place = jnp.stack([grid.core, grid.y, grid.pair, grid.low]) if by_links else jnp.zeros((4,), jnp.int32)
    micro = jnp.arange(6, dtype=jnp.int32) % 3
    micro = jnp.where(jnp.arange(6) < 3, micro - section, micro - 1 + section)
    picked = jnp.clip(micro, 0, 1)[:, None]
    run = (micro[:, None] == picked).astype(jnp.int32)
    first = picked == 0
    here = jnp.concatenate([section[None].astype(jnp.int32), place])
    steps = jnp.concatenate(
        [
            run,
            picked,
            jnp.broadcast_to(here[None, :1], (6, 1)),
            jnp.where(first, bucket[:1], bucket[1:]),
            jnp.where(first, lengths[:1], lengths[1:]),
            jnp.broadcast_to(here[None, 1:], (6, 4)),
        ],
        axis=1,
    )
    if by_links:
        padded = jnp.pad(row_table, ((0, share - count), (0, LANES - share)))
        part_a = jnp.concatenate([part_a, padded], axis=1)
        got_a, got_up = grid.swap_near(part_a), grid.swap_near(part_up)
        down_other = grid.swap_y(part_down)
        ended = (got_a, got_up, down_other, steps)
        near_a, near_up = jnp.stack([part_a, got_a]), jnp.stack([part_up, got_up])

        near_a, both_down = after(ended, near_a, jnp.stack([part_down, down_other]))
        middle_a, got_down = grid.swap_middle(near_a), grid.swap_near(both_down)
        near_a_y = grid.swap_y(near_a)
        ended = (middle_a, got_down, near_a_y)
        near_down = jnp.stack([part_down, got_down[0]])
        near_down_y = jnp.stack([down_other, got_down[1]])

        middle_a, near_up = after(ended, middle_a, near_up)
        out_a, middle_up = grid.send_out(middle_a), grid.swap_middle(near_up)
        near_up_y = grid.swap_y(near_up)
        ended = (out_a, middle_up, near_up_y)
        far_a = jnp.where(grid.is_middle, middle_a, out_a)

        middle_up, near_down, far_a, near_a, near_a_y = after(
            ended, middle_up, near_down, far_a, near_a, near_a_y
        )
        out_up, middle_down = grid.send_out(middle_up), grid.swap_middle(near_down)
        far_a_y = grid.swap_y(far_a)
        near_a_c, near_a_yc = grid.swap_core(near_a), grid.swap_core(near_a_y)
        ended = (out_up, middle_down, far_a_y, near_a_c, near_a_yc)
        far_up = jnp.where(grid.is_middle, middle_up, out_up)

        middle_down, near_down_y, far_up, far_a, far_a_y, near_up, near_up_y, near_down = after(
            ended, middle_down, near_down_y, far_up, far_a, far_a_y, near_up, near_up_y, near_down
        )
        out_down, middle_down_y = grid.send_out(middle_down), grid.swap_middle(near_down_y)
        far_up_y = grid.swap_y(far_up)
        far_a_c, far_a_yc = grid.swap_core(far_a), grid.swap_core(far_a_y)
        near_up_c, near_up_yc = grid.swap_core(near_up), grid.swap_core(near_up_y)
        near_down_c, near_down_yc = grid.swap_core(near_down), grid.swap_core(near_down_y)
        ended = (out_down, middle_down_y, far_up_y, far_a_c, far_a_yc)
        ended += (near_up_c, near_up_yc, near_down_c, near_down_yc)
        far_down = jnp.where(grid.is_middle, middle_down, out_down)
        pieces_a = (near_a, far_a, near_a_y, far_a_y, near_a_c, far_a_c, near_a_yc, far_a_yc)
        table = grid.ordered([piece[:, :, 4 * width :] for piece in pieces_a])
        table = table[:, :count, :share]
    else:
        w_a, full_up, full_down = (
            lax.all_gather(part, "dp", axis=0, tiled=True) for part in (part_a, part_up, part_down)
        )
        table = lax.all_gather(row_table[None], "dp", axis=0, tiled=True)
    table = table.astype(F32).transpose(1, 0, 2)
    rows = table[:8].reshape(8, width)
    small = jnp.concatenate(
        [rows[:1], jnp.zeros((1, width), F32), rows[1:], jnp.zeros((7, width), F32)]
    )
    full_bias_up = table[8:].transpose(1, 0, 2).reshape(1, ff)

    none = jnp.zeros((ROWS, width), BF16)

    def ahead(step, received, held=None):
        attn_held, ffn_held = (None, None) if held is None else held
        attn = forward_attn(step, steps, tokens, received, w_a, small, attn_held)
        return attn, forward_ffn(
            step, steps, full_up, full_down, small, full_bias_up, attn[2], attn[4], ffn_held
        )

    def back_ffn(step, upstream, kept, held=None, far=False):
        return ffn_back(
            3 + step, steps, cotangent[min(step, 1)], upstream, full_up, full_down, small, *kept, held, far
        )

    if by_links:
        middle_down_y, far_up, far_up_y, far_down = after(
            ended, middle_down_y, far_up, far_up_y, far_down
        )
        out_down_y = grid.send_out(middle_down_y)
        far_up_c, far_up_yc = grid.swap_core(far_up), grid.swap_core(far_up_y)
        far_down_c = grid.swap_core(far_down)
        first, *others = pieces_a
        pieces = (
            (tie(first, far_up_c, far_up_yc, far_down_c), *others),
            (near_up, far_up, near_up_y, far_up_y, near_up_c, far_up_c, near_up_yc, far_up_yc),
        )
        made = forward_first(0, steps, tokens, none, small, full_bias_up, pieces)
        attn, (d_act, act, x, context, hid, far_act, w_a, full_up) = made[:6], made[6:]
        far_down_y = jnp.where(grid.is_middle, middle_down_y, tie(out_down_y, d_act))
        pieces = (near_down, far_down, near_down_y, far_down_y, near_down_c, far_down_c)
        pieces += (near_down_yc, grid.swap_core(far_down_y))
        *end, full_down = forward_down(0, steps, pieces, small, attn[2], act)
        outer = ((*attn, x, context), (d_act, *end, far_act, hid))
    else:
        outer = ahead(0, none)
    got = passed_along(outer[1][3], "section", 1)
    middle = ahead(1, got)
    got = passed_along(middle[1][3], "section", 1)
    back_outer = back_ffn(0, none, middle)
    back_attn_outer = attn_back(3, steps, w_a, back_outer[2], back_outer[0], middle[0])
    sent = passed_along(back_attn_outer[0], "section", -1)
    outer = ahead(2, got, outer)
    back_middle = back_ffn(1, sent, outer, far=by_links)
    back_attn_middle = attn_back(
        4, steps, w_a, back_middle[2], back_middle[0], outer[0], far=by_links
    )
    sent = passed_along(back_attn_middle[0], "section", -1)
    back_outer = back_ffn(2, sent, middle, back_outer)

    def last_attn_back(steps):
        return attn_back(5, steps, w_a, back_outer[2], back_outer[0], middle_attn, back_attn_outer)

    middle_attn = middle[0]
    x, context = zip(outer[0][6:], middle[0][6:])
    hid = outer[1][5], middle[1][5]
    act, outputs = (outer[1][4], middle[1][4]), (outer[1][3], middle[1][3])
    sums_ffn = back_middle[1], back_outer[1]
    d_ffn, d_pre = zip(back_middle[3:5], back_outer[3:5])
    d_branch = back_attn_middle[3] if by_links else back_middle[0], back_outer[0]

    def by_micro(one, two):
        first = section == 0
        return jnp.stack([jnp.where(first, one, two), jnp.where(first, two, one)])[None]

    if by_links:
        def plus(one, two):
            return one.astype(F32) + two.astype(F32)

        mine_down, theirs = grad_call(
            grad_down_body,
            "grad_down",
            place,
            (d_ffn[0], *act),
            (d_ffn[1],),
            ff // 16,
            width,
            (1, 4, 4),
            fetch=False,
        )
        got_down = grid.swap_core(theirs)
        mine_up, theirs = grad_call(
            grad_up_body,
            "grad_up",
            place,
            (tie(hid[0], mine_down), hid[1], d_pre[0]),
            (d_pre[1],),
            share,
            ff,
            (1, 1, 4),
            fetch=False,
        )

        def low_sum(*parts):
            return sum(part.astype(F32) for part in parts).astype(BF16)

        down_parts = [(mine_down[i, 1], got_down[i, 1]) for i in range(2)]
        out, out_y = (low_sum(*parts) for parts in down_parts)
        out, out_y, theirs, table = after((got_down, mine_up), out, out_y, theirs, steps)
        got_out, got_up = grid.send_in(out), grid.swap_core(theirs)
        last = last_attn_back(table)
        (got_out,) = after((last[1],), got_out)

        out_y, early_up, early_got = after((got_out,), out_y, mine_up, got_up)
        away_up, away_near = (low_sum(early_up[1, i], early_got[1, i]) for i in (1, 0))
        middle = low_sum(out, got_out)
        far_up_y, got_out_y = grid.swap_y(away_up), grid.send_in(out_y)
        got_middle = grid.swap_middle(middle)
        up_home = low_sum(early_up[0, 1], early_got[0, 1])
        (first_x,) = after((middle, away_up, away_near, up_home), x[0])
    else:
        last = last_attn_back(steps)
    input_grads, sums_attn, d_qkv = zip(back_attn_middle[:3], last)
    total = sums_ffn[0] + sums_ffn[1]
    total_attn = sums_attn[0] + sums_attn[1]
    vector_rows = jnp.stack(
        [
            total_attn[0],
            total_attn[1],
            total[2, width : 2 * width],
            total[1, 3 * width :],
            total[2, :width],
            total[1, :width],
            total[1, width : 2 * width],
            total[1, 2 * width : 3 * width],
        ]
    ).reshape(8, n_dp, share)
    table = jnp.concatenate(
        [vector_rows.transpose(1, 0, 2), total[0].reshape(n_dp, shares, share)], axis=1
    )
    if by_links:
        mine_a, theirs = grad_call(
            grad_attn_body,
            "grad_attn",
            place,
            (first_x, x[1], d_qkv[0], *context, d_branch[0]),
            (d_qkv[1], d_branch[1], *sums_ffn, *sums_attn),
            share,
            4 * width + LANES,
            (1, 1, 3, 1, 1, 1),
        )
        far_up_y, got_out_y, got_middle = after((mine_a,), far_up_y, got_out_y, got_middle)
        theirs, away_up = after((far_up_y, got_out_y, got_middle), theirs, away_near)
        got_a, near_up_y = grid.swap_core(theirs), grid.swap_y(away_up)
        far_up = low_sum(up_home, far_up_y)
        got_out_up = grid.send_in(far_up)
        got_middle_y = grid.swap_middle(low_sum(out_y, got_out_y))
        mine_up, got_up, mine_down, got_down = after(
            (got_a,), mine_up, got_up, mine_down, got_down
        )
        away_a, away_a_near = (low_sum(mine_a[1, i], got_a[1, i]) for i in (1, 0))
        got_out_up, got_middle_y, near_up_y = after(
            (away_a, away_a_near), got_out_up, got_middle_y, near_up_y
        )

        def down_sum(at, i):
            parts = (mine_down[i, 0], got_down[i, 0], (got_middle, got_middle_y)[i])
            return sum(grid.picked(part, at, 0).astype(F32) for part in parts)

        def up_sum(at):
            parts = (mine_up[0, 0], got_up[0, 0], near_up_y, got_middle_up)
            return sum(grid.picked(part, at, 0).astype(F32) for part in parts)

        def a_sum(at):
            parts = (mine_a[0, 0], got_a[0, 0], near_a_y)
            return sum(grid.picked(part, at, 0).astype(F32) for part in parts)

        (away_a,) = after((got_out_up, got_middle_y, near_up_y), away_a)
        far_a_y = grid.swap_y(away_a)
        got_middle_up = grid.swap_middle(low_sum(far_up, got_out_up))
        away = [down_sum(1 - grid.low, i).astype(BF16) for i in range(2)]
        got_near_down = grid.swap_near(jnp.stack(away))

        (away_a,) = after((far_a_y, got_middle_up, got_near_down), away_a_near)
        parts = (mine_a[0, 1], got_a[0, 1], far_a_y)
        one, other = (
            low_sum(*(grid.picked(part, at, 0) for part in parts)) for at in (grid.low, 1 - grid.low)
        )
        got_in, got_over, got_skip = grid.send_in(one), grid.swap_middle(one), grid.skip_in(other)
        near_a_y = grid.swap_y(away_a)
        both_down = [down_sum(grid.low, i) + got_near_down[i].astype(F32) for i in range(2)]
        away_down, away_up = both_down[1].astype(BF16), up_sum(1 - grid.low).astype(BF16)
        got_in, got_over, got_skip, near_a_y = after(
            (away_down, away_up), got_in, got_over, got_skip, near_a_y
        )

        away_down, away_up = after((got_in, got_over, got_skip, near_a_y), away_down, away_up)
        away = a_sum(1 - grid.low) + got_over.astype(F32) + got_skip.astype(F32)
        outputs, input_grads = after((got_in, got_over), outputs, input_grads)
        got_near_a = grid.swap_near(away.astype(BF16))
        got_middle_a = grid.swap_middle(low_sum(other, got_in))
        got_near_up, got_down_y = grid.swap_near(away_up), grid.swap_y(away_down)
        g_down = both_down[0] + got_down_y.astype(F32)
        g_up = up_sum(grid.low) + got_near_up.astype(F32)
        g_a = a_sum(grid.low) + got_near_a.astype(F32) + got_middle_a.astype(F32)
        table = g_a[:count, 4 * width : 4 * width + share]
    else:

        def summed(values):
            return lax.psum_scatter(values, "dp", scatter_dimension=0, tiled=True).astype(F32)

        g_down = summed(weight_grad(act, d_ffn))
        g_up = summed(weight_grad(hid, d_pre))
        g_qkv = weight_grad(x, d_qkv)
        g_out = weight_grad(context, d_branch)
        g_a = summed(jnp.concatenate([g_qkv, g_out], axis=1))
        table = summed(table)[0]
    hidden_states, input_grads = by_micro(*outputs), by_micro(*input_grads)
    g_down, g_up = g_down[None], g_up[None]
    g_qkv, g_out = g_a[None, :, : 3 * width], g_a[None, :, 3 * width : 4 * width]
    g_vectors = [table[i : i + 1] for i in range(8)]
    g_bias_up = table[8:].reshape(1, ff // n_dp)
    (
        g_bias_q,
        g_bias_v,
        g_bias_out,
        g_gain_attn,
        g_shift_attn,
        g_bias_down,
        g_gain_ffn,
        g_shift_ffn,
    ) = g_vectors
    return (
        hidden_states,
        input_grads,
        g_qkv,
        g_bias_q,
        g_bias_v,
        g_out,
        g_bias_out,
        g_gain_attn,
        g_shift_attn,
        g_up,
        g_bias_up,
        g_down,
        g_bias_down,
        g_gain_ffn,
        g_shift_ffn,
    )


def solution(mesh):
    matrix = P("section", "dp", None)
    vector = P("section", "dp")
    rows = P(None, "dp", None)
    outs = P("section", None, "dp", None)
    params = (
        matrix,
        vector,
        vector,
        matrix,
        vector,
        vector,
        vector,
        matrix,
        vector,
        matrix,
        vector,
        vector,
        vector,
    )
    return jax.shard_map(
        on_device,
        mesh=mesh,
        in_specs=(rows, rows, P(None, "dp"), P(None, "dp")) + params,
        out_specs=(outs, outs) + params,
        check_vma=False,
    )
```

```python
import functools

import jax
import jax.numpy as jnp
from jax import lax
from jax.experimental import pallas as pl
from jax.experimental.pallas import tpu as pltpu
from jax.sharding import PartitionSpec as P

HEADS = 12
SEGMENT = 64
PAIRS = 6
ROWS = 384
EPSILON = 1e-06
MASKED = -1000000000.0
LANES = 128
FF_TILE = 1024
LIMIT = 4
LIMIT_GRAD = 6
VMEM_LIMIT = 60 * 1024 * 1024
F32 = jnp.float32
BF16 = jnp.bfloat16

BIAS_Q, BIAS_K, BIAS_V, BIAS_OUT, GAIN_ATTN, SHIFT_ATTN, BIAS_DOWN, GAIN_FFN, SHIFT_FFN = range(9)
RUN, MICRO, SECTION, BUCKET, LENGTHS = range(5)
CORE, Y, PAIR, LOW = range(LENGTHS + PAIRS, LENGTHS + PAIRS + 4)

ANY = pl.BlockSpec(memory_space=pl.ANY)
WHOLE = pl.BlockSpec(memory_space=pltpu.VMEM)
SCALARS = pl.BlockSpec(memory_space=pltpu.SMEM)
FAR = pl.BlockSpec(memory_space=pltpu.HBM)
COST = pl.CostEstimate(flops=1, bytes_accessed=1, transcendentals=0)


def in_hbm(arrays):
    return [pltpu.with_memory_space_constraint(array, pltpu.HBM) for array in arrays]


def dot_nn(a, b):
    return lax.dot_general(a, b, (((1,), (0,)), ((), ())), preferred_element_type=F32)


def dot_nt(a, b):
    return lax.dot_general(a, b, (((1,), (1,)), ((), ())), preferred_element_type=F32)


def dot_tn(a, b):
    return lax.dot_general(a, b, (((0,), (0,)), ((), ())), preferred_element_type=F32)


class Row:
    def __init__(self, table, row):
        self.table, self.row = table, row

    def __getitem__(self, at):
        return self.table[self.row, at]


def fold(values):
    rows, n = values.shape
    return jnp.sum(values.reshape(rows // 8, 8, n), axis=0)


def write_bias(info, bias, block, count):
    segment = (info[BUCKET] + 1) * SEGMENT
    per_block = jnp.where(info[BUCKET] == 0, block // SEGMENT, 1)
    k_row = lax.broadcasted_iota(jnp.int32, (block, block), 0)
    q_row = lax.broadcasted_iota(jnp.int32, (block, block), 1)

    def pair_of(row):
        return (row >= segment).astype(jnp.int32) + (row >= 2 * segment).astype(jnp.int32)

    k_pair = pair_of(k_row)
    same = k_pair == pair_of(q_row)
    position = k_row - k_pair * segment
    for at in range(count):
        valid = [
            jnp.minimum(info[LENGTHS + jnp.minimum(at * per_block + i, PAIRS - 1)], segment)
            for i in range(3)
        ]
        length = jnp.where(k_pair == 0, valid[0], jnp.where(k_pair == 1, valid[1], valid[2]))
        bias[at, :block, :block] = jnp.where(same & (position < length), 0.0, MASKED)


def half_masks():
    lane = lax.broadcasted_iota(jnp.int32, (1, LANES), 1)
    low = (lane < LANES // 2).astype(F32)
    return low.astype(BF16), (1.0 - low).astype(BF16)


def by_block(info, body):
    @pl.when(info[BUCKET] == 1)
    def _():
        body(2 * SEGMENT, ROWS // (2 * SEGMENT))

    @pl.when(info[BUCKET] != 1)
    def _():
        body(3 * SEGMENT, ROWS // (3 * SEGMENT))


def attention(info, qkv, context, lse, bias):
    width = context.shape[1]
    low, high = half_masks()

    def both_heads(values):
        return jnp.concatenate([values * low, values * high], axis=0)

    def body(block, count):
        write_bias(info, bias, block, count)

        def pair_step(pair, carry):
            at_q = pl.multiple_of(pair * LANES, LANES)
            at_k = pl.multiple_of(width + pair * LANES, LANES)
            at_v = pl.multiple_of(2 * width + pair * LANES, LANES)
            rows = [pl.ds(at * block, block) for at in range(count)]
            q = [qkv[r, pl.ds(at_q, LANES)] for r in rows]
            k = [both_heads(qkv[r, pl.ds(at_k, LANES)]) for r in rows]
            v = [both_heads(qkv[r, pl.ds(at_v, LANES)]) for r in rows]
            masks = [bias[at, :block, :block] for at in range(count)]
            scores = [
                dot_nt(k[at], q[at]).reshape(2, block, block) + masks[at][None]
                for at in range(count)
            ]
            tops = [jnp.max(x, axis=1, keepdims=True) for x in scores]
            weights = [jnp.exp(x - top) for x, top in zip(scores, tops)]
            totals = [jnp.sum(x, axis=1, keepdims=True) for x in weights]
            probs = [
                (x * (1.0 / total)).astype(BF16).reshape(2 * block, block)
                for x, total in zip(weights, totals)
            ]
            parts = [dot_tn(x, values) for x, values in zip(probs, v)]
            for at in range(count):
                ends = tops[at] + jnp.log(totals[at])
                for half in range(2):
                    lse[2 * pair + half, at : at + 1, :block] = ends[half]
                context[rows[at], pl.ds(at_q, LANES)] = parts[at].astype(BF16)
            return carry

        def steps(i, carry):
            for sub in range(3):
                pair_step(i * 3 + sub, carry)
            return carry

        lax.fori_loop(0, HEADS // 2 // 3, steps, 0)

    by_block(info, body)


def attention_back(info, qkv, d_context, lse, bias, d_qkv):
    width = d_context.shape[1]
    low, high = half_masks()
    scale = (width // HEADS) ** -0.5

    def both_heads(values):
        return jnp.concatenate([values * low, values * high], axis=0)

    def flat(values):
        return values.astype(BF16).reshape(2 * values.shape[1], values.shape[2])

    def body(block, count):
        write_bias(info, bias, block, count)

        def pair_step(pair, carry):
            at_q = pl.multiple_of(pair * LANES, LANES)
            at_k = pl.multiple_of(width + pair * LANES, LANES)
            at_v = pl.multiple_of(2 * width + pair * LANES, LANES)
            is_low = lax.broadcasted_iota(jnp.int32, (block, LANES), 1) < LANES // 2
            rows = [pl.ds(at * block, block) for at in range(count)]
            q = [qkv[r, pl.ds(at_q, LANES)] for r in rows]
            k = [both_heads(qkv[r, pl.ds(at_k, LANES)]) for r in rows]
            v = [both_heads(qkv[r, pl.ds(at_v, LANES)]) for r in rows]
            d_out = [d_context[r, pl.ds(at_q, LANES)] for r in rows]
            masks = [bias[at, :block, :block] for at in range(count)]
            scores = [
                dot_nt(k[at], q[at]).reshape(2, block, block) + masks[at][None]
                for at in range(count)
            ]
            d_probs = [dot_nt(v[at], d_out[at]).reshape(2, block, block) for at in range(count)]
            ends = [
                jnp.stack([lse[2 * pair + half, at : at + 1, :block] for half in range(2)])
                for at in range(count)
            ]
            probs = [jnp.exp(x - end) for x, end in zip(scores, ends)]
            d_v = [dot_nn(flat(x), d_out[at]) for at, x in enumerate(probs)]
            inner = [jnp.sum(x * d_x, axis=1, keepdims=True) for x, d_x in zip(probs, d_probs)]
            d_scores = [
                flat(x * (d_x - total)) for x, d_x, total in zip(probs, d_probs, inner)
            ]
            d_k = [dot_nn(x, q[at]) for at, x in enumerate(d_scores)]
            d_q = [dot_tn(x, k[at]) for at, x in enumerate(d_scores)]
            for at, r in enumerate(rows):
                d_qkv[r, pl.ds(at_q, LANES)] = (d_q[at] * scale).astype(BF16)
                for to, part in ((at_k, d_k[at]), (at_v, d_v[at])):
                    part = jnp.where(is_low, part[:block], part[block:])
                    d_qkv[r, pl.ds(to, LANES)] = part.astype(BF16)
            return carry

        def steps(i, carry):
            for sub in range(3):
                pair_step(i * 3 + sub, carry)
            return carry

        lax.fori_loop(0, HEADS // 2 // 3, steps, 0)

    by_block(info, body)


def norm(values):
    centered = values - jnp.mean(values, axis=-1, keepdims=True)
    inverse = lax.rsqrt(jnp.mean(centered * centered, axis=-1, keepdims=True) + EPSILON)
    return centered * inverse, inverse


def norm_back(upstream, normed, inverse, gain):
    scaled = upstream * gain
    return inverse * (
        scaled
        - jnp.mean(scaled, axis=-1, keepdims=True)
        - normed * jnp.mean(scaled * normed, axis=-1, keepdims=True)
    )


CHUNK = 64


def by_rows(step, carry=0):
    def body(i, carry):
        return step(pl.ds(pl.multiple_of(i * CHUNK, CHUNK), CHUNK), carry)

    return lax.fori_loop(0, ROWS // CHUNK, body, carry)


def carry_over(src, dst):
    if src.shape[0] == ROWS:

        def step(rows, carry):
            dst[rows, :] = src[rows, :]
            return carry

        by_rows(step)
    else:
        dst[...] = src[...]


def join_copies(info, pieces, out, sems):
    core, y, pair, low = (info[i] for i in (CORE, Y, PAIR, LOW))
    near = (pair * 2 + low, pair * 2 + 1 - low)
    far = (jnp.where(pair == 0, 2, 1), jnp.where(pair == 0, 3, 0))
    share = pieces[0].shape[1]
    copies = []
    for index, piece in enumerate(pieces):
        dc, dy, away = index // 4, (index // 2) % 2, index % 2
        for i, z in enumerate(far if away else near):
            at = z * 4 + jnp.bitwise_xor(y, dy) * 2 + jnp.bitwise_xor(core, dc)
            rows = pl.ds(pl.multiple_of(at * share, 16), share)
            copies.append(pltpu.make_async_copy(piece.at[i], out.at[rows, :], sems.at[len(copies)]))
    return copies


def kernel_call(body, name, step, ins, out_shapes, held, scratch, limit, far=(), pieces=(), far_ins=()):
    held = [] if held is None else list(held)
    given = len(ins) - 1
    count = len(out_shapes)
    spec = [FAR if i in far else WHOLE for i in range(count)]

    def kernel(table, *refs):
        info = Row(table, step)
        blocks, refs = refs[: 8 * len(pieces)], refs[8 * len(pieces) :]
        kept = refs[given : given + len(held)]
        outs = refs[given + len(held) :][:count]
        own = refs[given + len(held) + count :]
        joins = [
            join_copies(
                info, blocks[8 * i : 8 * i + 8], outs[count - len(pieces) + i], own[len(scratch)].at[i]
            )
            for i in range(len(pieces))
        ]
        for copy in sum(joins, []):
            copy.start()

        def wait_for(join):
            def wait():
                for copy in join:
                    copy.wait()

            return wait

        waits = [wait_for(join) for join in joins]

        @pl.when(info[RUN] == 1)
        def _():
            copies = []

            def flush(index, ref):
                copy = pltpu.make_async_copy(ref, outs[index], own[-1].at[len(copies)])
                copy.start()
                copies.append(copy)

            near = [out for i, out in enumerate(outs) if i not in far]
            given_waits = (waits,) if pieces else ()
            body(info, flush, *given_waits, *refs[:given], *near, *own[: len(scratch)])
            for copy in copies:
                copy.wait()

        if held or pieces:

            @pl.when(info[RUN] != 1)
            def _():
                for wait in waits:
                    wait()
                for i, (src, dst) in enumerate(zip(kept, outs)):
                    if i not in far:
                        carry_over(src, dst)

    return pl.pallas_call(
        kernel,
        in_specs=[SCALARS]
        + [FAR] * (8 * len(pieces))
        + [FAR if i in far_ins else WHOLE for i in range(given)]
        + spec[: len(held)],
        out_specs=spec,
        out_shape=[
            pltpu.HBM(shape, kind) if i in far else jax.ShapeDtypeStruct(shape, kind)
            for i, (shape, kind) in enumerate(out_shapes)
        ],
        input_output_aliases={1 + given + i: i for i in range(len(held))},
        scratch_shapes=scratch
        + ([pltpu.SemaphoreType.DMA((len(pieces), 16))] if pieces else [])
        + ([pltpu.SemaphoreType.DMA((len(far),))] if far else []),
        compiler_params=pltpu.CompilerParams(vmem_limit_bytes=int(limit * 1024 * 1024)),
        cost_estimate=COST,
        name=name,
    )(
        ins[0],
        *in_hbm([piece for group in pieces for piece in group]),
        *(in_hbm([x])[0] if i in far_ins else x for i, x in enumerate(ins[1:])),
        *(in_hbm([x])[0] if i in far else x for i, x in enumerate(held)),
    )


def forward_attn_body(
    info, flush, tok, rec, w_a, small, qkv, lse, n1, inv1, hid, n1_low, x, context, acc, bias, sem, ready=None
):
    width = x.shape[1]

    @pl.when(info[SECTION] == 0)
    def _():
        copy = pltpu.make_async_copy(tok.at[info[MICRO]], x, sem)
        copy.start()
        copy.wait()

    @pl.when(info[SECTION] != 0)
    def _():
        x[...] = rec[...]

    flush(6, x)
    if ready is not None:
        ready()
    for j, (row, factor) in enumerate(
        ((BIAS_Q, (width // HEADS) ** -0.5), (BIAS_K, 1.0), (BIAS_V, 1.0))
    ):
        cols = slice(j * width, (j + 1) * width)
        part = dot_nn(x[...], w_a[:, cols]) + small[row : row + 1, :]
        qkv[:, cols] = (part * factor).astype(BF16)
    attention(info, qkv, context, lse, bias)
    flush(7, context)
    acc[...] = dot_nn(context[...], w_a[:, 3 * width : 4 * width])

    def norm_one(rows, carry):
        total = x[rows, :].astype(F32) + acc[rows, :]
        normed, inverse = norm(total + small[BIAS_OUT : BIAS_OUT + 1, :])
        n1[rows, :] = normed
        n1_low[rows, :] = normed.astype(BF16)
        inv1[rows, :] = jnp.broadcast_to(inverse, (CHUNK, LANES))
        hidden = normed * small[GAIN_ATTN : GAIN_ATTN + 1, :]
        hid[rows, :] = (hidden + small[SHIFT_ATTN : SHIFT_ATTN + 1, :]).astype(BF16)
        return carry

    by_rows(norm_one)


def up_tile(j, hid, w_up, bias_up, act, d_act):
    cols = slice(j * FF_TILE, (j + 1) * FF_TILE)
    pre = dot_nn(hid[...], w_up[:, cols]) + bias_up[:, cols]
    below = 0.5 * (1.0 + lax.erf(pre * 0.7071067811865476))
    density = jnp.exp(pre * pre * -0.5) * 0.3989422804014327
    act[:, cols] = (pre * below).astype(BF16)
    d_act[:, cols] = (below + pre * density).astype(BF16)


def down_tile(j, act, w_down, acc):
    cols = slice(j * FF_TILE, (j + 1) * FF_TILE)
    part = dot_nn(act[:, cols], w_down[cols, :])
    acc[...] = part if j == 0 else acc[...] + part


def layer_end(small, n1, n2, inv2, out, acc):
    def norm_two(rows, carry):
        hidden = n1[rows, :] * small[GAIN_ATTN : GAIN_ATTN + 1, :]
        hidden = hidden + small[SHIFT_ATTN : SHIFT_ATTN + 1, :]
        normed, inverse = norm(hidden + acc[rows, :] + small[BIAS_DOWN : BIAS_DOWN + 1, :])
        n2[rows, :] = normed.astype(BF16)
        inv2[rows, :] = jnp.broadcast_to(inverse, (CHUNK, LANES))
        out[rows, :] = (
            normed * small[GAIN_FFN : GAIN_FFN + 1, :] + small[SHIFT_FFN : SHIFT_FFN + 1, :]
        ).astype(BF16)
        return carry

    by_rows(norm_two)


def forward_ffn_body(
    info, flush, w_up, w_down, small, bias_up, n1, hid, d_act, n2, inv2, out, act, acc
):
    tiles = act.shape[1] // FF_TILE
    flush(5, hid)
    up_tile(0, hid, w_up, bias_up, act, d_act)
    for j in range(1, tiles):
        up_tile(j, hid, w_up, bias_up, act, d_act)
        down_tile(j - 1, act, w_down, acc)
    flush(4, act)
    down_tile(tiles - 1, act, w_down, acc)
    layer_end(small, n1, n2, inv2, out, acc)


def forward_down_body(info, flush, w_down, small, n1, act, n2, inv2, out, acc):
    for j in range(act.shape[1] // FF_TILE):
        down_tile(j, act, w_down, acc)
    layer_end(small, n1, n2, inv2, out, acc)


def bias_scratch():
    return pltpu.VMEM((3, 3 * SEGMENT, 3 * SEGMENT), F32)


def joined_shape(pieces):
    share, n = pieces[0].shape[-2:]
    return (((16 * share, n), BF16),)


def forward_attn(step, info, tokens, received, w_a, small, held=None):
    width = small.shape[1]
    rows = ((ROWS, width), BF16)
    return kernel_call(
        forward_attn_body,
        "forward_attn",
        step,
        (info, tokens, received, w_a, small),
        attn_shapes(width) + (rows, rows),
        held,
        [pltpu.VMEM(*rows)] * 2
        + [pltpu.VMEM((ROWS, width), F32), bias_scratch(), pltpu.SemaphoreType.DMA],
        LIMIT + 1.2,
        far=(6, 7),
        far_ins=(0,),
    )


def attn_shapes(width):
    rows = ((ROWS, width), BF16)
    return (
        ((ROWS, 3 * width), BF16),
        ((HEADS, 8, 256), F32),
        ((ROWS, width), F32),
        ((ROWS, LANES), F32),
        rows,
        rows,
    )


def forward_first_body(info, flush, waits, tok, rec, small, bias_up, *refs):
    attn_refs, (d_act, act, w_a, w_up), (x, context, acc, bias, sem) = refs[:6], refs[6:10], refs[10:]

    def flush_attn(index, ref):
        flush(index + 2, ref)

    forward_attn_body(
        info, flush_attn, tok, rec, w_a, small, *attn_refs, x, context, acc, bias, sem, waits[0]
    )
    hid = attn_refs[4]
    flush(10, hid)
    waits[1]()
    for j in range(act.shape[1] // FF_TILE):
        up_tile(j, hid, w_up, bias_up, act, d_act)
    flush(11, act)


def forward_first(step, info, tokens, received, small, bias_up, pieces):
    width, ff = small.shape[1], bias_up.shape[1]
    rows, wide = ((ROWS, width), BF16), ((ROWS, ff), BF16)
    return kernel_call(
        forward_first_body,
        "forward_first",
        step,
        (info, tokens, received, small, bias_up),
        attn_shapes(width)
        + (wide, wide, rows, rows, rows, wide)
        + joined_shape(pieces[0])
        + joined_shape(pieces[1]),
        None,
        [pltpu.VMEM(*rows)] * 2
        + [pltpu.VMEM((ROWS, width), F32), bias_scratch(), pltpu.SemaphoreType.DMA],
        LIMIT + 1.2,
        far=(8, 9, 10, 11),
        pieces=pieces,
        far_ins=(0,),
    )


def forward_ffn(step, info, w_up, w_down, small, bias_up, n1, hid, held=None):
    width, ff = small.shape[1], bias_up.shape[1]
    rows, wide = ((ROWS, width), BF16), ((ROWS, ff), BF16)
    return kernel_call(
        forward_ffn_body,
        "forward_ffn",
        step,
        (info, w_up, w_down, small, bias_up, n1, hid),
        (wide, rows, ((ROWS, LANES), F32), rows, wide, rows),
        held,
        [pltpu.VMEM((ROWS, ff), BF16), pltpu.VMEM((ROWS, width), F32)],
        LIMIT + 2.4,
        far=(4, 5),
    )


def forward_down(step, info, pieces, small, n1, act):
    width = small.shape[1]

    def body(info, flush, waits, small, n1, act, n2, inv2, out, w_down, acc):
        waits[0]()
        forward_down_body(info, flush, w_down, small, n1, act, n2, inv2, out, acc)

    shapes = (((ROWS, width), BF16), ((ROWS, LANES), F32), ((ROWS, width), BF16))
    return kernel_call(
        body,
        "forward_down",
        step,
        (info, small, n1, act),
        shapes + joined_shape(pieces),
        None,
        [pltpu.VMEM((ROWS, width), F32)],
        LIMIT,
        pieces=(pieces,),
    )


def norm_back_rows(upstream, normed, inverse, gain, grad, low):
    zeros = jnp.zeros((8, grad.shape[1]), F32)

    def step(rows, carry):
        up, nm = upstream(rows), normed(rows)
        values = norm_back(up, nm, inverse(rows), gain)
        grad[rows, :] = values
        rounded = values.astype(BF16)
        low(rows, rounded)
        return (
            carry[0] + fold(up),
            carry[1] + fold(up * nm),
            carry[2] + fold(rounded.astype(F32)),
        )

    sums = by_rows(step, (zeros, zeros, zeros))
    return [jnp.sum(part, axis=0, keepdims=True) for part in sums]


def ffn_back_body(
    far,
    info,
    flush,
    cot,
    rec,
    w_up,
    w_down,
    small,
    n1,
    inv1,
    d_act,
    n2,
    inv2,
    d_branch,
    sums,
    d_first,
    d_ffn,
    d_pre,
    acc,
):
    if not far:

        def flush(index, ref):
            pass

    width = rec.shape[1]
    ff = d_pre.shape[1]
    tiles = ff // FF_TILE

    last = info[SECTION] == 1

    def upstream(rows):
        return jnp.where(last, cot[rows, :], rec[rows, :]).astype(F32)

    def keep_ffn(rows, low):
        d_ffn[rows, :] = low

    sum_g, sum_gn, sum_d = norm_back_rows(
        upstream,
        lambda rows: n2[rows, :].astype(F32),
        lambda rows: inv2[rows, :1],
        small[GAIN_FFN : GAIN_FFN + 1, :],
        acc,
        keep_ffn,
    )
    flush(3, d_ffn)
    sums[1:2, :width] = sum_d
    sums[1:2, width : 2 * width] = sum_gn
    sums[1:2, 2 * width : 3 * width] = sum_g

    def first(j):
        cols = slice(j * FF_TILE, (j + 1) * FF_TILE)
        part = dot_nt(d_ffn[...], w_down[cols, :]) * d_act[:, cols].astype(F32)
        low = part.astype(BF16)
        d_pre[:, cols] = low
        sums[0:1, cols] = jnp.sum(fold(low.astype(F32)), axis=0, keepdims=True)

    def second(j):
        cols = slice(j * FF_TILE, (j + 1) * FF_TILE)
        acc[...] += dot_nt(d_pre[:, cols], w_up[:, cols])

    first(0)
    for j in range(1, tiles):
        first(j)
        second(j - 1)
    flush(4, d_pre)
    second(tiles - 1)

    def keep_branch(rows, low):
        d_branch[rows, :] = low

    sum_g, sum_gn, sum_d = norm_back_rows(
        lambda rows: acc[rows, :],
        lambda rows: n1[rows, :].astype(F32),
        lambda rows: inv1[rows, :1],
        small[GAIN_ATTN : GAIN_ATTN + 1, :],
        d_first,
        keep_branch,
    )
    sums[1:2, 3 * width :] = sum_gn
    sums[2:3, :width] = sum_g
    sums[2:3, width : 2 * width] = sum_d


def ffn_back(step, info, cotangent, received, w_up, w_down, small, attn, ffn, held=None, far=False):
    width, ff = w_up.shape
    rows, wide = ((ROWS, width), BF16), ((ROWS, ff), BF16)
    shapes = (rows, ((8, ff), F32), ((ROWS, width), F32), rows, wide)
    scratch = [pltpu.VMEM(*rows), pltpu.VMEM(*wide)] if far else []
    return kernel_call(
        functools.partial(ffn_back_body, far),
        "ffn_backward",
        step,
        (info, cotangent, received, w_up, w_down, small, attn[5], attn[3], ffn[0], ffn[1], ffn[2]),
        shapes,
        held,
        scratch + [pltpu.VMEM((ROWS, width), F32)],
        LIMIT + (3 if far else 0),
        far=(3, 4) if far else (),
    )


def attn_back_body(
    far, info, flush, w_a, d_first, d_branch, qkv, lse, grads, sums, d_qkv, d_context, bias
):
    if not far:

        def flush(index, ref):
            pass

    flush(3, d_branch)
    width = d_first.shape[1]

    d_context[...] = dot_nt(d_branch[...], w_a[:, 3 * width : 4 * width]).astype(BF16)
    attention_back(info, qkv, d_context, lse, bias, d_qkv)
    flush(2, d_qkv)
    grad = d_first[...] + dot_nt(d_qkv[...], w_a[:, : 3 * width])
    low = grad.astype(BF16)
    grads[...] = low
    for row, at in ((0, 0), (1, 2 * width)):
        sums[row : row + 1, :] = jnp.sum(
            fold(d_qkv[:, at : at + width].astype(F32)), axis=0, keepdims=True
        )


def attn_back(step, info, w_a, d_first, d_branch, attn, held=None, far=False):
    width = d_first.shape[1]
    rows, wide = ((ROWS, width), BF16), ((ROWS, 3 * width), BF16)
    return kernel_call(
        functools.partial(attn_back_body, far),
        "attention_backward",
        step,
        (info, w_a, d_first, d_branch, attn[0], attn[1]),
        (rows, ((8, width), F32), wide) + ((rows,) if far else ()),
        held,
        ([pltpu.VMEM(*wide)] if far else []) + [pltpu.VMEM(*rows), bias_scratch()],
        LIMIT + (1.8 if far else 0),
        far=(2, 3) if far else (),
    )


def split_blocks(values, place, halves, cols, first_z=0):
    share = halves.shape[4]
    core, y, pair = place[0], place[1], place[2]
    for index in range(values.shape[0] // (4 * share)):
        z = first_z + index
        for yy in range(2):
            for cc in range(2):
                at = (index * 4 + yy * 2 + cc) * share
                part = values[at : at + share].astype(BF16)
                to = [jnp.bitwise_xor(core, cc), jnp.bitwise_xor(y, yy), jnp.bitwise_xor(pair, z // 2)]
                halves[(*to, z % 2, slice(None), cols)] = part


def grad_call(body, name, place, far, near, share, n, cuts, fetch=True):
    shape = (2, 2, 2, share, n)
    total = sum(cuts)

    def kernel(place, *refs):
        sources, refs = refs[: len(far)], refs[len(far) :]
        kept, refs = refs[: len(near)], refs[len(near) :]
        if not fetch:
            refs = (*refs[:3], *sources, refs[-1])
        mine_out, theirs_out, halves, *held, sems = refs
        copies = []
        for src, dst, cut in zip(sources, held, cuts) if fetch else ():
            size = src.shape[1] // cut
            group = []
            for i in range(cut):
                cols = slice(i * size, (i + 1) * size)
                sem = sems.at[sum(map(len, copies)) + i]
                group.append(pltpu.make_async_copy(src.at[:, cols], dst.at[:, cols], sem))
            copies.append(group)
        for i in range(max(cuts)):
            for group in copies:
                if i < len(group):
                    group[i].start()
        done = set()

        def wait(index, part=0):
            if fetch and (index, part) not in done:
                done.add((index, part))
                copies[index][part].wait()

        sent = []

        def flush(*at):
            for core, dst in ((1, theirs_out), (0, mine_out)):
                src = halves.at[(core, *at)]
                copy = pltpu.make_async_copy(src, dst.at[at], sems.at[total + len(sent)])
                copy.start()
                sent.append(copy)

        body(place, wait, flush, held, kept, halves)
        for copy in sent:
            copy.wait()

    held = far if fetch else ()
    scratch = [pltpu.VMEM((2, *shape), BF16)] + [pltpu.VMEM(x.shape, x.dtype) for x in held]
    size = sum(x.size * 2 for x in held) + 32 * share * n
    return pl.pallas_call(
        kernel,
        in_specs=[SCALARS] + [FAR if fetch else WHOLE] * len(far) + [WHOLE] * len(near),
        out_specs=[FAR] * 2,
        out_shape=[pltpu.HBM(shape, BF16)] * 2,
        scratch_shapes=scratch + [pltpu.SemaphoreType.DMA((total + 8,))],
        compiler_params=pltpu.CompilerParams(vmem_limit_bytes=size + LIMIT_GRAD * 1024 * 1024),
        cost_estimate=COST,
        name=name,
    )(place, *(in_hbm(far) if fetch else far), *near)


def stacked(one, two, cols=slice(None)):
    return jnp.concatenate([one[:, cols], two[:, cols]], axis=0)


def grad_down_body(place, wait, flush, held, kept, halves):
    d_middle, act, act2 = held
    wait(0)
    right = stacked(d_middle, kept[0])
    rows = 4 * halves.shape[4]
    for z in range(4):
        wait(1, z)
        wait(2, z)
        left = stacked(act, act2, slice(z * rows, (z + 1) * rows))
        split_blocks(dot_tn(left, right), place, halves, slice(None), z)
        if z % 2:
            pair = pl.ds(jnp.bitwise_xor(place[2], z // 2), 1)
            flush(slice(None), pair)


def grad_up_body(place, wait, flush, held, kept, halves):
    hid, hid2, d_middle = held
    wait(0)
    wait(1)
    left = stacked(hid, hid2)
    tile = d_middle.shape[1] // 4
    for i in range(4):
        wait(2, i)
        cols = slice(i * tile, (i + 1) * tile)
        split_blocks(dot_tn(left, stacked(d_middle, kept[0], cols)), place, halves, cols)
        flush(slice(None), slice(None), slice(None), slice(None), cols)


def write_table(place, sums, halves, first):
    share = halves.shape[4]
    width, wide = sums[2].shape[1], sums[0].shape[1]
    ffn, attn = sums[0][...] + sums[1][...], sums[2][...] + sums[3][...]
    vectors = [attn[0:1], attn[1:2], ffn[2:3, width : 2 * width], ffn[1:2, 3 * width : 4 * width]]
    vectors += [ffn[2:3, :width]] + [ffn[1:2, i * width : (i + 1) * width] for i in range(3)]
    vectors = jnp.concatenate(vectors, axis=0)
    core, y, pair = place[0], place[1], place[2]
    count = wide // width
    for at in range(16):
        z, yy, cc = at // 4, (at // 2) % 2, at % 2
        rows = [vectors[:, at * share : (at + 1) * share]]
        for i in range(count):
            begin = (at * count + i) * share
            rows.append(ffn[0:1, begin : begin + share])
        rows.append(jnp.zeros((share - 8 - count, share), F32))
        part = jnp.concatenate(rows, axis=0)
        part = jnp.concatenate([part, jnp.zeros((share, LANES - share), F32)], axis=1)
        to = [jnp.bitwise_xor(core, cc), jnp.bitwise_xor(y, yy), jnp.bitwise_xor(pair, z // 2)]
        halves[(*to, z % 2, slice(None), slice(first, first + LANES))] = part.astype(BF16)


def grad_attn_body(place, wait, flush, held, kept, halves):
    x, x2, d_middle, context, context2, d_branch = held
    width = x.shape[1]
    wait(0)
    wait(1)
    left = stacked(x, x2)
    for i in range(3):
        wait(2, i)
        cols = slice(i * width, (i + 1) * width)
        split_blocks(dot_tn(left, stacked(d_middle, kept[0], cols)), place, halves, cols)
        flush(slice(None), slice(None), slice(None), slice(None), cols)
    for i in range(3, 6):
        wait(i)
    values = dot_tn(stacked(context, context2), stacked(d_branch, kept[1]))
    split_blocks(values, place, halves, slice(3 * width, 4 * width))
    write_table(place, kept[2:], halves, 4 * width)
    cols = slice(3 * width, 4 * width + LANES)
    flush(slice(None), slice(None), slice(None), slice(None), cols)


def weight_grad(a, b):
    return sum(dot_tn(one, two) for one, two in zip(a, b)).astype(BF16)


def tie(value, *others):
    return lax.optimization_barrier((value, others))[0]


def after(before, *values):
    return lax.optimization_barrier((values, tuple(before)))[0]


class Grid:
    def __init__(self):
        index = lax.axis_index("dp")
        self.core = index % 2
        self.y = (index // 2) % 2
        self.low = (index // 4) % 2
        self.pair = index // 8
        self.is_middle = self.low != self.pair

    def move(self, block, route):
        return lax.ppermute(block, "dp", route)

    def swap_core(self, block):
        return self.move(block, [(i, i ^ 1) for i in range(16)])

    def swap_y(self, block):
        return self.move(block, [(i, i ^ 2) for i in range(16)])

    def swap_near(self, block):
        return self.move(block, [(i, i ^ 4) for i in range(16)])

    def swap_middle(self, block):
        return self.move(block, [(i, i ^ 12) for i in range(4, 12)])

    def send_out(self, block):
        return self.move(block, [(i, i ^ 4) for i in range(4, 12)])

    def send_in(self, block):
        return self.move(block, [(i, i ^ 4) for i in range(16) if not 4 <= i < 12])

    def skip_out(self, block):
        return self.move(block, [(i, i ^ 8) for i in range(4, 12)])

    def skip_in(self, block):
        return self.move(block, [(i, i ^ 8) for i in range(16) if not 4 <= i < 12])

    def picked(self, blocks, at, axis):
        return lax.dynamic_index_in_dim(blocks, at, axis, keepdims=False)

    def ordered(self, pieces):
        near, far = (self.pair * 2 + self.low, self.pair * 2 + 1 - self.low), (
            jnp.where(self.pair == 0, 2, 1),
            jnp.where(self.pair == 0, 3, 0),
        )
        places = []
        for index in range(8):
            dc, dy, away = index // 4, (index // 2) % 2, index % 2
            for z in far if away else near:
                places.append(z * 4 + (self.y ^ dy) * 2 + (self.core ^ dc))
        return jnp.zeros_like(jnp.concatenate(pieces)).at[jnp.stack(places)].set(
            jnp.concatenate(pieces)
        )


def passed_along(block, axis, distance):
    devices = range(lax.axis_size(axis))
    route = [(i - distance, i) for i in devices if i - distance in devices]
    return lax.ppermute(block, axis, route)


def on_device(
    tokens,
    cotangent,
    bucket,
    lengths,
    w_qkv,
    bias_q,
    bias_v,
    w_out,
    bias_out,
    gain_attn,
    shift_attn,
    w_up,
    bias_up,
    w_down,
    bias_down,
    gain_ffn,
    shift_ffn,
):
    section = lax.axis_index("section")
    width = tokens.shape[2]
    ff = w_up.shape[2]
    share = bias_q.shape[1]
    n_dp = width // share
    vectors = (bias_q, bias_v, bias_out, gain_attn, shift_attn, bias_down, gain_ffn, shift_ffn)
    by_links = n_dp == 16 and share % 16 == 0
    shares = ff // width
    count = len(vectors) + shares
    row_table = jnp.concatenate(vectors + (bias_up.reshape(shares, share),))
    row_table = lax.optimization_barrier(row_table).astype(BF16)
    part_a = jnp.concatenate([w_qkv[0], w_out[0]], axis=1).astype(BF16)
    part_up, part_down = w_up[0].astype(BF16), w_down[0].astype(BF16)
    grid = Grid() if by_links else None
    place = jnp.stack([grid.core, grid.y, grid.pair, grid.low]) if by_links else jnp.zeros((4,), jnp.int32)
    micro = jnp.arange(6, dtype=jnp.int32) % 3
    micro = jnp.where(jnp.arange(6) < 3, micro - section, micro - 1 + section)
    picked = jnp.clip(micro, 0, 1)[:, None]
    run = (micro[:, None] == picked).astype(jnp.int32)
    first = picked == 0
    here = jnp.concatenate([section[None].astype(jnp.int32), place])
    steps = jnp.concatenate(
        [
            run,
            picked,
            jnp.broadcast_to(here[None, :1], (6, 1)),
            jnp.where(first, bucket[:1], bucket[1:]),
            jnp.where(first, lengths[:1], lengths[1:]),
            jnp.broadcast_to(here[None, 1:], (6, 4)),
        ],
        axis=1,
    )
    if by_links:
        padded = jnp.pad(row_table, ((0, share - count), (0, LANES - share)))
        part_a = jnp.concatenate([part_a, padded], axis=1)
        got_a, got_up = grid.swap_near(part_a), grid.swap_near(part_up)
        down_other = grid.swap_y(part_down)
        ended = (got_a, got_up, down_other, steps)
        near_a, near_up = jnp.stack([part_a, got_a]), jnp.stack([part_up, got_up])

        near_a, both_down = after(ended, near_a, jnp.stack([part_down, down_other]))
        middle_a, got_down = grid.swap_middle(near_a), grid.swap_near(both_down)
        near_a_y = grid.swap_y(near_a)
        ended = (middle_a, got_down, near_a_y)
        near_down = jnp.stack([part_down, got_down[0]])
        near_down_y = jnp.stack([down_other, got_down[1]])

        middle_a, near_up = after(ended, middle_a, near_up)
        out_a, middle_up = grid.send_out(middle_a), grid.swap_middle(near_up)
        near_up_y = grid.swap_y(near_up)
        ended = (out_a, middle_up, near_up_y)
        far_a = jnp.where(grid.is_middle, middle_a, out_a)

        middle_up, near_down, near_a, near_a_y = after(
            ended, middle_up, near_down, near_a, near_a_y
        )
        far_a = tie(far_a, near_up_y)
        out_up, middle_down = grid.send_out(middle_up), grid.swap_middle(near_down)
        far_a_y = grid.swap_y(far_a)
        near_a_c, near_a_yc = grid.swap_core(near_a), grid.swap_core(near_a_y)
        ended = (out_up, middle_down, far_a_y, near_a_c, near_a_yc)
        far_up = jnp.where(grid.is_middle, middle_up, out_up)

        middle_down, near_down_y, far_a, far_a_y, near_up, near_up_y, near_down = after(
            ended, middle_down, near_down_y, far_a, far_a_y, near_up, near_up_y, near_down
        )
        far_up = tie(far_up, far_a_y)
        out_down, middle_down_y = grid.send_out(middle_down), grid.swap_middle(near_down_y)
        far_up_y = grid.swap_y(far_up)
        far_a_c, far_a_yc = grid.swap_core(far_a), grid.swap_core(far_a_y)
        near_up_c, near_up_yc = grid.swap_core(near_up), grid.swap_core(near_up_y)
        near_down_c, near_down_yc = grid.swap_core(near_down), grid.swap_core(near_down_y)
        ended = (out_down, middle_down_y, far_up_y, far_a_c, far_a_yc)
        ended += (near_up_c, near_up_yc, near_down_c, near_down_yc)
        far_down = jnp.where(grid.is_middle, middle_down, out_down)
        pieces_a = (near_a, far_a, near_a_y, far_a_y, near_a_c, far_a_c, near_a_yc, far_a_yc)
        table = grid.ordered([piece[:, :, 4 * width :] for piece in pieces_a])
        table = table[:, :count, :share]
    else:
        w_a, full_up, full_down = (
            lax.all_gather(part, "dp", axis=0, tiled=True) for part in (part_a, part_up, part_down)
        )
        table = lax.all_gather(row_table[None], "dp", axis=0, tiled=True)
    table = table.astype(F32).transpose(1, 0, 2)
    rows = table[:8].reshape(8, width)
    small = jnp.concatenate(
        [rows[:1], jnp.zeros((1, width), F32), rows[1:], jnp.zeros((7, width), F32)]
    )
    full_bias_up = table[8:].transpose(1, 0, 2).reshape(1, ff)

    none = jnp.zeros((ROWS, width), BF16)

    def ahead(step, received, held=None):
        attn_held, ffn_held = (None, None) if held is None else held
        attn = forward_attn(step, steps, tokens, received, w_a, small, attn_held)
        return attn, forward_ffn(
            step, steps, full_up, full_down, small, full_bias_up, attn[2], attn[4], ffn_held
        )

    def back_ffn(step, upstream, kept, held=None, far=False):
        return ffn_back(
            3 + step, steps, cotangent[min(step, 1)], upstream, full_up, full_down, small, *kept, held, far
        )

    if by_links:
        middle_down_y, far_up, far_up_y = after(ended, middle_down_y, far_up, far_up_y)
        out_down_y = grid.send_out(middle_down_y)
        far_up_c, far_up_yc = grid.swap_core(far_up), grid.swap_core(far_up_y)
        far_down_c = grid.swap_core(far_down)
        first, *others = pieces_a
        pieces = (
            (tie(first, far_up_c, far_up_yc, far_down_c), *others),
            (near_up, far_up, near_up_y, far_up_y, near_up_c, far_up_c, near_up_yc, far_up_yc),
        )
        made = forward_first(0, steps, tokens, none, small, full_bias_up, pieces)
        attn, (d_act, act, x, context, hid, far_act, w_a, full_up) = made[:6], made[6:]
        far_down_y = jnp.where(grid.is_middle, middle_down_y, tie(out_down_y, d_act))
        pieces = (near_down, far_down, near_down_y, far_down_y, near_down_c, far_down_c)
        pieces += (near_down_yc, grid.swap_core(far_down_y))
        *end, full_down = forward_down(0, steps, pieces, small, attn[2], act)
        outer = ((*attn, x, context), (d_act, *end, far_act, hid))
    else:
        outer = ahead(0, none)
    got = passed_along(outer[1][3], "section", 1)
    middle = ahead(1, got)
    got = passed_along(middle[1][3], "section", 1)
    back_outer = back_ffn(0, none, middle)
    back_attn_outer = attn_back(3, steps, w_a, back_outer[2], back_outer[0], middle[0])
    sent = passed_along(back_attn_outer[0], "section", -1)
    outer = ahead(2, got, outer)
    back_middle = back_ffn(1, sent, outer, far=by_links)
    back_attn_middle = attn_back(
        4, steps, w_a, back_middle[2], back_middle[0], outer[0], far=by_links
    )
    sent = passed_along(back_attn_middle[0], "section", -1)
    back_outer = back_ffn(2, sent, middle, back_outer)

    def last_attn_back(steps):
        return attn_back(5, steps, w_a, back_outer[2], back_outer[0], middle_attn, back_attn_outer)

    middle_attn = middle[0]
    x, context = zip(outer[0][6:], middle[0][6:])
    hid = outer[1][5], middle[1][5]
    act, outputs = (outer[1][4], middle[1][4]), (outer[1][3], middle[1][3])
    sums_ffn = back_middle[1], back_outer[1]
    d_ffn, d_pre = zip(back_middle[3:5], back_outer[3:5])
    d_branch = back_attn_middle[3] if by_links else back_middle[0], back_outer[0]

    def by_micro(one, two):
        first = section == 0
        return jnp.stack([jnp.where(first, one, two), jnp.where(first, two, one)])[None]

    if by_links:
        def plus(one, two):
            return one.astype(F32) + two.astype(F32)

        mine_down, theirs = grad_call(
            grad_down_body,
            "grad_down",
            place,
            (d_ffn[0], *act),
            (d_ffn[1],),
            ff // 16,
            width,
            (1, 4, 4),
            fetch=False,
        )
        got_down = grid.swap_core(theirs)
        mine_up, theirs = grad_call(
            grad_up_body,
            "grad_up",
            place,
            (tie(hid[0], mine_down), hid[1], d_pre[0]),
            (d_pre[1],),
            share,
            ff,
            (1, 1, 4),
            fetch=False,
        )

        def low_sum(*parts):
            return sum(part.astype(F32) for part in parts).astype(BF16)

        down_parts = [(mine_down[i, 1], got_down[i, 1]) for i in range(2)]
        out, out_y = (low_sum(*parts) for parts in down_parts)
        out, out_y, theirs, table = after((got_down, mine_up), out, out_y, theirs, steps)
        got_out, got_up = grid.send_in(out), grid.swap_core(theirs)
        last = last_attn_back(table)
        (got_out,) = after((last[1],), got_out)

        out_y, early_up, early_got = after((got_out,), out_y, mine_up, got_up)
        away_up, away_near = (low_sum(early_up[1, i], early_got[1, i]) for i in (1, 0))
        middle = low_sum(out, got_out)
        far_up_y, got_out_y = grid.swap_y(away_up), grid.send_in(out_y)
        got_middle = grid.swap_middle(middle)
        up_home = low_sum(early_up[0, 1], early_got[0, 1])
        (first_x,) = after((middle, away_up, away_near, up_home), x[0])
    else:
        last = last_attn_back(steps)
    input_grads, sums_attn, d_qkv = zip(back_attn_middle[:3], last)
    total = sums_ffn[0] + sums_ffn[1]
    total_attn = sums_attn[0] + sums_attn[1]
    vector_rows = jnp.stack(
        [
            total_attn[0],
            total_attn[1],
            total[2, width : 2 * width],
            total[1, 3 * width :],
            total[2, :width],
            total[1, :width],
            total[1, width : 2 * width],
            total[1, 2 * width : 3 * width],
        ]
    ).reshape(8, n_dp, share)
    table = jnp.concatenate(
        [vector_rows.transpose(1, 0, 2), total[0].reshape(n_dp, shares, share)], axis=1
    )
    if by_links:
        mine_a, theirs = grad_call(
            grad_attn_body,
            "grad_attn",
            place,
            (first_x, x[1], d_qkv[0], *context, d_branch[0]),
            (d_qkv[1], d_branch[1], *sums_ffn, *sums_attn),
            share,
            4 * width + LANES,
            (1, 1, 3, 1, 1, 1),
        )
        far_up_y, got_out_y, got_middle = after((mine_a,), far_up_y, got_out_y, got_middle)
        theirs, away_up = after((far_up_y, got_out_y, got_middle), theirs, away_near)
        got_a, near_up_y = grid.swap_core(theirs), grid.swap_y(away_up)
        far_up = low_sum(up_home, far_up_y)
        got_out_up = grid.send_in(far_up)
        got_middle_y = grid.swap_middle(low_sum(out_y, got_out_y))
        mine_up, got_up, mine_down, got_down = after(
            (got_a,), mine_up, got_up, mine_down, got_down
        )
        away_a, away_a_near = (low_sum(mine_a[1, i], got_a[1, i]) for i in (1, 0))
        got_out_up, got_middle_y, near_up_y = after(
            (away_a, away_a_near), got_out_up, got_middle_y, near_up_y
        )

        def down_sum(at, i):
            parts = (mine_down[i, 0], got_down[i, 0], (got_middle, got_middle_y)[i])
            return sum(grid.picked(part, at, 0).astype(F32) for part in parts)

        def up_sum(at):
            parts = (mine_up[0, 0], got_up[0, 0], near_up_y, got_middle_up)
            return sum(grid.picked(part, at, 0).astype(F32) for part in parts)

        def a_sum(at):
            parts = (mine_a[0, 0], got_a[0, 0], near_a_y)
            return sum(grid.picked(part, at, 0).astype(F32) for part in parts)

        (away_a,) = after((got_out_up, got_middle_y, near_up_y), away_a)
        far_a_y = grid.swap_y(away_a)
        got_middle_up = grid.swap_middle(low_sum(far_up, got_out_up))
        away = [down_sum(1 - grid.low, i).astype(BF16) for i in range(2)]
        got_near_down = grid.swap_near(jnp.stack(away))

        (away_a,) = after((far_a_y, got_middle_up, got_near_down), away_a_near)
        parts = (mine_a[0, 1], got_a[0, 1], far_a_y)
        one, other = (
            low_sum(*(grid.picked(part, at, 0) for part in parts)) for at in (grid.low, 1 - grid.low)
        )
        got_in, got_over, got_skip = grid.send_in(one), grid.swap_middle(one), grid.skip_in(other)
        near_a_y = grid.swap_y(away_a)
        both_down = [down_sum(grid.low, i) + got_near_down[i].astype(F32) for i in range(2)]
        away_down, away_up = both_down[1].astype(BF16), up_sum(1 - grid.low).astype(BF16)
        got_in, got_over, got_skip, near_a_y = after(
            (away_down, away_up), got_in, got_over, got_skip, near_a_y
        )

        away_down, away_up = after((got_in, got_over, got_skip, near_a_y), away_down, away_up)
        away = a_sum(1 - grid.low) + got_over.astype(F32) + got_skip.astype(F32)
        outputs, input_grads = after((got_in, got_over), outputs, input_grads)
        got_near_a = grid.swap_near(away.astype(BF16))
        got_middle_a = grid.swap_middle(low_sum(other, got_in))
        got_near_up, got_down_y = grid.swap_near(away_up), grid.swap_y(away_down)
        g_down = both_down[0] + got_down_y.astype(F32)
        g_up = up_sum(grid.low) + got_near_up.astype(F32)
        g_a = a_sum(grid.low) + got_near_a.astype(F32) + got_middle_a.astype(F32)
        table = g_a[:count, 4 * width : 4 * width + share]
    else:

        def summed(values):
            return lax.psum_scatter(values, "dp", scatter_dimension=0, tiled=True).astype(F32)

        g_down = summed(weight_grad(act, d_ffn))
        g_up = summed(weight_grad(hid, d_pre))
        g_qkv = weight_grad(x, d_qkv)
        g_out = weight_grad(context, d_branch)
        g_a = summed(jnp.concatenate([g_qkv, g_out], axis=1))
        table = summed(table)[0]
    hidden_states, input_grads = by_micro(*outputs), by_micro(*input_grads)
    g_down, g_up = g_down[None], g_up[None]
    g_qkv, g_out = g_a[None, :, : 3 * width], g_a[None, :, 3 * width : 4 * width]
    g_vectors = [table[i : i + 1] for i in range(8)]
    g_bias_up = table[8:].reshape(1, ff // n_dp)
    (
        g_bias_q,
        g_bias_v,
        g_bias_out,
        g_gain_attn,
        g_shift_attn,
        g_bias_down,
        g_gain_ffn,
        g_shift_ffn,
    ) = g_vectors
    return (
        hidden_states,
        input_grads,
        g_qkv,
        g_bias_q,
        g_bias_v,
        g_out,
        g_bias_out,
        g_gain_attn,
        g_shift_attn,
        g_up,
        g_bias_up,
        g_down,
        g_bias_down,
        g_gain_ffn,
        g_shift_ffn,
    )


def solution(mesh):
    matrix = P("section", "dp", None)
    vector = P("section", "dp")
    rows = P(None, "dp", None)
    outs = P("section", None, "dp", None)
    params = (
        matrix,
        vector,
        vector,
        matrix,
        vector,
        vector,
        vector,
        matrix,
        vector,
        matrix,
        vector,
        vector,
        vector,
    )
    return jax.shard_map(
        on_device,
        mesh=mesh,
        in_specs=(rows, rows, P(None, "dp"), P(None, "dp")) + params,
        out_specs=(outs, outs) + params,
        check_vma=False,
    )
```

```python
import functools

import jax
import jax.numpy as jnp
from jax import lax
from jax.experimental import pallas as pl
from jax.experimental.pallas import tpu as pltpu
from jax.sharding import PartitionSpec as P

HEADS = 12
SEGMENT = 64
PAIRS = 6
ROWS = 384
EPSILON = 1e-06
MASKED = -1000000000.0
LANES = 128
FF_TILE = 1024
LIMIT = 4
LIMIT_GRAD = 6
VMEM_LIMIT = 60 * 1024 * 1024
F32 = jnp.float32
BF16 = jnp.bfloat16

BIAS_Q, BIAS_K, BIAS_V, BIAS_OUT, GAIN_ATTN, SHIFT_ATTN, BIAS_DOWN, GAIN_FFN, SHIFT_FFN = range(9)
RUN, MICRO, SECTION, BUCKET, LENGTHS = range(5)
CORE, Y, PAIR, LOW = range(LENGTHS + PAIRS, LENGTHS + PAIRS + 4)

ANY = pl.BlockSpec(memory_space=pl.ANY)
WHOLE = pl.BlockSpec(memory_space=pltpu.VMEM)
SCALARS = pl.BlockSpec(memory_space=pltpu.SMEM)
FAR = pl.BlockSpec(memory_space=pltpu.HBM)
COST = pl.CostEstimate(flops=1, bytes_accessed=1, transcendentals=0)


def in_hbm(arrays):
    return [pltpu.with_memory_space_constraint(array, pltpu.HBM) for array in arrays]


def dot_nn(a, b):
    return lax.dot_general(a, b, (((1,), (0,)), ((), ())), preferred_element_type=F32)


def dot_nt(a, b):
    return lax.dot_general(a, b, (((1,), (1,)), ((), ())), preferred_element_type=F32)


def dot_tn(a, b):
    return lax.dot_general(a, b, (((0,), (0,)), ((), ())), preferred_element_type=F32)


class Row:
    def __init__(self, table, row):
        self.table, self.row = table, row

    def __getitem__(self, at):
        return self.table[self.row, at]


def fold(values):
    rows, n = values.shape
    return jnp.sum(values.reshape(rows // 8, 8, n), axis=0)


def write_bias(info, bias, block, count):
    segment = (info[BUCKET] + 1) * SEGMENT
    per_block = jnp.where(info[BUCKET] == 0, block // SEGMENT, 1)
    k_row = lax.broadcasted_iota(jnp.int32, (block, block), 0)
    q_row = lax.broadcasted_iota(jnp.int32, (block, block), 1)

    def pair_of(row):
        return (row >= segment).astype(jnp.int32) + (row >= 2 * segment).astype(jnp.int32)

    k_pair = pair_of(k_row)
    same = k_pair == pair_of(q_row)
    position = k_row - k_pair * segment
    for at in range(count):
        valid = [
            jnp.minimum(info[LENGTHS + jnp.minimum(at * per_block + i, PAIRS - 1)], segment)
            for i in range(3)
        ]
        length = jnp.where(k_pair == 0, valid[0], jnp.where(k_pair == 1, valid[1], valid[2]))
        bias[at, :block, :block] = jnp.where(same & (position < length), 0.0, MASKED)


def half_masks():
    lane = lax.broadcasted_iota(jnp.int32, (1, LANES), 1)
    low = (lane < LANES // 2).astype(F32)
    return low.astype(BF16), (1.0 - low).astype(BF16)


def by_block(info, body):
    @pl.when(info[BUCKET] == 1)
    def _():
        body(2 * SEGMENT, ROWS // (2 * SEGMENT))

    @pl.when(info[BUCKET] != 1)
    def _():
        body(3 * SEGMENT, ROWS // (3 * SEGMENT))


def attention(info, qkv, context, lse, bias):
    width = context.shape[1]
    low, high = half_masks()

    def both_heads(values):
        return jnp.concatenate([values * low, values * high], axis=0)

    def body(block, count):
        write_bias(info, bias, block, count)

        def pair_step(pair, carry):
            at_q = pl.multiple_of(pair * LANES, LANES)
            at_k = pl.multiple_of(width + pair * LANES, LANES)
            at_v = pl.multiple_of(2 * width + pair * LANES, LANES)
            rows = [pl.ds(at * block, block) for at in range(count)]
            q = [qkv[r, pl.ds(at_q, LANES)] for r in rows]
            k = [both_heads(qkv[r, pl.ds(at_k, LANES)]) for r in rows]
            v = [both_heads(qkv[r, pl.ds(at_v, LANES)]) for r in rows]
            masks = [bias[at, :block, :block] for at in range(count)]
            scores = [
                dot_nt(k[at], q[at]).reshape(2, block, block) + masks[at][None]
                for at in range(count)
            ]
            tops = [jnp.max(x, axis=1, keepdims=True) for x in scores]
            weights = [jnp.exp(x - top) for x, top in zip(scores, tops)]
            totals = [jnp.sum(x, axis=1, keepdims=True) for x in weights]
            probs = [
                (x * (1.0 / total)).astype(BF16).reshape(2 * block, block)
                for x, total in zip(weights, totals)
            ]
            parts = [dot_tn(x, values) for x, values in zip(probs, v)]
            for at in range(count):
                ends = tops[at] + jnp.log(totals[at])
                for half in range(2):
                    lse[2 * pair + half, at : at + 1, :block] = ends[half]
                context[rows[at], pl.ds(at_q, LANES)] = parts[at].astype(BF16)
            return carry

        def steps(i, carry):
            for sub in range(3):
                pair_step(i * 3 + sub, carry)
            return carry

        lax.fori_loop(0, HEADS // 2 // 3, steps, 0)

    by_block(info, body)


def attention_back(info, qkv, d_context, lse, bias, d_qkv):
    width = d_context.shape[1]
    low, high = half_masks()
    scale = (width // HEADS) ** -0.5

    def both_heads(values):
        return jnp.concatenate([values * low, values * high], axis=0)

    def flat(values):
        return values.astype(BF16).reshape(2 * values.shape[1], values.shape[2])

    def body(block, count):
        write_bias(info, bias, block, count)

        def pair_step(pair, carry):
            at_q = pl.multiple_of(pair * LANES, LANES)
            at_k = pl.multiple_of(width + pair * LANES, LANES)
            at_v = pl.multiple_of(2 * width + pair * LANES, LANES)
            is_low = lax.broadcasted_iota(jnp.int32, (block, LANES), 1) < LANES // 2
            rows = [pl.ds(at * block, block) for at in range(count)]
            q = [qkv[r, pl.ds(at_q, LANES)] for r in rows]
            k = [both_heads(qkv[r, pl.ds(at_k, LANES)]) for r in rows]
            v = [both_heads(qkv[r, pl.ds(at_v, LANES)]) for r in rows]
            d_out = [d_context[r, pl.ds(at_q, LANES)] for r in rows]
            masks = [bias[at, :block, :block] for at in range(count)]
            scores = [
                dot_nt(k[at], q[at]).reshape(2, block, block) + masks[at][None]
                for at in range(count)
            ]
            d_probs = [dot_nt(v[at], d_out[at]).reshape(2, block, block) for at in range(count)]
            ends = [
                jnp.stack([lse[2 * pair + half, at : at + 1, :block] for half in range(2)])
                for at in range(count)
            ]
            probs = [jnp.exp(x - end) for x, end in zip(scores, ends)]
            d_v = [dot_nn(flat(x), d_out[at]) for at, x in enumerate(probs)]
            inner = [jnp.sum(x * d_x, axis=1, keepdims=True) for x, d_x in zip(probs, d_probs)]
            d_scores = [
                flat(x * (d_x - total)) for x, d_x, total in zip(probs, d_probs, inner)
            ]
            d_k = [dot_nn(x, q[at]) for at, x in enumerate(d_scores)]
            d_q = [dot_tn(x, k[at]) for at, x in enumerate(d_scores)]
            for at, r in enumerate(rows):
                d_qkv[r, pl.ds(at_q, LANES)] = (d_q[at] * scale).astype(BF16)
                for to, part in ((at_k, d_k[at]), (at_v, d_v[at])):
                    part = jnp.where(is_low, part[:block], part[block:])
                    d_qkv[r, pl.ds(to, LANES)] = part.astype(BF16)
            return carry

        def steps(i, carry):
            for sub in range(3):
                pair_step(i * 3 + sub, carry)
            return carry

        lax.fori_loop(0, HEADS // 2 // 3, steps, 0)

    by_block(info, body)


def norm(values):
    centered = values - jnp.mean(values, axis=-1, keepdims=True)
    inverse = lax.rsqrt(jnp.mean(centered * centered, axis=-1, keepdims=True) + EPSILON)
    return centered * inverse, inverse


def norm_back(upstream, normed, inverse, gain):
    scaled = upstream * gain
    return inverse * (
        scaled
        - jnp.mean(scaled, axis=-1, keepdims=True)
        - normed * jnp.mean(scaled * normed, axis=-1, keepdims=True)
    )


CHUNK = 64


def by_rows(step, carry=0):
    def body(i, carry):
        return step(pl.ds(pl.multiple_of(i * CHUNK, CHUNK), CHUNK), carry)

    return lax.fori_loop(0, ROWS // CHUNK, body, carry)


def carry_over(src, dst):
    if src.shape[0] == ROWS:

        def step(rows, carry):
            dst[rows, :] = src[rows, :]
            return carry

        by_rows(step)
    else:
        dst[...] = src[...]


def join_copies(info, pieces, out, sems):
    core, y, pair, low = (info[i] for i in (CORE, Y, PAIR, LOW))
    near = (pair * 2 + low, pair * 2 + 1 - low)
    far = (jnp.where(pair == 0, 2, 1), jnp.where(pair == 0, 3, 0))
    share = pieces[0].shape[1]
    copies = []
    for index, piece in enumerate(pieces):
        dc, dy, away = index // 4, (index // 2) % 2, index % 2
        for i, z in enumerate(far if away else near):
            at = z * 4 + jnp.bitwise_xor(y, dy) * 2 + jnp.bitwise_xor(core, dc)
            rows = pl.ds(pl.multiple_of(at * share, 16), share)
            copies.append(pltpu.make_async_copy(piece.at[i], out.at[rows, :], sems.at[len(copies)]))
    return copies


def kernel_call(body, name, step, ins, out_shapes, held, scratch, limit, far=(), pieces=(), far_ins=()):
    held = [] if held is None else list(held)
    given = len(ins) - 1
    count = len(out_shapes)
    spec = [FAR if i in far else WHOLE for i in range(count)]

    def kernel(table, *refs):
        info = Row(table, step)
        blocks, refs = refs[: 8 * len(pieces)], refs[8 * len(pieces) :]
        kept = refs[given : given + len(held)]
        outs = refs[given + len(held) :][:count]
        own = refs[given + len(held) + count :]
        joins = [
            join_copies(
                info, blocks[8 * i : 8 * i + 8], outs[count - len(pieces) + i], own[len(scratch)].at[i]
            )
            for i in range(len(pieces))
        ]
        for copy in sum(joins, []):
            copy.start()

        def wait_for(join):
            def wait():
                for copy in join:
                    copy.wait()

            return wait

        waits = [wait_for(join) for join in joins]

        @pl.when(info[RUN] == 1)
        def _():
            copies = []

            def flush(index, ref):
                copy = pltpu.make_async_copy(ref, outs[index], own[-1].at[len(copies)])
                copy.start()
                copies.append(copy)

            near = [out for i, out in enumerate(outs) if i not in far]
            given_waits = (waits,) if pieces else ()
            body(info, flush, *given_waits, *refs[:given], *near, *own[: len(scratch)])
            for copy in copies:
                copy.wait()

        if held or pieces:

            @pl.when(info[RUN] != 1)
            def _():
                for wait in waits:
                    wait()
                for i, (src, dst) in enumerate(zip(kept, outs)):
                    if i not in far:
                        carry_over(src, dst)

    return pl.pallas_call(
        kernel,
        in_specs=[SCALARS]
        + [FAR] * (8 * len(pieces))
        + [FAR if i in far_ins else WHOLE for i in range(given)]
        + spec[: len(held)],
        out_specs=spec,
        out_shape=[
            pltpu.HBM(shape, kind) if i in far else jax.ShapeDtypeStruct(shape, kind)
            for i, (shape, kind) in enumerate(out_shapes)
        ],
        input_output_aliases={1 + given + i: i for i in range(len(held))},
        scratch_shapes=scratch
        + ([pltpu.SemaphoreType.DMA((len(pieces), 16))] if pieces else [])
        + ([pltpu.SemaphoreType.DMA((len(far),))] if far else []),
        compiler_params=pltpu.CompilerParams(vmem_limit_bytes=int(limit * 1024 * 1024)),
        cost_estimate=COST,
        name=name,
    )(
        ins[0],
        *in_hbm([piece for group in pieces for piece in group]),
        *(in_hbm([x])[0] if i in far_ins else x for i, x in enumerate(ins[1:])),
        *(in_hbm([x])[0] if i in far else x for i, x in enumerate(held)),
    )


def forward_attn_body(
    info, flush, tok, rec, w_a, small, qkv, lse, n1, inv1, hid, n1_low, x, context, acc, bias, sem, ready=None
):
    width = x.shape[1]

    @pl.when(info[SECTION] == 0)
    def _():
        copy = pltpu.make_async_copy(tok.at[info[MICRO]], x, sem)
        copy.start()
        copy.wait()

    @pl.when(info[SECTION] != 0)
    def _():
        x[...] = rec[...]

    flush(6, x)
    if ready is not None:
        ready()
    for j, (row, factor) in enumerate(
        ((BIAS_Q, (width // HEADS) ** -0.5), (BIAS_K, 1.0), (BIAS_V, 1.0))
    ):
        cols = slice(j * width, (j + 1) * width)
        part = dot_nn(x[...], w_a[:, cols]) + small[row : row + 1, :]
        qkv[:, cols] = (part * factor).astype(BF16)
    attention(info, qkv, context, lse, bias)
    flush(7, context)
    acc[...] = dot_nn(context[...], w_a[:, 3 * width : 4 * width])

    def norm_one(rows, carry):
        total = x[rows, :].astype(F32) + acc[rows, :]
        normed, inverse = norm(total + small[BIAS_OUT : BIAS_OUT + 1, :])
        n1[rows, :] = normed
        n1_low[rows, :] = normed.astype(BF16)
        inv1[rows, :] = jnp.broadcast_to(inverse, (CHUNK, LANES))
        hidden = normed * small[GAIN_ATTN : GAIN_ATTN + 1, :]
        hid[rows, :] = (hidden + small[SHIFT_ATTN : SHIFT_ATTN + 1, :]).astype(BF16)
        return carry

    by_rows(norm_one)


def up_tile(j, hid, w_up, bias_up, act, d_act):
    cols = slice(j * FF_TILE, (j + 1) * FF_TILE)
    pre = dot_nn(hid[...], w_up[:, cols]) + bias_up[:, cols]
    below = 0.5 * (1.0 + lax.erf(pre * 0.7071067811865476))
    density = jnp.exp(pre * pre * -0.5) * 0.3989422804014327
    act[:, cols] = (pre * below).astype(BF16)
    d_act[:, cols] = (below + pre * density).astype(BF16)


def down_tile(j, act, w_down, acc):
    cols = slice(j * FF_TILE, (j + 1) * FF_TILE)
    part = dot_nn(act[:, cols], w_down[cols, :])
    acc[...] = part if j == 0 else acc[...] + part


def layer_end(small, n1, n2, inv2, out, acc):
    def norm_two(rows, carry):
        hidden = n1[rows, :] * small[GAIN_ATTN : GAIN_ATTN + 1, :]
        hidden = hidden + small[SHIFT_ATTN : SHIFT_ATTN + 1, :]
        normed, inverse = norm(hidden + acc[rows, :] + small[BIAS_DOWN : BIAS_DOWN + 1, :])
        n2[rows, :] = normed.astype(BF16)
        inv2[rows, :] = jnp.broadcast_to(inverse, (CHUNK, LANES))
        out[rows, :] = (
            normed * small[GAIN_FFN : GAIN_FFN + 1, :] + small[SHIFT_FFN : SHIFT_FFN + 1, :]
        ).astype(BF16)
        return carry

    by_rows(norm_two)


def forward_ffn_body(
    info, flush, w_up, w_down, small, bias_up, n1, hid, d_act, n2, inv2, out, act, acc
):
    tiles = act.shape[1] // FF_TILE
    flush(5, hid)
    up_tile(0, hid, w_up, bias_up, act, d_act)
    for j in range(1, tiles):
        up_tile(j, hid, w_up, bias_up, act, d_act)
        down_tile(j - 1, act, w_down, acc)
    flush(4, act)
    down_tile(tiles - 1, act, w_down, acc)
    layer_end(small, n1, n2, inv2, out, acc)


def forward_down_body(info, flush, w_down, small, n1, act, n2, inv2, out, acc):
    for j in range(act.shape[1] // FF_TILE):
        down_tile(j, act, w_down, acc)
    layer_end(small, n1, n2, inv2, out, acc)


def bias_scratch():
    return pltpu.VMEM((3, 3 * SEGMENT, 3 * SEGMENT), F32)


def joined_shape(pieces):
    share, n = pieces[0].shape[-2:]
    return (((16 * share, n), BF16),)


def forward_attn(step, info, tokens, received, w_a, small, held=None):
    width = small.shape[1]
    rows = ((ROWS, width), BF16)
    return kernel_call(
        forward_attn_body,
        "forward_attn",
        step,
        (info, tokens, received, w_a, small),
        attn_shapes(width) + (rows, rows),
        held,
        [pltpu.VMEM(*rows)] * 2
        + [pltpu.VMEM((ROWS, width), F32), bias_scratch(), pltpu.SemaphoreType.DMA],
        LIMIT + 1.2,
        far=(6, 7),
        far_ins=(0,),
    )


def attn_shapes(width):
    rows = ((ROWS, width), BF16)
    return (
        ((ROWS, 3 * width), BF16),
        ((HEADS, 8, 256), F32),
        ((ROWS, width), F32),
        ((ROWS, LANES), F32),
        rows,
        rows,
    )


def forward_first_body(info, flush, waits, tok, rec, small, bias_up, *refs):
    attn_refs, (d_act, act, w_a, w_up), (x, context, acc, bias, sem) = refs[:6], refs[6:10], refs[10:]

    def flush_attn(index, ref):
        flush(index + 2, ref)

    forward_attn_body(
        info, flush_attn, tok, rec, w_a, small, *attn_refs, x, context, acc, bias, sem, waits[0]
    )
    hid = attn_refs[4]
    flush(10, hid)
    waits[1]()
    for j in range(act.shape[1] // FF_TILE):
        up_tile(j, hid, w_up, bias_up, act, d_act)
    flush(11, act)


def forward_first(step, info, tokens, received, small, bias_up, pieces):
    width, ff = small.shape[1], bias_up.shape[1]
    rows, wide = ((ROWS, width), BF16), ((ROWS, ff), BF16)
    return kernel_call(
        forward_first_body,
        "forward_first",
        step,
        (info, tokens, received, small, bias_up),
        attn_shapes(width)
        + (wide, wide, rows, rows, rows, wide)
        + joined_shape(pieces[0])
        + joined_shape(pieces[1]),
        None,
        [pltpu.VMEM(*rows)] * 2
        + [pltpu.VMEM((ROWS, width), F32), bias_scratch(), pltpu.SemaphoreType.DMA],
        LIMIT + 1.2,
        far=(8, 9, 10, 11),
        pieces=pieces,
        far_ins=(0,),
    )


def forward_ffn(step, info, w_up, w_down, small, bias_up, n1, hid, held=None):
    width, ff = small.shape[1], bias_up.shape[1]
    rows, wide = ((ROWS, width), BF16), ((ROWS, ff), BF16)
    return kernel_call(
        forward_ffn_body,
        "forward_ffn",
        step,
        (info, w_up, w_down, small, bias_up, n1, hid),
        (wide, rows, ((ROWS, LANES), F32), rows, wide, rows),
        held,
        [pltpu.VMEM((ROWS, ff), BF16), pltpu.VMEM((ROWS, width), F32)],
        LIMIT + 2.4,
        far=(4, 5),
    )


def forward_down(step, info, pieces, small, n1, act):
    width = small.shape[1]

    def body(info, flush, waits, small, n1, act, n2, inv2, out, w_down, acc):
        waits[0]()
        forward_down_body(info, flush, w_down, small, n1, act, n2, inv2, out, acc)

    shapes = (((ROWS, width), BF16), ((ROWS, LANES), F32), ((ROWS, width), BF16))
    return kernel_call(
        body,
        "forward_down",
        step,
        (info, small, n1, act),
        shapes + joined_shape(pieces),
        None,
        [pltpu.VMEM((ROWS, width), F32)],
        LIMIT,
        pieces=(pieces,),
    )


def norm_back_rows(upstream, normed, inverse, gain, grad, low):
    zeros = jnp.zeros((8, grad.shape[1]), F32)

    def step(rows, carry):
        up, nm = upstream(rows), normed(rows)
        values = norm_back(up, nm, inverse(rows), gain)
        grad[rows, :] = values
        rounded = values.astype(BF16)
        low(rows, rounded)
        return (
            carry[0] + fold(up),
            carry[1] + fold(up * nm),
            carry[2] + fold(rounded.astype(F32)),
        )

    sums = by_rows(step, (zeros, zeros, zeros))
    return [jnp.sum(part, axis=0, keepdims=True) for part in sums]


def ffn_back_body(
    far,
    info,
    flush,
    cot,
    rec,
    w_up,
    w_down,
    small,
    n1,
    inv1,
    d_act,
    n2,
    inv2,
    d_branch,
    sums,
    d_first,
    d_ffn,
    d_pre,
    acc,
):
    if not far:

        def flush(index, ref):
            pass

    width = rec.shape[1]
    ff = d_pre.shape[1]
    tiles = ff // FF_TILE

    last = info[SECTION] == 1

    def upstream(rows):
        return jnp.where(last, cot[rows, :], rec[rows, :]).astype(F32)

    def keep_ffn(rows, low):
        d_ffn[rows, :] = low

    sum_g, sum_gn, sum_d = norm_back_rows(
        upstream,
        lambda rows: n2[rows, :].astype(F32),
        lambda rows: inv2[rows, :1],
        small[GAIN_FFN : GAIN_FFN + 1, :],
        acc,
        keep_ffn,
    )
    flush(3, d_ffn)
    sums[1:2, :width] = sum_d
    sums[1:2, width : 2 * width] = sum_gn
    sums[1:2, 2 * width : 3 * width] = sum_g

    def first(j):
        cols = slice(j * FF_TILE, (j + 1) * FF_TILE)
        part = dot_nt(d_ffn[...], w_down[cols, :]) * d_act[:, cols].astype(F32)
        low = part.astype(BF16)
        d_pre[:, cols] = low
        sums[0:1, cols] = jnp.sum(fold(low.astype(F32)), axis=0, keepdims=True)

    def second(j):
        cols = slice(j * FF_TILE, (j + 1) * FF_TILE)
        acc[...] += dot_nt(d_pre[:, cols], w_up[:, cols])

    first(0)
    for j in range(1, tiles):
        first(j)
        second(j - 1)
    flush(4, d_pre)
    second(tiles - 1)

    def keep_branch(rows, low):
        d_branch[rows, :] = low

    sum_g, sum_gn, sum_d = norm_back_rows(
        lambda rows: acc[rows, :],
        lambda rows: n1[rows, :].astype(F32),
        lambda rows: inv1[rows, :1],
        small[GAIN_ATTN : GAIN_ATTN + 1, :],
        d_first,
        keep_branch,
    )
    sums[1:2, 3 * width :] = sum_gn
    sums[2:3, :width] = sum_g
    sums[2:3, width : 2 * width] = sum_d


def ffn_back(step, info, cotangent, received, w_up, w_down, small, attn, ffn, held=None, far=False):
    width, ff = w_up.shape
    rows, wide = ((ROWS, width), BF16), ((ROWS, ff), BF16)
    shapes = (rows, ((8, ff), F32), ((ROWS, width), F32), rows, wide)
    scratch = [pltpu.VMEM(*rows), pltpu.VMEM(*wide)] if far else []
    return kernel_call(
        functools.partial(ffn_back_body, far),
        "ffn_backward",
        step,
        (info, cotangent, received, w_up, w_down, small, attn[5], attn[3], ffn[0], ffn[1], ffn[2]),
        shapes,
        held,
        scratch + [pltpu.VMEM((ROWS, width), F32)],
        LIMIT + (3 if far else 0),
        far=(3, 4) if far else (),
    )


def attn_back_body(
    far, info, flush, w_a, d_first, d_branch, qkv, lse, grads, sums, d_qkv, d_context, bias
):
    if not far:

        def flush(index, ref):
            pass

    flush(3, d_branch)
    width = d_first.shape[1]

    d_context[...] = dot_nt(d_branch[...], w_a[:, 3 * width : 4 * width]).astype(BF16)
    attention_back(info, qkv, d_context, lse, bias, d_qkv)
    flush(2, d_qkv)
    grad = d_first[...] + dot_nt(d_qkv[...], w_a[:, : 3 * width])
    low = grad.astype(BF16)
    grads[...] = low
    for row, at in ((0, 0), (1, 2 * width)):
        sums[row : row + 1, :] = jnp.sum(
            fold(d_qkv[:, at : at + width].astype(F32)), axis=0, keepdims=True
        )


def attn_back(step, info, w_a, d_first, d_branch, attn, held=None, far=False):
    width = d_first.shape[1]
    rows, wide = ((ROWS, width), BF16), ((ROWS, 3 * width), BF16)
    return kernel_call(
        functools.partial(attn_back_body, far),
        "attention_backward",
        step,
        (info, w_a, d_first, d_branch, attn[0], attn[1]),
        (rows, ((8, width), F32), wide) + ((rows,) if far else ()),
        held,
        ([pltpu.VMEM(*wide)] if far else []) + [pltpu.VMEM(*rows), bias_scratch()],
        LIMIT + (1.8 if far else 0),
        far=(2, 3) if far else (),
    )


def split_blocks(values, place, halves, cols, first_z=0):
    share = halves.shape[4]
    core, y, pair = place[0], place[1], place[2]
    for index in range(values.shape[0] // (4 * share)):
        z = first_z + index
        for yy in range(2):
            for cc in range(2):
                at = (index * 4 + yy * 2 + cc) * share
                part = values[at : at + share].astype(BF16)
                to = [jnp.bitwise_xor(core, cc), jnp.bitwise_xor(y, yy), jnp.bitwise_xor(pair, z // 2)]
                halves[(*to, z % 2, slice(None), cols)] = part


def grad_call(body, name, place, far, near, share, n, cuts, fetch=True):
    shape = (2, 2, 2, share, n)
    total = sum(cuts)

    def kernel(place, *refs):
        sources, refs = refs[: len(far)], refs[len(far) :]
        kept, refs = refs[: len(near)], refs[len(near) :]
        if not fetch:
            refs = (*refs[:3], *sources, refs[-1])
        mine_out, theirs_out, halves, *held, sems = refs
        copies = []
        for src, dst, cut in zip(sources, held, cuts) if fetch else ():
            size = src.shape[1] // cut
            group = []
            for i in range(cut):
                cols = slice(i * size, (i + 1) * size)
                sem = sems.at[sum(map(len, copies)) + i]
                group.append(pltpu.make_async_copy(src.at[:, cols], dst.at[:, cols], sem))
            copies.append(group)
        for i in range(max(cuts)):
            for group in copies:
                if i < len(group):
                    group[i].start()
        done = set()

        def wait(index, part=0):
            if fetch and (index, part) not in done:
                done.add((index, part))
                copies[index][part].wait()

        sent = []

        def flush(*at):
            for core, dst in ((1, theirs_out), (0, mine_out)):
                src = halves.at[(core, *at)]
                copy = pltpu.make_async_copy(src, dst.at[at], sems.at[total + len(sent)])
                copy.start()
                sent.append(copy)

        body(place, wait, flush, held, kept, halves)
        for copy in sent:
            copy.wait()

    held = far if fetch else ()
    scratch = [pltpu.VMEM((2, *shape), BF16)] + [pltpu.VMEM(x.shape, x.dtype) for x in held]
    size = sum(x.size * 2 for x in held) + 32 * share * n
    return pl.pallas_call(
        kernel,
        in_specs=[SCALARS] + [FAR if fetch else WHOLE] * len(far) + [WHOLE] * len(near),
        out_specs=[FAR] * 2,
        out_shape=[pltpu.HBM(shape, BF16)] * 2,
        scratch_shapes=scratch + [pltpu.SemaphoreType.DMA((total + 8,))],
        compiler_params=pltpu.CompilerParams(vmem_limit_bytes=size + LIMIT_GRAD * 1024 * 1024),
        cost_estimate=COST,
        name=name,
    )(place, *(in_hbm(far) if fetch else far), *near)


def stacked(one, two, cols=slice(None)):
    return jnp.concatenate([one[:, cols], two[:, cols]], axis=0)


def grad_down_body(place, wait, flush, held, kept, halves):
    d_middle, act, act2 = held
    wait(0)
    right = stacked(d_middle, kept[0])
    rows = 4 * halves.shape[4]
    for z in range(4):
        wait(1, z)
        wait(2, z)
        left = stacked(act, act2, slice(z * rows, (z + 1) * rows))
        split_blocks(dot_tn(left, right), place, halves, slice(None), z)
        if z % 2:
            pair = pl.ds(jnp.bitwise_xor(place[2], z // 2), 1)
            flush(slice(None), pair)


def grad_up_body(place, wait, flush, held, kept, halves):
    hid, hid2, d_middle = held
    wait(0)
    wait(1)
    left = stacked(hid, hid2)
    tile = d_middle.shape[1] // 4
    for i in range(4):
        wait(2, i)
        cols = slice(i * tile, (i + 1) * tile)
        split_blocks(dot_tn(left, stacked(d_middle, kept[0], cols)), place, halves, cols)
        flush(slice(None), slice(None), slice(None), slice(None), cols)


def write_table(place, sums, halves, first):
    share = halves.shape[4]
    width, wide = sums[2].shape[1], sums[0].shape[1]
    ffn, attn = sums[0][...] + sums[1][...], sums[2][...] + sums[3][...]
    vectors = [attn[0:1], attn[1:2], ffn[2:3, width : 2 * width], ffn[1:2, 3 * width : 4 * width]]
    vectors += [ffn[2:3, :width]] + [ffn[1:2, i * width : (i + 1) * width] for i in range(3)]
    vectors = jnp.concatenate(vectors, axis=0)
    core, y, pair = place[0], place[1], place[2]
    count = wide // width
    for at in range(16):
        z, yy, cc = at // 4, (at // 2) % 2, at % 2
        rows = [vectors[:, at * share : (at + 1) * share]]
        for i in range(count):
            begin = (at * count + i) * share
            rows.append(ffn[0:1, begin : begin + share])
        rows.append(jnp.zeros((share - 8 - count, share), F32))
        part = jnp.concatenate(rows, axis=0)
        part = jnp.concatenate([part, jnp.zeros((share, LANES - share), F32)], axis=1)
        to = [jnp.bitwise_xor(core, cc), jnp.bitwise_xor(y, yy), jnp.bitwise_xor(pair, z // 2)]
        halves[(*to, z % 2, slice(None), slice(first, first + LANES))] = part.astype(BF16)


def grad_attn_body(place, wait, flush, held, kept, halves):
    x, x2, d_middle, context, context2, d_branch = held
    width = x.shape[1]
    wait(0)
    wait(1)
    left = stacked(x, x2)
    for i in range(3):
        wait(2, i)
        cols = slice(i * width, (i + 1) * width)
        split_blocks(dot_tn(left, stacked(d_middle, kept[0], cols)), place, halves, cols)
        flush(slice(None), slice(None), slice(None), slice(None), cols)
    for i in range(3, 6):
        wait(i)
    values = dot_tn(stacked(context, context2), stacked(d_branch, kept[1]))
    split_blocks(values, place, halves, slice(3 * width, 4 * width))
    write_table(place, kept[2:], halves, 4 * width)
    cols = slice(3 * width, 4 * width + LANES)
    flush(slice(None), slice(None), slice(None), slice(None), cols)


def weight_grad(a, b):
    return sum(dot_tn(one, two) for one, two in zip(a, b)).astype(BF16)


def tie(value, *others):
    return lax.optimization_barrier((value, others))[0]


def after(before, *values):
    return lax.optimization_barrier((values, tuple(before)))[0]


class Grid:
    def __init__(self):
        index = lax.axis_index("dp")
        self.core = index % 2
        self.y = (index // 2) % 2
        self.low = (index // 4) % 2
        self.pair = index // 8
        self.is_middle = self.low != self.pair

    def move(self, block, route):
        return lax.ppermute(block, "dp", route)

    def swap_core(self, block):
        return self.move(block, [(i, i ^ 1) for i in range(16)])

    def swap_y(self, block):
        return self.move(block, [(i, i ^ 2) for i in range(16)])

    def swap_near(self, block):
        return self.move(block, [(i, i ^ 4) for i in range(16)])

    def swap_middle(self, block):
        return self.move(block, [(i, i ^ 12) for i in range(4, 12)])

    def send_out(self, block):
        return self.move(block, [(i, i ^ 4) for i in range(4, 12)])

    def send_in(self, block):
        return self.move(block, [(i, i ^ 4) for i in range(16) if not 4 <= i < 12])

    def skip_out(self, block):
        return self.move(block, [(i, i ^ 8) for i in range(4, 12)])

    def skip_in(self, block):
        return self.move(block, [(i, i ^ 8) for i in range(16) if not 4 <= i < 12])

    def picked(self, blocks, at, axis):
        return lax.dynamic_index_in_dim(blocks, at, axis, keepdims=False)

    def ordered(self, pieces):
        near, far = (self.pair * 2 + self.low, self.pair * 2 + 1 - self.low), (
            jnp.where(self.pair == 0, 2, 1),
            jnp.where(self.pair == 0, 3, 0),
        )
        places = []
        for index in range(8):
            dc, dy, away = index // 4, (index // 2) % 2, index % 2
            for z in far if away else near:
                places.append(z * 4 + (self.y ^ dy) * 2 + (self.core ^ dc))
        return jnp.zeros_like(jnp.concatenate(pieces)).at[jnp.stack(places)].set(
            jnp.concatenate(pieces)
        )


def passed_along(block, axis, distance):
    devices = range(lax.axis_size(axis))
    route = [(i - distance, i) for i in devices if i - distance in devices]
    return lax.ppermute(block, axis, route)


def on_device(
    tokens,
    cotangent,
    bucket,
    lengths,
    w_qkv,
    bias_q,
    bias_v,
    w_out,
    bias_out,
    gain_attn,
    shift_attn,
    w_up,
    bias_up,
    w_down,
    bias_down,
    gain_ffn,
    shift_ffn,
):
    section = lax.axis_index("section")
    width = tokens.shape[2]
    ff = w_up.shape[2]
    share = bias_q.shape[1]
    n_dp = width // share
    vectors = (bias_q, bias_v, bias_out, gain_attn, shift_attn, bias_down, gain_ffn, shift_ffn)
    by_links = n_dp == 16 and share % 16 == 0
    shares = ff // width
    count = len(vectors) + shares
    up_rows = tuple(bias_up[:, i * share : (i + 1) * share] for i in range(shares))
    row_table = jnp.concatenate(vectors + up_rows)
    row_table = lax.optimization_barrier(row_table).astype(BF16)
    part_a = jnp.concatenate([w_qkv[0], w_out[0]], axis=1).astype(BF16)
    part_up, part_down = w_up[0].astype(BF16), w_down[0].astype(BF16)
    grid = Grid() if by_links else None
    place = jnp.stack([grid.core, grid.y, grid.pair, grid.low]) if by_links else jnp.zeros((4,), jnp.int32)
    micro = jnp.arange(6, dtype=jnp.int32) % 3
    micro = jnp.where(jnp.arange(6) < 3, micro - section, micro - 1 + section)
    picked = jnp.clip(micro, 0, 1)[:, None]
    run = (micro[:, None] == picked).astype(jnp.int32)
    first = picked == 0
    here = jnp.concatenate([section[None].astype(jnp.int32), place])
    steps = jnp.concatenate(
        [
            run,
            picked,
            jnp.broadcast_to(here[None, :1], (6, 1)),
            jnp.where(first, bucket[:1], bucket[1:]),
            jnp.where(first, lengths[:1], lengths[1:]),
            jnp.broadcast_to(here[None, 1:], (6, 4)),
        ],
        axis=1,
    )
    if by_links:
        padded = jnp.pad(row_table, ((0, share - count), (0, LANES - share)))
        part_a = jnp.concatenate([part_a, padded], axis=1)
        got_a, got_up = grid.swap_near(part_a), grid.swap_near(part_up)
        down_other = grid.swap_y(part_down)
        ended = (got_a, got_up, down_other, steps)
        near_a, near_up = jnp.stack([part_a, got_a]), jnp.stack([part_up, got_up])

        near_a, both_down = after(ended, near_a, jnp.stack([part_down, down_other]))
        middle_a, got_down = grid.swap_middle(near_a), grid.swap_near(both_down)
        near_a_y = grid.swap_y(near_a)
        ended = (middle_a, got_down, near_a_y)
        near_down = jnp.stack([part_down, got_down[0]])
        near_down_y = jnp.stack([down_other, got_down[1]])

        middle_a, near_up = after(ended, middle_a, near_up)
        out_a, middle_up = grid.send_out(middle_a), grid.swap_middle(near_up)
        near_up_y = grid.swap_y(near_up)
        ended = (out_a, middle_up, near_up_y)
        far_a = jnp.where(grid.is_middle, middle_a, out_a)

        middle_up, near_down, near_a, near_a_y = after(
            ended, middle_up, near_down, near_a, near_a_y
        )
        far_a = tie(far_a, near_up_y)
        out_up, middle_down = grid.send_out(middle_up), grid.swap_middle(near_down)
        far_a_y = grid.swap_y(far_a)
        near_a_c, near_a_yc = grid.swap_core(near_a), grid.swap_core(near_a_y)
        ended = (out_up, middle_down, far_a_y, near_a_c, near_a_yc)
        far_up = jnp.where(grid.is_middle, middle_up, out_up)

        middle_down, near_down_y, far_a, far_a_y, near_up, near_up_y, near_down = after(
            ended, middle_down, near_down_y, far_a, far_a_y, near_up, near_up_y, near_down
        )
        far_up = tie(far_up, far_a_y)
        out_down, middle_down_y = grid.send_out(middle_down), grid.swap_middle(near_down_y)
        far_up_y = grid.swap_y(far_up)
        far_a_c, far_a_yc = grid.swap_core(far_a), grid.swap_core(far_a_y)
        near_up_c, near_up_yc = grid.swap_core(near_up), grid.swap_core(near_up_y)
        near_down_c, near_down_yc = grid.swap_core(near_down), grid.swap_core(near_down_y)
        ended = (out_down, middle_down_y, far_up_y, far_a_c, far_a_yc)
        ended += (near_up_c, near_up_yc, near_down_c, near_down_yc)
        far_down = jnp.where(grid.is_middle, middle_down, out_down)
        pieces_a = (near_a, far_a, near_a_y, far_a_y, near_a_c, far_a_c, near_a_yc, far_a_yc)
        table = grid.ordered([piece[:, :, 4 * width :] for piece in pieces_a])
        table = table[:, :count, :share]
    else:
        w_a, full_up, full_down = (
            lax.all_gather(part, "dp", axis=0, tiled=True) for part in (part_a, part_up, part_down)
        )
        table = lax.all_gather(row_table[None], "dp", axis=0, tiled=True)
    table = table.astype(F32).transpose(1, 0, 2)
    rows = table[:8].reshape(8, width)
    small = jnp.concatenate(
        [rows[:1], jnp.zeros((1, width), F32), rows[1:], jnp.zeros((7, width), F32)]
    )
    full_bias_up = table[8:].transpose(1, 0, 2).reshape(1, ff)

    none = jnp.zeros((ROWS, width), BF16)

    def ahead(step, received, held=None):
        attn_held, ffn_held = (None, None) if held is None else held
        attn = forward_attn(step, steps, tokens, received, w_a, small, attn_held)
        return attn, forward_ffn(
            step, steps, full_up, full_down, small, full_bias_up, attn[2], attn[4], ffn_held
        )

    def back_ffn(step, upstream, kept, held=None, far=False):
        return ffn_back(
            3 + step, steps, cotangent[min(step, 1)], upstream, full_up, full_down, small, *kept, held, far
        )

    if by_links:
        middle_down_y, far_up, far_up_y = after(ended, middle_down_y, far_up, far_up_y)
        out_down_y = grid.send_out(middle_down_y)
        far_up_c, far_up_yc = grid.swap_core(far_up), grid.swap_core(far_up_y)
        far_down_c = grid.swap_core(far_down)
        first, *others = pieces_a
        pieces = (
            (tie(first, far_up_c, far_up_yc, far_down_c), *others),
            (near_up, far_up, near_up_y, far_up_y, near_up_c, far_up_c, near_up_yc, far_up_yc),
        )
        made = forward_first(0, steps, tokens, none, small, full_bias_up, pieces)
        attn, (d_act, act, x, context, hid, far_act, w_a, full_up) = made[:6], made[6:]
        far_down_y = jnp.where(grid.is_middle, middle_down_y, tie(out_down_y, d_act))
        pieces = (near_down, far_down, near_down_y, far_down_y, near_down_c, far_down_c)
        pieces += (near_down_yc, grid.swap_core(far_down_y))
        *end, full_down = forward_down(0, steps, pieces, small, attn[2], act)
        outer = ((*attn, x, context), (d_act, *end, far_act, hid))
    else:
        outer = ahead(0, none)
    got = passed_along(outer[1][3], "section", 1)
    middle = ahead(1, got)
    got = passed_along(middle[1][3], "section", 1)
    back_outer = back_ffn(0, none, middle)
    back_attn_outer = attn_back(3, steps, w_a, back_outer[2], back_outer[0], middle[0])
    sent = passed_along(back_attn_outer[0], "section", -1)
    outer = ahead(2, got, outer)
    back_middle = back_ffn(1, sent, outer, far=by_links)
    back_attn_middle = attn_back(
        4, steps, w_a, back_middle[2], back_middle[0], outer[0], far=by_links
    )
    sent = passed_along(back_attn_middle[0], "section", -1)
    back_outer = back_ffn(2, sent, middle, back_outer)

    def last_attn_back(steps):
        return attn_back(5, steps, w_a, back_outer[2], back_outer[0], middle_attn, back_attn_outer)

    middle_attn = middle[0]
    x, context = zip(outer[0][6:], middle[0][6:])
    hid = outer[1][5], middle[1][5]
    act, outputs = (outer[1][4], middle[1][4]), (outer[1][3], middle[1][3])
    sums_ffn = back_middle[1], back_outer[1]
    d_ffn, d_pre = zip(back_middle[3:5], back_outer[3:5])
    d_branch = back_attn_middle[3] if by_links else back_middle[0], back_outer[0]

    def by_micro(one, two):
        first = section == 0
        return jnp.stack([jnp.where(first, one, two), jnp.where(first, two, one)])[None]

    if by_links:
        def plus(one, two):
            return one.astype(F32) + two.astype(F32)

        mine_down, theirs = grad_call(
            grad_down_body,
            "grad_down",
            place,
            (d_ffn[0], *act),
            (d_ffn[1],),
            ff // 16,
            width,
            (1, 4, 4),
            fetch=False,
        )
        got_down = grid.swap_core(theirs)
        mine_up, theirs = grad_call(
            grad_up_body,
            "grad_up",
            place,
            (tie(hid[0], mine_down), hid[1], d_pre[0]),
            (d_pre[1],),
            share,
            ff,
            (1, 1, 4),
            fetch=False,
        )

        def low_sum(*parts):
            return sum(part.astype(F32) for part in parts).astype(BF16)

        down_parts = [(mine_down[i, 1], got_down[i, 1]) for i in range(2)]
        out, out_y = (low_sum(*parts) for parts in down_parts)
        out, out_y, theirs, table = after((got_down, mine_up), out, out_y, theirs, steps)
        got_out, got_up = grid.send_in(out), grid.swap_core(theirs)
        last = last_attn_back(table)
        (got_out,) = after((last[1],), got_out)

        out_y, early_up, early_got = after((got_out,), out_y, mine_up, got_up)
        away_up, away_near = (low_sum(early_up[1, i], early_got[1, i]) for i in (1, 0))
        middle = low_sum(out, got_out)
        far_up_y, got_out_y = grid.swap_y(away_up), grid.send_in(out_y)
        got_middle = grid.swap_middle(middle)
        up_home = low_sum(early_up[0, 1], early_got[0, 1])
        (first_x,) = after((middle, away_up, away_near, up_home), x[0])
    else:
        last = last_attn_back(steps)
    input_grads, sums_attn, d_qkv = zip(back_attn_middle[:3], last)
    total = sums_ffn[0] + sums_ffn[1]
    total_attn = sums_attn[0] + sums_attn[1]
    vector_rows = jnp.stack(
        [
            total_attn[0],
            total_attn[1],
            total[2, width : 2 * width],
            total[1, 3 * width :],
            total[2, :width],
            total[1, :width],
            total[1, width : 2 * width],
            total[1, 2 * width : 3 * width],
        ]
    ).reshape(8, n_dp, share)
    table = jnp.concatenate(
        [vector_rows.transpose(1, 0, 2), total[0].reshape(n_dp, shares, share)], axis=1
    )
    if by_links:
        mine_a, theirs = grad_call(
            grad_attn_body,
            "grad_attn",
            place,
            (first_x, x[1], d_qkv[0], *context, d_branch[0]),
            (d_qkv[1], d_branch[1], *sums_ffn, *sums_attn),
            share,
            4 * width + LANES,
            (1, 1, 3, 1, 1, 1),
        )
        far_up_y, got_out_y, got_middle = after((mine_a,), far_up_y, got_out_y, got_middle)
        theirs, away_up = after((far_up_y, got_out_y, got_middle), theirs, away_near)
        got_a, near_up_y = grid.swap_core(theirs), grid.swap_y(away_up)
        far_up = low_sum(up_home, far_up_y)
        got_out_up = grid.send_in(far_up)
        got_middle_y = grid.swap_middle(low_sum(out_y, got_out_y))
        mine_up, got_up, mine_down, got_down = after(
            (got_a,), mine_up, got_up, mine_down, got_down
        )
        away_a, away_a_near = (low_sum(mine_a[1, i], got_a[1, i]) for i in (1, 0))
        got_out_up, got_middle_y, near_up_y = after(
            (away_a, away_a_near), got_out_up, got_middle_y, near_up_y
        )

        def down_sum(at, i):
            parts = (mine_down[i, 0], got_down[i, 0], (got_middle, got_middle_y)[i])
            return sum(grid.picked(part, at, 0).astype(F32) for part in parts)

        def up_sum(at):
            parts = (mine_up[0, 0], got_up[0, 0], near_up_y, got_middle_up)
            return sum(grid.picked(part, at, 0).astype(F32) for part in parts)

        def a_sum(at):
            parts = (mine_a[0, 0], got_a[0, 0], near_a_y)
            return sum(grid.picked(part, at, 0).astype(F32) for part in parts)

        (away_a,) = after((got_out_up, got_middle_y, near_up_y), away_a)
        far_a_y = grid.swap_y(away_a)
        got_middle_up = grid.swap_middle(low_sum(far_up, got_out_up))
        away = [down_sum(1 - grid.low, i).astype(BF16) for i in range(2)]
        got_near_down = grid.swap_near(jnp.stack(away))

        (away_a,) = after((far_a_y, got_middle_up, got_near_down), away_a_near)
        parts = (mine_a[0, 1], got_a[0, 1], far_a_y)
        one, other = (
            low_sum(*(grid.picked(part, at, 0) for part in parts)) for at in (grid.low, 1 - grid.low)
        )
        got_in, got_over, got_skip = grid.send_in(one), grid.swap_middle(one), grid.skip_in(other)
        near_a_y = grid.swap_y(away_a)
        both_down = [down_sum(grid.low, i) + got_near_down[i].astype(F32) for i in range(2)]
        away_down, away_up = both_down[1].astype(BF16), up_sum(1 - grid.low).astype(BF16)
        got_in, got_over, got_skip, near_a_y = after(
            (away_down, away_up), got_in, got_over, got_skip, near_a_y
        )

        away_down, away_up = after((got_in, got_over, got_skip, near_a_y), away_down, away_up)
        away = a_sum(1 - grid.low) + got_over.astype(F32) + got_skip.astype(F32)
        outputs, input_grads = after((got_in, got_over), outputs, input_grads)
        got_near_a = grid.swap_near(away.astype(BF16))
        got_middle_a = grid.swap_middle(low_sum(other, got_in))
        got_near_up, got_down_y = grid.swap_near(away_up), grid.swap_y(away_down)
        g_down = both_down[0] + got_down_y.astype(F32)
        g_up = up_sum(grid.low) + got_near_up.astype(F32)
        g_a = a_sum(grid.low) + got_near_a.astype(F32) + got_middle_a.astype(F32)
        table = g_a[:count, 4 * width : 4 * width + share]
    else:

        def summed(values):
            return lax.psum_scatter(values, "dp", scatter_dimension=0, tiled=True).astype(F32)

        g_down = summed(weight_grad(act, d_ffn))
        g_up = summed(weight_grad(hid, d_pre))
        g_qkv = weight_grad(x, d_qkv)
        g_out = weight_grad(context, d_branch)
        g_a = summed(jnp.concatenate([g_qkv, g_out], axis=1))
        table = summed(table)[0]
    hidden_states, input_grads = by_micro(*outputs), by_micro(*input_grads)
    g_down, g_up = g_down[None], g_up[None]
    g_qkv, g_out = g_a[None, :, : 3 * width], g_a[None, :, 3 * width : 4 * width]
    g_vectors = [table[i : i + 1] for i in range(8)]
    g_bias_up = table[8:].reshape(1, ff // n_dp)
    (
        g_bias_q,
        g_bias_v,
        g_bias_out,
        g_gain_attn,
        g_shift_attn,
        g_bias_down,
        g_gain_ffn,
        g_shift_ffn,
    ) = g_vectors
    return (
        hidden_states,
        input_grads,
        g_qkv,
        g_bias_q,
        g_bias_v,
        g_out,
        g_bias_out,
        g_gain_attn,
        g_shift_attn,
        g_up,
        g_bias_up,
        g_down,
        g_bias_down,
        g_gain_ffn,
        g_shift_ffn,
    )


def solution(mesh):
    matrix = P("section", "dp", None)
    vector = P("section", "dp")
    rows = P(None, "dp", None)
    outs = P("section", None, "dp", None)
    params = (
        matrix,
        vector,
        vector,
        matrix,
        vector,
        vector,
        vector,
        matrix,
        vector,
        matrix,
        vector,
        vector,
        vector,
    )
    return jax.shard_map(
        on_device,
        mesh=mesh,
        in_specs=(rows, rows, P(None, "dp"), P(None, "dp")) + params,
        out_specs=(outs, outs) + params,
        check_vma=False,
    )
```
